32 devices in a mesh: exp: 8 (over z, y), ctx: 4 (over x, core).
Axes of the slice: x: 2, y: 2, z: 4, core: 2. Of those that a mesh axis runs over, the one named last changes fastest.
Arguments:
- tokens: bfloat16 [32, 1024, 1024], P('exp', 'ctx'), may hold values from -6 to 6
- lengths: int32 [32], P('exp'), may hold values from 64 to 1024, as said below
- expert_ids: int32 [4, 32, 256, 1], P('ctx', 'exp'), may hold values from 0 to 15; in each aligned block of 1024 rows (0 to 1023, 1024 to 2047, ..., all dimensions but the last counted through in order) at most 106 rows name the same one
- cotangent: bfloat16 [32, 1024, 1024], P('exp', 'ctx'), may hold values from -6 to 6
- query_weight: float32 [1024, 1024], P(('exp', 'ctx')), may hold values from -0.1875 to 0.1875
- key_weight: float32 [1024, 1024], P(('exp', 'ctx')), may hold values from -0.1875 to 0.1875
- value_weight: float32 [1024, 1024], P(('exp', 'ctx')), may hold values from -0.1875 to 0.1875
- output_weight: float32 [1024, 1024], P(('exp', 'ctx')), may hold values from -1.5 to 1.5
- gain_one: float32 [1024], replicated, may hold values from 0.25 to 1.75
- shift_one: float32 [1024], replicated, may hold values from -2 to 2
- gain_two: float32 [1024], replicated, may hold values from 0.25 to 1.75
- shift_two: float32 [1024], replicated, may hold values from -2 to 2
- expert_in: float32 [16, 4096, 1024], P('exp', 'ctx'), may hold values from -0.1875 to 0.1875
- expert_out: float32 [16, 4096, 1024], P('exp', 'ctx'), may hold values from -0.09375 to 0.09375
Outputs:
- block_out: bfloat16 [32, 1024, 1024], P('exp', 'ctx')
- grad_tokens: bfloat16 [32, 1024, 1024], P('exp', 'ctx')
- grad_query: float32 [1024, 1024], P(('exp', 'ctx'))
- grad_key: float32 [1024, 1024], P(('exp', 'ctx'))
- grad_value: float32 [1024, 1024], P(('exp', 'ctx'))
- grad_output: float32 [1024, 1024], P(('exp', 'ctx'))
- grad_gain_one: float32 [1024], P(('exp', 'ctx'))
- grad_shift_one: float32 [1024], P(('exp', 'ctx'))
- grad_gain_two: float32 [1024], P(('exp', 'ctx'))
- grad_shift_two: float32 [1024], P(('exp', 'ctx'))
- grad_expert_in: float32 [16, 4096, 1024], P('exp', 'ctx')
- grad_expert_out: float32 [16, 4096, 1024], P('exp', 'ctx')
The draws below stay inside these ranges and needn't reach their ends.
Inputs may be any that keep to these rules, and one draw needn't show every extreme that they name: `expert_ids`: among the tokens of one device (1024 entries with one c and the 4 sequences of one index of exp), no expert is named more than 106 times, a bound that some block reaches. `lengths`: among the 4 sequences that start at each multiple of 4, at least one has length 1024.
All inputs are finite; a program needn't handle non-finite values.
Results may differ from the reference program's by a relative error of at most 0.012.
Values may be sent and summed in bfloat16 or wider, within the bound.
No kernel may reach another device: no remote copies, remote signals or barrier semaphores. Data moves between devices by JAX's collectives and lax.ppermute only.
A program may use at most 576 MiB of HBM per device.

```python
import functools
import math
import jax
import jax.numpy as jnp
import numpy as np
from jax import lax

D = 1024
HEADS = 16
HEAD_DIM = 64
FF = 4096
LEN = 1024
SHORTEST = 64
SEQS_DEV = 4
EXPERTS = 16
SEQS = 32
SPAN = 256
TOK_DEV = 1024
CAP = 80
MOST = 106
N_EXP = 8
N_CTX = 4


def draw_lengths(key, part):
    key = jax.random.fold_in(key, 11)
    key_list = jax.random.split(key, 4)
    longer = jax.random.randint(key_list[0], (SEQS,), 3 * LEN // 4, LEN + 1)
    anyone = jax.random.randint(key_list[1], (SEQS,), SHORTEST, LEN + 1)
    picker = jax.random.randint(key_list[2], (SEQS,), 0, 5)
    baseline = jnp.where(picker == 0, anyone, longer)
    chosen = jax.random.randint(key_list[3], (SEQS // SEQS_DEV,), 0, SEQS_DEV)
    fullest = jnp.arange(SEQS) % SEQS_DEV == jnp.repeat(chosen, SEQS_DEV)
    return jnp.where(fullest, LEN, baseline).astype(jnp.int32)


def block_scale(key, extent, cuts, least, largest):
    def one(dim, blocks):
        steps = jax.random.uniform(jax.random.fold_in(jax.random.fold_in(key, 6), dim), (blocks,), jnp.float32, least / len(cuts), largest / len(cuts))
        return jnp.repeat(jnp.exp(steps), extent[dim] // blocks).reshape((-1,) + (1,) * (len(extent) - dim - 1))

    factor_of = one(*cuts[0])
    for cut in cuts[1:]:
        factor_of = factor_of * one(*cut)
    return factor_of


def assign_block(own_key, own, number, rows, count, top, bound, lean):
    order = jax.random.permutation(own_key, count)
    heavy_load, ordinary = shares(count, rows * top, bound, lean, True), shares(count, rows * top, bound, lean, False)
    places = jnp.arange(count)

    def named(sizes, offset_by):
        used = int((sizes > 0).sum())
        fixed = max(1, used // 4)
        moved = fixed + (places - fixed + offset_by * (used - fixed)) % max(1, count - fixed)
        return jnp.zeros((count,), jnp.int32).at[order[jnp.where(places < fixed, places, moved)]].set(jnp.asarray(sizes, jnp.int32))

    sizes = jnp.where(number % 4 == 0, named(heavy_load, number // 4), named(ordinary, number - number // 4 - 1))
    mixed = jax.random.permutation(jax.random.fold_in(own, 3), count)
    donor, taker = mixed[0:count // 2 * 2:2], mixed[1:count // 2 * 2:2]
    slack = jnp.minimum(sizes[donor] - 1, bound - sizes[taker]) // 2
    slack = jnp.where((donor == order[0]) | (taker == order[0]) | (sizes[taker] == 0), 0, jnp.maximum(slack, 0))
    moved = jax.random.randint(jax.random.fold_in(own, 4), (count // 2,), 0, 1 << 20) % (slack + 1)
    sizes = sizes.at[donor].add(-moved).at[taker].add(moved)
    labels = jnp.searchsorted(jnp.cumsum(sizes), jnp.arange(rows * top), side="right").astype(jnp.int32)
    table = labels.reshape(top, rows).T
    table = table[jax.random.permutation(jax.random.fold_in(own, 1), rows)]
    offset_by = jax.random.randint(jax.random.fold_in(own, 2), (rows, 1), 0, top)
    return jnp.take_along_axis(table, (jnp.arange(top)[None, :] + offset_by) % top, axis=1)


def shares(count, total, most, lean, full):
    loads = [(1 << 20) // math.isqrt(standing ** lean) + 1 for standing in range(1, count + 1)]
    largest = most if full else min(most, max(-(-total // count), total * loads[0] // sum(loads)))
    least = 1 if total - largest >= count - 1 else 0
    given, rest = [largest] + [least] * (count - 1), total - largest - least * (count - 1)
    while rest > 0:
        candidates = [i for i in range(1, count) if given[i] < largest] or [i for i in range(1, count) if given[i] < most]
        mass, remaining = sum([loads[i] for i in candidates]), rest
        for i in candidates:
            addition = min(most - given[i], max(1, remaining * loads[i] // mass), rest)
            given[i] = given[i] + addition
            rest = rest - addition
    return np.array(given)


def centred(own_key, dims, spread, bound, cuts=(), dtype=jnp.bfloat16):
    level = block_scale(own_key, dims, cuts, -0.22, 0.18) if cuts else 1.0
    drawn = jax.random.normal(own_key, dims, jnp.float32) * spread * level
    return jnp.minimum(jnp.maximum(drawn, -bound), bound).astype(dtype)


def setup_inputs(seed: int = 0) -> dict:
    streams_of = jax.random.split(jax.random.key(seed), 15)
    tokens = centred(streams_of[0], (SEQS, LEN, D), 1.0, 6.0, ((0, 8), (1, 4)))
    lengths = draw_lengths(jax.random.fold_in(streams_of[14], 71), 0)
    expert_ids_keys = jax.random.split(jax.random.fold_in(streams_of[2], 1), N_CTX * SEQS * SPAN // TOK_DEV)
    expert_ids_turns = jax.random.permutation(jax.random.fold_in(streams_of[2], 3), N_CTX * SEQS * SPAN // TOK_DEV)
    expert_ids = jax.vmap(lambda own, number: assign_block(jax.random.fold_in(streams_of[2], 2), own, number, TOK_DEV, EXPERTS, 1, MOST, 1))(expert_ids_keys, expert_ids_turns).reshape((N_CTX, SEQS, SPAN, 1))
    cotangent = centred(streams_of[3], (SEQS, LEN, D), 1.0, 6.0, ((0, 8), (1, 4)))
    query_weight = centred(streams_of[4], (D, D), D ** -0.5, 0.1875, ((0, 32),), jnp.float32)
    key_weight = centred(streams_of[5], (D, D), D ** -0.5, 0.1875, ((0, 32),), jnp.float32)
    value_weight = centred(streams_of[6], (D, D), D ** -0.5, 0.1875, ((0, 32),), jnp.float32)
    output_weight = centred(streams_of[7], (D, D), (max(D // 64, 1)) ** -0.5, 1.5, ((0, 32),), jnp.float32)
    gain_one = jnp.clip(1.0 + 0.15 * jax.random.normal(streams_of[8], (D,), jnp.float32), 0.25, 1.75)
    shift_one = centred(streams_of[9], (D,), 0.3, 2.0, (), jnp.float32)
    gain_two = jnp.clip(1.0 + 0.15 * jax.random.normal(streams_of[10], (D,), jnp.float32), 0.25, 1.75)
    shift_two = centred(streams_of[11], (D,), 0.3, 2.0, (), jnp.float32)
    expert_in = centred(streams_of[12], (EXPERTS, FF, D), D ** -0.5, 0.1875, ((0, 8), (1, 4)), jnp.float32)
    expert_out = centred(streams_of[13], (EXPERTS, FF, D), FF ** -0.5, 0.09375, ((0, 8), (1, 4)), jnp.float32)
    return dict(tokens=tokens, lengths=lengths, expert_ids=expert_ids, cotangent=cotangent, query_weight=query_weight, key_weight=key_weight, value_weight=value_weight, output_weight=output_weight, gain_one=gain_one, shift_one=shift_one, gain_two=gain_two, shift_two=shift_two, expert_in=expert_in, expert_out=expert_out)


@jax.custom_vjp
def low(v):
    return lax.optimization_barrier(v.astype(jnp.bfloat16)).astype(jnp.float32)

@jax.custom_vjp
def low_back(v):
    return v

def low_keep(v):
    return (low(v), None)

def low_pass(kept, grad):
    return (grad,)

def back_keep(v):
    return (v, None)

def back_low(kept, grad):
    return (low(grad),)
low.defvjp(low_keep, low_pass)
low_back.defvjp(back_keep, back_low)
eps_norm = 1e-05
masked_score = -1e+30
highest = lax.Precision.HIGHEST

def layer_norm(values, gain, shift):
    average = lax.optimization_barrier(jnp.mean(values, axis=-1, keepdims=True))
    centered = values - average
    variance = lax.optimization_barrier(jnp.mean(centered * centered, axis=-1, keepdims=True))
    return centered * lax.rsqrt(variance + eps_norm) * gain + shift

def route_table(lengths, expert_ids):
    ids_block = expert_ids[..., 0].reshape(N_CTX, N_EXP, TOK_DEV).astype(jnp.int32)
    within = jnp.arange(TOK_DEV).astype(jnp.int32)
    position = (jnp.arange(N_CTX).astype(jnp.int32)[:, None, None] * SPAN + (within % SPAN)[None, None, :]).astype(jnp.int32)
    seq_index = (jnp.arange(N_EXP).astype(jnp.int32)[None, :, None] * SEQS_DEV + (within // SPAN)[None, None, :]).astype(jnp.int32)
    live = position < lengths[seq_index]
    onehot = ((ids_block[..., None] == jnp.arange(EXPERTS).astype(jnp.int32)) & live[..., None]).astype(jnp.int32)
    running = jnp.cumsum(onehot, axis=2).astype(jnp.int32)
    ranks = lax.optimization_barrier(jnp.sum(onehot * (running - 1), axis=-1)).astype(jnp.int32)
    keep = live & (ranks < CAP)
    block_index = (jnp.arange(N_CTX).astype(jnp.int32)[:, None, None] * N_EXP + jnp.arange(N_EXP).astype(jnp.int32)[None, :, None]).astype(jnp.int32)
    token_flat = (seq_index * LEN + position).astype(jnp.int32)
    target_expert = jnp.where(keep, ids_block, EXPERTS).astype(jnp.int32)
    target_slot = jnp.where(keep, block_index * CAP + ranks, 0).astype(jnp.int32)
    table = jnp.full((EXPERTS, N_CTX * N_EXP * CAP), SEQS * LEN, jnp.int32)
    table = table.at[target_expert.reshape(-1), target_slot.reshape(-1)].set(token_flat.reshape(-1), mode='drop')
    return table

def forward(lengths, table, tokens, query_weight, key_weight, value_weight, output_weight, gain_one, shift_one, gain_two, shift_two, expert_in, expert_out):
    query_low = low(query_weight)
    key_low = low(key_weight)
    value_low = low(value_weight)
    output_low = low(output_weight)
    act_low = low(layer_norm(tokens, gain_one, shift_one))
    per_group = math.gcd(SEQS, max(1, 4096 // LEN))
    group_count = SEQS // per_group
    position = jnp.arange(LEN).astype(jnp.int32)
    causal = position[None, :] <= position[:, None]

    def attend(pack):
        act_group, len_group = pack
        flat = act_group.reshape(per_group * LEN, D)
        queries = low_back(low(jnp.dot(flat, query_low, precision=highest))).reshape(per_group, LEN, HEADS, HEAD_DIM)
        keys_all = low_back(low(jnp.dot(flat, key_low, precision=highest))).reshape(per_group, LEN, HEADS, HEAD_DIM)
        values_all = low_back(low(jnp.dot(flat, value_low, precision=highest))).reshape(per_group, LEN, HEADS, HEAD_DIM)
        scores = jnp.einsum('gqhd,gkhd->ghqk', queries, keys_all, precision=highest) * HEAD_DIM ** (-0.5)
        scores = low_back(scores)
        allowed = causal[None, None] & (position[None, None, None, :] < len_group[:, None, None, None])
        probs = low(jax.nn.softmax(jnp.where(allowed, scores, masked_score), axis=-1))
        mixed = jnp.einsum('ghqk,gkhd->gqhd', probs, values_all, precision=highest)
        mixed = low_back(low(mixed.reshape(per_group * LEN, D)))
        return low_back(jnp.dot(mixed, output_low, precision=highest)).reshape(per_group, LEN, D)
    branch_one = lax.map(jax.checkpoint(attend), (act_low.reshape(group_count, per_group, LEN, D), lengths.reshape(group_count, per_group)))
    hidden = tokens + branch_one.reshape(SEQS, LEN, D)
    sent = low_back(low(layer_norm(hidden, gain_two, shift_two).reshape(SEQS * LEN, D)))
    padded = jnp.concatenate([sent, jnp.zeros((1, D), jnp.float32)], axis=0)
    gathered = padded[table]
    in_low = low(expert_in)
    out_low = low(expert_out)

    def expert_fn(pack):
        rows, first, second = pack
        pre = low_back(jnp.dot(rows, first.T, precision=highest))
        activ = low(jax.nn.gelu(pre))
        return low_back(low(jnp.dot(activ, second, precision=highest)))
    outputs = lax.map(jax.checkpoint(expert_fn), (gathered, in_low, out_low))
    routed = jnp.zeros((SEQS * LEN + 1, D), jnp.float32).at[table.reshape(-1)].add(outputs.reshape(-1, D))[:-1]
    return hidden + routed.reshape(SEQS, LEN, D)

def reference(tokens, lengths, expert_ids, cotangent, query_weight, key_weight, value_weight, output_weight, gain_one, shift_one, gain_two, shift_two, expert_in, expert_out):
    table = route_table(lengths, expert_ids)
    bound_forward = functools.partial(forward, lengths, table)
    result, pullback = jax.vjp(bound_forward, tokens.astype(jnp.float32), query_weight, key_weight, value_weight, output_weight, gain_one, shift_one, gain_two, shift_two, expert_in, expert_out)
    grads = pullback(cotangent.astype(jnp.float32))
    return (result.astype(jnp.bfloat16), grads[0].astype(jnp.bfloat16), grads[1], grads[2], grads[3], grads[4], grads[5], grads[6], grads[7], grads[8], grads[9], grads[10])
```

```python
import functools

import jax
import jax.numpy as jnp
from jax import lax
from jax.experimental import pallas as pl
from jax.experimental.pallas import tpu as pltpu
from jax.sharding import PartitionSpec as P

HEAD_DIM = 64
LANES = 128
PAIR = 3 * LANES
BLOCK = 256
LOG2E = 1.4426950408889634
CORES = 2

eps_norm = 1e-05
masked_score = -1e30
f32 = jnp.float32
bf16 = jnp.bfloat16
NN = (((1,), (0,)), ((), ()))
NT = (((1,), (1,)), ((), ()))
TN = (((0,), (0,)), ((), ()))
VMEM_LIMIT = 56 * 1024 * 1024


def mm(a, b, dims=NN):
    return lax.dot_general(a, b, dims, preferred_element_type=f32)


def head_operands(length, q, k):
    full = q.shape[0]
    lane = lax.broadcasted_iota(jnp.int32, (full, LANES), 1)
    pos = lax.broadcasted_iota(jnp.int32, (full, LANES), 0)
    bias = jnp.where(pos < length, 0.0, masked_score).astype(f32)
    inside, q_aug, k_aug = [], [], []
    for head in range(2):
        own = (lane // HEAD_DIM) == head
        spare = lane == HEAD_DIM * (1 - head)
        inside.append(own)
        q_aug.append(jnp.where(own, q, jnp.where(spare, 1.0, 0.0)).astype(bf16))
        k_aug.append(jnp.where(own, k, jnp.where(spare, bias, 0.0)).astype(bf16))
    return inside, q_aug, k_aug


def attention_forward_kernel(len_ref, x_ref, o_ref):
    full = x_ref.shape[0]
    q, k, v = (x_ref[:, LANES * t : LANES * (t + 1)].astype(f32) for t in range(3))
    inside, q_aug, k_aug = head_operands(len_ref[pl.program_id(0)], q, k)
    v_own = [jnp.where(own, v, 0.0).astype(bf16) for own in inside]
    to_log2 = HEAD_DIM**-0.5 * LOG2E
    row = lax.broadcasted_iota(jnp.int32, (BLOCK, BLOCK), 0)
    col = lax.broadcasted_iota(jnp.int32, (BLOCK, BLOCK), 1)
    causal = col <= row
    for i in range(full // BLOCK):
        here, before = slice(i * BLOCK, (i + 1) * BLOCK), slice(0, i * BLOCK)
        total = jnp.zeros((BLOCK, LANES), f32)
        for head in range(2):
            qi = q_aug[head][here]
            s_here = jnp.where(causal, mm(qi, k_aug[head][here], NT) * to_log2, masked_score)
            top = jnp.max(s_here, axis=1, keepdims=True)
            if i:
                s_before = mm(qi, k_aug[head][before], NT) * to_log2
                top = jnp.maximum(top, jnp.max(s_before, axis=1, keepdims=True))
            p_here = jnp.exp2(s_here - top)
            mass = jnp.sum(p_here, axis=1, keepdims=True)
            if i:
                p_before = jnp.exp2(s_before - top)
                mass = mass + jnp.sum(p_before, axis=1, keepdims=True)
            inverse = 1.0 / mass
            total = total + mm((p_here * inverse).astype(bf16), v_own[head][here])
            if i:
                total = total + mm((p_before * inverse).astype(bf16), v_own[head][before])
        o_ref[here, :] = total.astype(bf16)


def attention_forward(lens, qkv, full):
    n_seq, pairs = qkv.shape[0] // full, qkv.shape[1] // PAIR
    return pl.pallas_call(
        attention_forward_kernel,
        grid_spec=pltpu.PrefetchScalarGridSpec(
            num_scalar_prefetch=1,
            grid=(n_seq, pairs),
            in_specs=[pl.BlockSpec((full, PAIR), lambda s, p, l: (s, p))],
            out_specs=pl.BlockSpec((full, LANES), lambda s, p, l: (s, p)),
        ),
        out_shape=jax.ShapeDtypeStruct((n_seq * full, pairs * LANES), bf16),
        compiler_params=pltpu.CompilerParams(vmem_limit_bytes=VMEM_LIMIT),
        cost_estimate=pl.CostEstimate(
            flops=n_seq * pairs * 2 * 2 * 2 * full * full * 256,
            bytes_accessed=n_seq * full * pairs * 512 * 2,
            transcendentals=n_seq * pairs * full * full,
        ),
        name="attention_forward",
    )(lens, qkv)


def attention_backward_kernel(len_ref, x_ref, g_ref, o_ref, p_scr, d_scr):
    full = x_ref.shape[0]
    q, k = (x_ref[:, LANES * t : LANES * (t + 1)].astype(f32) for t in range(2))
    v = x_ref[:, 2 * LANES : 3 * LANES]
    g = g_ref[...].astype(f32)
    inside, q_aug, k_aug = head_operands(len_ref[pl.program_id(0)], q, k)
    q_own = [jnp.where(own, q, 0.0).astype(bf16) for own in inside]
    k_own = [jnp.where(own, k, 0.0).astype(bf16) for own in inside]
    g_own = [jnp.where(own, g, 0.0).astype(bf16) for own in inside]
    scale = HEAD_DIM**-0.5
    to_log2 = scale * LOG2E
    row = lax.broadcasted_iota(jnp.int32, (BLOCK, BLOCK), 0)
    col = lax.broadcasted_iota(jnp.int32, (BLOCK, BLOCK), 1)
    causal = row <= col
    count = full // BLOCK
    for i in range(count):
        here, before = slice(i * BLOCK, (i + 1) * BLOCK), slice(0, i * BLOCK)
        dq = jnp.zeros((BLOCK, LANES), f32)
        for head in range(2):
            qi, gi = q_aug[head][here], g_own[head][here]
            s_here = jnp.where(causal, mm(k_aug[head][here], qi, NT) * to_log2, masked_score)
            top = jnp.max(s_here, axis=0, keepdims=True)
            if i:
                s_before = mm(k_aug[head][before], qi, NT) * to_log2
                top = jnp.maximum(top, jnp.max(s_before, axis=0, keepdims=True))
            p_here = jnp.exp2(s_here - top)
            mass = jnp.sum(p_here, axis=0, keepdims=True)
            if i:
                p_before = jnp.exp2(s_before - top)
                mass = mass + jnp.sum(p_before, axis=0, keepdims=True)
            inverse = 1.0 / mass
            p_here = p_here * inverse
            g_here = mm(v[here], gi, NT)
            delta = jnp.sum(g_here * p_here, axis=0, keepdims=True)
            if i:
                p_before = p_before * inverse
                g_before = mm(v[before], gi, NT)
                delta = delta + jnp.sum(g_before * p_before, axis=0, keepdims=True)
            d_here = (p_here * (g_here - delta)).astype(bf16)
            p_scr[head, here, here] = p_here.astype(bf16)
            d_scr[head, here, here] = d_here
            dq = dq + mm(d_here, k_own[head][here], TN)
            if i:
                d_before = (p_before * (g_before - delta)).astype(bf16)
                p_scr[head, before, here] = p_before.astype(bf16)
                d_scr[head, before, here] = d_before
                dq = dq + mm(d_before, k_own[head][before], TN)
        o_ref[here, 0:LANES] = (dq * scale).astype(bf16)
    for j in range(count):
        here, after = slice(j * BLOCK, (j + 1) * BLOCK), slice(j * BLOCK, full)
        dk = mm(d_scr[0, here, after], q_own[0][after]) + mm(d_scr[1, here, after], q_own[1][after])
        dv = mm(p_scr[0, here, after], g_own[0][after]) + mm(p_scr[1, here, after], g_own[1][after])
        o_ref[here, LANES : 2 * LANES] = (dk * scale).astype(bf16)
        o_ref[here, 2 * LANES : 3 * LANES] = dv.astype(bf16)


def attention_backward(lens, qkv, g, full):
    n_seq, pairs = qkv.shape[0] // full, qkv.shape[1] // PAIR
    return pl.pallas_call(
        attention_backward_kernel,
        grid_spec=pltpu.PrefetchScalarGridSpec(
            num_scalar_prefetch=1,
            grid=(n_seq, pairs),
            in_specs=[
                pl.BlockSpec((full, PAIR), lambda s, p, l: (s, p)),
                pl.BlockSpec((full, LANES), lambda s, p, l: (s, p)),
            ],
            out_specs=pl.BlockSpec((full, PAIR), lambda s, p, l: (s, p)),
            scratch_shapes=[pltpu.VMEM((2, full, full), bf16)] * 2,
        ),
        out_shape=jax.ShapeDtypeStruct(qkv.shape, bf16),
        compiler_params=pltpu.CompilerParams(vmem_limit_bytes=VMEM_LIMIT),
        cost_estimate=pl.CostEstimate(
            flops=n_seq * pairs * 2 * 5 * 2 * full * full * 256,
            bytes_accessed=n_seq * full * pairs * 896 * 2,
            transcendentals=n_seq * pairs * full * full,
        ),
        name="attention_backward",
    )(lens, qkv, g)


def norm_parts(values):
    average = jnp.mean(values, axis=-1, keepdims=True)
    centered = values - average
    variance = jnp.mean(centered * centered, axis=-1, keepdims=True)
    inverse = lax.rsqrt(variance + eps_norm)
    return centered * inverse, inverse


def norm_back(grad, normal, inverse, gain):
    inner = grad * gain
    mean_one = jnp.mean(inner, axis=-1, keepdims=True)
    mean_two = jnp.mean(inner * normal, axis=-1, keepdims=True)
    return inverse * (inner - mean_one - normal * mean_two)


def gelu_parts(pre):
    outer, inner = 0.7978845608028654, 0.044715
    square = pre * pre
    half = 0.5 + 0.5 * jnp.tanh(outer * pre * (1.0 + inner * square))
    slope = outer * (1.0 + 3.0 * inner * square)
    return pre * half, half + 2.0 * pre * half * (1.0 - half) * slope


def body(
    tokens,
    lengths,
    expert_ids,
    cotangent,
    query_weight,
    key_weight,
    value_weight,
    output_weight,
    gain_one,
    shift_one,
    gain_two,
    shift_two,
    expert_in,
    expert_out,
):
    seq_local, span, width = tokens.shape
    rows = seq_local * span
    n_ctx, n_exp = lax.axis_size("ctx"), lax.axis_size("exp")
    ctx = lax.axis_index("ctx")
    chips = n_ctx // CORES
    chip, core = ctx // CORES, ctx % CORES
    seqs = seq_local // chips
    full = span * n_ctx
    half = width // CORES
    experts = expert_in.shape[0]
    group = n_ctx // experts
    sub, member = ctx // group, ctx % group
    shard = expert_in.shape[1]
    all_experts = experts * n_exp
    capacity = max(2, rows * 5 // (4 * all_experts))
    devices = n_exp * n_ctx
    everyone = ("exp", "ctx")

    def ctx_send(value, target):
        return lax.ppermute(value, "ctx", [(c, target(c)) for c in range(n_ctx)])

    def other_core(value):
        return ctx_send(value, lambda c: c ^ 1)

    def to_chip(value, shift):
        return ctx_send(value, lambda c: ((c // CORES + shift) % chips) * CORES + c % CORES)

    def pick(value, index):
        return lax.dynamic_index_in_dim(value, index, 0, keepdims=False)

    def in_order(found, mine, size):
        out = []
        for place in range(size):
            chosen = found[0]
            for r in range(1, size):
                chosen = jnp.where((mine - place) % size == r, found[r], chosen)
            out.append(chosen)
        return jnp.stack(out)

    def chip_exchange(value):
        if chips == 1:
            return value
        found = [pick(value, chip)]
        for r in range(1, chips):
            found.append(to_chip(pick(value, (chip + r) % chips), r))
        return in_order(found, chip, chips)

    def by_core(mine, other, axis=0):
        first = jnp.where(core == 0, mine, other)
        second = jnp.where(core == 0, other, mine)
        return jnp.stack([first, second], axis=axis)

    def exchange_all(value):
        return lax.all_to_all(value, everyone, split_axis=0, concat_axis=0, tiled=True)

    def by_pair(weight):
        return weight.astype(bf16).reshape(weight.shape[0], width // LANES, 1, LANES)

    local_qkv = jnp.concatenate(
        [by_pair(query_weight), by_pair(key_weight), by_pair(value_weight)], axis=2
    ).reshape(query_weight.shape[0], 3 * width)
    qkv_all = lax.all_gather(local_qkv, everyone, axis=0, tiled=True)
    qkv_weight = lax.dynamic_slice_in_dim(qkv_all, core * 3 * half, 3 * half, axis=1)
    out_weight = lax.all_gather(output_weight.astype(bf16), everyone, axis=0, tiled=True)
    out_weight = jnp.concatenate(
        [
            lax.dynamic_slice_in_dim(out_weight, core * half, half, axis=0),
            lax.dynamic_slice_in_dim(out_weight, (1 - core) * half, half, axis=0),
        ],
        axis=0,
    )

    inputs = tokens.astype(f32).reshape(rows, width)
    normal_one, inverse_one = norm_parts(inputs)
    act = (normal_one * gain_one + shift_one).astype(bf16)
    act_chip = chip_exchange(act.reshape(chips, seqs, span, width))
    act_pair = by_core(act_chip, other_core(act_chip), axis=1)
    act_full = jnp.transpose(act_pair, (2, 0, 1, 3, 4)).reshape(seqs * full, width)

    lens = lax.dynamic_slice_in_dim(lengths, chip * seqs, seqs)
    qkv = mm(act_full, qkv_weight).astype(bf16)
    mixed_chip = attention_forward(lens, qkv, full)
    mixed_chip = mixed_chip.reshape(seqs, chips, CORES, span, half)
    by_dest = jnp.transpose(mixed_chip, (2, 1, 0, 3, 4))
    mixed_own = pick(by_dest, core)
    mixed_other = other_core(pick(by_dest, 1 - core))
    mixed = chip_exchange(jnp.stack([mixed_own, mixed_other], axis=1))
    mixed_low = jnp.transpose(mixed, (0, 2, 3, 1, 4)).reshape(rows, width)
    hidden = inputs + mm(mixed_low, out_weight)
    normal_two, inverse_two = norm_parts(hidden)
    sent_low = (normal_two * gain_two + shift_two).astype(bf16)

    ids_flat = expert_ids.reshape(rows)
    positions = ctx * span + jnp.arange(span)
    live = (positions[None, :] < lengths[:, None]).reshape(rows)
    onehot = ((ids_flat[:, None] == jnp.arange(all_experts)[None, :]) & live[:, None]).astype(
        jnp.int32
    )
    running = jnp.cumsum(onehot, axis=0)
    ranks = jnp.sum(onehot * (running - 1), axis=1)
    keep = live & (ranks < capacity)
    target = ids_flat * capacity + ranks
    slots = all_experts * capacity
    select = ((target[None, :] == jnp.arange(slots)[:, None]) & keep[None, :]).astype(bf16)

    grad_low = cotangent.reshape(rows, width)
    grad_send = mm(select, grad_low).astype(bf16)
    grad_arrived = exchange_all(grad_send)
    send_rows = mm(select, sent_low).astype(bf16)
    arrived = exchange_all(send_rows)

    def group_send(value, shift):
        return ctx_send(value, lambda c: (c // group) * group + (c % group + shift) % group)

    def sub_send(value, shift):
        return ctx_send(value, lambda c: ((c // group + shift) % experts) * group + c % group)

    def gather_group(value):
        return jnp.concatenate([value] + [group_send(value, r) for r in range(1, group)], axis=0)

    def swap_weights(weight):
        low = weight.astype(bf16)
        parts = [pick(low, sub)]
        for r in range(1, experts):
            parts.append(sub_send(pick(low, (sub + r) % experts), r))
        return jnp.concatenate(parts, axis=0)

    first_low, second_low = swap_weights(expert_in), swap_weights(expert_out)
    x_rows, g_rows = gather_group(arrived), gather_group(grad_arrived)
    mine = arrived.shape[0]

    def sum_group(partial):
        total = partial[:mine]
        for r in range(1, group):
            part = partial[r * mine : (r + 1) * mine].astype(bf16)
            total = total + group_send(part, group - r).astype(f32)
        return total.astype(bf16)

    pre = mm(x_rows, first_low, NT)
    grad_activ = mm(g_rows, second_low, NT)
    activ, slope = gelu_parts(pre)
    activ_low = activ.astype(bf16)
    grad_pre_low = (grad_activ * slope).astype(bf16)
    grad_sent_rows = sum_group(mm(grad_pre_low, first_low))
    grad_back = exchange_all(grad_sent_rows)
    result_rows = sum_group(mm(activ_low, second_low))
    returned = exchange_all(result_rows)
    routed = mm(select, returned, TN)
    block_out = (hidden + routed).astype(bf16).reshape(tokens.shape)

    def swap_grads(grad):
        grad = grad.reshape(experts, shard, width).astype(bf16)
        found = [grad[0]]
        for r in range(1, experts):
            found.append(sub_send(grad[r], experts - r))
        found = [found[0]] + found[:0:-1]
        return in_order(found, sub, experts).astype(f32)

    grad_expert_out = swap_grads(mm(activ_low, g_rows, TN))
    grad_expert_in = swap_grads(mm(grad_pre_low, x_rows, TN))

    grad_sent = mm(select, grad_back, TN)
    grad_gain_two = jnp.sum(grad_sent * normal_two, axis=0)
    grad_shift_two = jnp.sum(grad_sent, axis=0)
    grad_hidden = cotangent.astype(f32).reshape(rows, width) + norm_back(
        grad_sent, normal_two, inverse_two, gain_two
    )
    grad_branch = grad_hidden.astype(bf16)
    grad_mixed = mm(grad_branch, out_weight, NT).astype(bf16)
    grad_mixed = jnp.transpose(
        grad_mixed.reshape(chips, seqs, span, CORES, half), (0, 3, 1, 2, 4)
    )
    grad_mixed = chip_exchange(grad_mixed)
    gm_mine = grad_mixed[:, 0]
    gm_other = other_core(grad_mixed[:, 1])
    gm_full = jnp.transpose(by_core(gm_mine, gm_other, axis=1), (2, 0, 1, 3, 4)).reshape(
        seqs * full, half
    )
    grad_qkv = attention_backward(lens, qkv, gm_full, full)
    grad_act = mm(grad_qkv, qkv_weight, NT).astype(bf16)
    grad_act = jnp.transpose(
        grad_act.reshape(seqs, chips, CORES, span, width), (2, 1, 0, 3, 4)
    )
    grad_act_sum = pick(grad_act, core).astype(f32) + other_core(pick(grad_act, 1 - core)).astype(
        f32
    )
    grad_act_own = chip_exchange(grad_act_sum.astype(bf16)).reshape(rows, width).astype(f32)
    grad_gain_one = jnp.sum(grad_act_own * normal_one, axis=0)
    grad_shift_one = jnp.sum(grad_act_own, axis=0)
    grad_tokens = grad_hidden + norm_back(grad_act_own, normal_one, inverse_one, gain_one)
    grad_tokens = grad_tokens.astype(bf16).reshape(tokens.shape)

    wo_rows = mm(mixed_low, grad_branch, TN)
    wo_rows = by_core(wo_rows[:half], wo_rows[half:]).reshape(width, width).astype(bf16)
    wo_cols = jnp.stack([wo_rows[:, :half], wo_rows[:, half:]])
    wo_mine = pick(wo_cols, core).astype(f32) + other_core(pick(wo_cols, 1 - core)).astype(f32)
    own = width // devices

    def to_owner(partial):
        got = exchange_all(partial.astype(bf16)).reshape(devices // CORES, CORES, own, -1)
        return jnp.sum(got.astype(f32), axis=0)

    grad_wo = to_owner(wo_mine)
    grad_output = jnp.transpose(grad_wo, (1, 0, 2)).reshape(own, width)
    grad_w = to_owner(mm(act_full, grad_qkv, TN))
    grad_w = jnp.transpose(grad_w, (1, 0, 2)).reshape(own, width // LANES, 3, LANES)
    grad_query, grad_key, grad_value = (grad_w[:, :, t].reshape(own, width) for t in range(3))

    def small_to_owner(one, two):
        both = jnp.stack([one.reshape(devices, own), two.reshape(devices, own)], axis=1)
        return jnp.sum(exchange_all(both), axis=0)

    small_two = small_to_owner(grad_gain_two, grad_shift_two)
    small_one = small_to_owner(grad_gain_one, grad_shift_one)
    return (
        block_out,
        grad_tokens,
        grad_query,
        grad_key,
        grad_value,
        grad_output,
        small_one[0],
        small_one[1],
        small_two[0],
        small_two[1],
        grad_expert_in,
        grad_expert_out,
    )


def solution(mesh):
    rows = P("exp", "ctx", None)
    weight = P(("exp", "ctx"), None)
    vector = P(("exp", "ctx"))
    return jax.shard_map(
        body,
        mesh=mesh,
        in_specs=(
            rows,
            P("exp"),
            P("ctx", "exp", None, None),
            rows,
            weight,
            weight,
            weight,
            weight,
            P(),
            P(),
            P(),
            P(),
            rows,
            rows,
        ),
        out_specs=(rows, rows, weight, weight, weight, weight)
        + (vector, vector, vector, vector)
        + (rows, rows),
        check_vma=False,
    )
```

```python
import functools

import jax
import jax.numpy as jnp
from jax import lax
from jax.experimental import pallas as pl
from jax.experimental.pallas import tpu as pltpu
from jax.sharding import PartitionSpec as P

HEAD_DIM = 64
LANES = 128
PAIR = 3 * LANES
BLOCK = 256
LOG2E = 1.4426950408889634
CORES = 2

eps_norm = 1e-05
masked_score = -1e30
f32 = jnp.float32
bf16 = jnp.bfloat16
NN = (((1,), (0,)), ((), ()))
NT = (((1,), (1,)), ((), ()))
TN = (((0,), (0,)), ((), ()))
VMEM_LIMIT = 56 * 1024 * 1024
PARAMS = pltpu.CompilerParams(vmem_limit_bytes=VMEM_LIMIT)


def cost(flops):
    return pl.CostEstimate(flops=int(flops), bytes_accessed=1024, transcendentals=0)


hold = lax.optimization_barrier


def mm(a, b, dims=NN):
    return lax.dot_general(a, b, dims, preferred_element_type=f32)


def head_operands(length, q, k):
    full = q.shape[0]
    lane = lax.broadcasted_iota(jnp.int32, (full, LANES), 1)
    pos = lax.broadcasted_iota(jnp.int32, (full, LANES), 0)
    bias = jnp.where(pos < length, 0.0, masked_score).astype(f32)
    inside, q_aug, k_aug = [], [], []
    for head in range(2):
        own = (lane // HEAD_DIM) == head
        spare = lane == HEAD_DIM * (1 - head)
        inside.append(own)
        q_aug.append(jnp.where(own, q, jnp.where(spare, 1.0, 0.0)).astype(bf16))
        k_aug.append(jnp.where(own, k, jnp.where(spare, bias, 0.0)).astype(bf16))
    return inside, q_aug, k_aug


def attention_forward_kernel(len_ref, x_ref, o_ref):
    full = x_ref.shape[0]
    q, k, v = (x_ref[:, LANES * t : LANES * (t + 1)].astype(f32) for t in range(3))
    inside, q_aug, k_aug = head_operands(len_ref[pl.program_id(0)], q, k)
    v_own = [jnp.where(own, v, 0.0).astype(bf16) for own in inside]
    to_log2 = HEAD_DIM**-0.5 * LOG2E
    row = lax.broadcasted_iota(jnp.int32, (BLOCK, BLOCK), 0)
    col = lax.broadcasted_iota(jnp.int32, (BLOCK, BLOCK), 1)
    causal = col <= row
    for i in range(full // BLOCK):
        here, before = slice(i * BLOCK, (i + 1) * BLOCK), slice(0, i * BLOCK)
        total = jnp.zeros((BLOCK, LANES), f32)
        for head in range(2):
            qi = q_aug[head][here]
            s_here = jnp.where(causal, mm(qi, k_aug[head][here], NT) * to_log2, masked_score)
            top = jnp.max(s_here, axis=1, keepdims=True)
            if i:
                s_before = mm(qi, k_aug[head][before], NT) * to_log2
                top = jnp.maximum(top, jnp.max(s_before, axis=1, keepdims=True))
            p_here = jnp.exp2(s_here - top)
            mass = jnp.sum(p_here, axis=1, keepdims=True)
            if i:
                p_before = jnp.exp2(s_before - top)
                mass = mass + jnp.sum(p_before, axis=1, keepdims=True)
            inverse = 1.0 / mass
            total = total + mm((p_here * inverse).astype(bf16), v_own[head][here])
            if i:
                total = total + mm((p_before * inverse).astype(bf16), v_own[head][before])
        o_ref[here, :] = total.astype(bf16)


def attention_forward(lens, qkv, full):
    n_seq, pairs = qkv.shape[0] // full, qkv.shape[1] // PAIR
    return pl.pallas_call(
        attention_forward_kernel,
        grid_spec=pltpu.PrefetchScalarGridSpec(
            num_scalar_prefetch=1,
            grid=(n_seq, pairs),
            in_specs=[pl.BlockSpec((full, PAIR), lambda s, p, l: (s, p))],
            out_specs=pl.BlockSpec((full, LANES), lambda s, p, l: (s, p)),
        ),
        out_shape=jax.ShapeDtypeStruct((n_seq * full, pairs * LANES), bf16),
        compiler_params=PARAMS,
        cost_estimate=cost(n_seq * pairs * 4.0e9),
        name="attention_forward",
    )(lens, qkv)


def attention_backward_kernel(len_ref, x_ref, g_ref, o_ref, p_scr, d_scr):
    full = x_ref.shape[0]
    q, k = (x_ref[:, LANES * t : LANES * (t + 1)].astype(f32) for t in range(2))
    v = x_ref[:, 2 * LANES : 3 * LANES]
    g = g_ref[...].astype(f32)
    inside, q_aug, k_aug = head_operands(len_ref[pl.program_id(0)], q, k)
    q_own = [jnp.where(own, q, 0.0).astype(bf16) for own in inside]
    k_own = [jnp.where(own, k, 0.0).astype(bf16) for own in inside]
    g_own = [jnp.where(own, g, 0.0).astype(bf16) for own in inside]
    scale = HEAD_DIM**-0.5
    to_log2 = scale * LOG2E
    row = lax.broadcasted_iota(jnp.int32, (BLOCK, BLOCK), 0)
    col = lax.broadcasted_iota(jnp.int32, (BLOCK, BLOCK), 1)
    causal = row <= col
    count = full // BLOCK
    for i in range(count):
        here, before = slice(i * BLOCK, (i + 1) * BLOCK), slice(0, i * BLOCK)
        dq = jnp.zeros((BLOCK, LANES), f32)
        for head in range(2):
            qi, gi = q_aug[head][here], g_own[head][here]
            s_here = jnp.where(causal, mm(k_aug[head][here], qi, NT) * to_log2, masked_score)
            top = jnp.max(s_here, axis=0, keepdims=True)
            if i:
                s_before = mm(k_aug[head][before], qi, NT) * to_log2
                top = jnp.maximum(top, jnp.max(s_before, axis=0, keepdims=True))
            p_here = jnp.exp2(s_here - top)
            mass = jnp.sum(p_here, axis=0, keepdims=True)
            if i:
                p_before = jnp.exp2(s_before - top)
                mass = mass + jnp.sum(p_before, axis=0, keepdims=True)
            inverse = 1.0 / mass
            p_here = p_here * inverse
            g_here = mm(v[here], gi, NT)
            delta = jnp.sum(g_here * p_here, axis=0, keepdims=True)
            if i:
                p_before = p_before * inverse
                g_before = mm(v[before], gi, NT)
                delta = delta + jnp.sum(g_before * p_before, axis=0, keepdims=True)
            d_here = (p_here * (g_here - delta)).astype(bf16)
            p_scr[head, here, here] = p_here.astype(bf16)
            d_scr[head, here, here] = d_here
            dq = dq + mm(d_here, k_own[head][here], TN)
            if i:
                d_before = (p_before * (g_before - delta)).astype(bf16)
                p_scr[head, before, here] = p_before.astype(bf16)
                d_scr[head, before, here] = d_before
                dq = dq + mm(d_before, k_own[head][before], TN)
        o_ref[here, 0:LANES] = (dq * scale).astype(bf16)
    for j in range(count):
        here, after = slice(j * BLOCK, (j + 1) * BLOCK), slice(j * BLOCK, full)
        dk = mm(d_scr[0, here, after], q_own[0][after]) + mm(d_scr[1, here, after], q_own[1][after])
        dv = mm(p_scr[0, here, after], g_own[0][after]) + mm(p_scr[1, here, after], g_own[1][after])
        o_ref[here, LANES : 2 * LANES] = (dk * scale).astype(bf16)
        o_ref[here, 2 * LANES : 3 * LANES] = dv.astype(bf16)


def attention_backward(lens, qkv, g, full):
    n_seq, pairs = qkv.shape[0] // full, qkv.shape[1] // PAIR
    return pl.pallas_call(
        attention_backward_kernel,
        grid_spec=pltpu.PrefetchScalarGridSpec(
            num_scalar_prefetch=1,
            grid=(n_seq, pairs),
            in_specs=[
                pl.BlockSpec((full, PAIR), lambda s, p, l: (s, p)),
                pl.BlockSpec((full, LANES), lambda s, p, l: (s, p)),
            ],
            out_specs=pl.BlockSpec((full, PAIR), lambda s, p, l: (s, p)),
            scratch_shapes=[pltpu.VMEM((2, full, full), bf16)] * 2,
        ),
        out_shape=jax.ShapeDtypeStruct(qkv.shape, bf16),
        compiler_params=PARAMS,
        cost_estimate=cost(n_seq * pairs * 7.0e9),
        name="attention_backward",
    )(lens, qkv, g)


def tile_of(count, most=320):
    return max(t for t in range(16, most + 1, 16) if count % t == 0)


def pieces_of(shards):
    start = 0
    for ref in shards:
        size = min(512, ref.shape[0])
        for h in range(0, ref.shape[0], size):
            yield ref, slice(h, h + size), slice(start, start + size)
            start += size


def shard_specs(shards):
    return [pl.BlockSpec(w.shape, lambda i: (0, 0)) for w in shards]


def hidden_of(shards):
    return sum(w.shape[0] for w in shards)


def grad_activ_kernel(g_ref, *refs):
    for w_ref, part, cols in pieces_of(refs[:-1]):
        refs[-1][:, cols] = mm(g_ref[...], w_ref[part, :], NT).astype(bf16)


def grad_activ_pass(g, shards):
    (count, width), hidden = g.shape, hidden_of(shards)
    tile = tile_of(count)
    return pl.pallas_call(
        grad_activ_kernel,
        grid=(count // tile,),
        in_specs=[pl.BlockSpec((tile, width), lambda i: (i, 0))] + shard_specs(shards),
        out_specs=pl.BlockSpec((tile, hidden), lambda i: (i, 0)),
        out_shape=jax.ShapeDtypeStruct((count, hidden), bf16),
        compiler_params=PARAMS,
        cost_estimate=cost(2 * count * hidden * width),
        name="grad_activ_pass",
    )(g, *shards)


def hidden_kernel(x_ref, ga_ref, *refs):
    shards, (a_ref, gp_ref, gs_ref) = refs[:-3], refs[-3:]
    for w_ref, part, cols in pieces_of(shards):
        activ, slope = gelu_parts(mm(x_ref[...], w_ref[part, :], NT))
        a_ref[:, cols] = activ.astype(bf16)
        gp_ref[:, cols] = (ga_ref[:, cols].astype(f32) * slope).astype(bf16)
    gs_ref[...] = product_of(gp_ref, shards).astype(gs_ref.dtype)


def product_of(rows_ref, shards):
    total, start = None, 0
    for w_ref in shards:
        cols = slice(start, start + w_ref.shape[0])
        part = mm(rows_ref[:, cols], w_ref[...])
        total = part if total is None else total + part
        start += w_ref.shape[0]
    return total


def hidden_pass(x, grad_activ, shards, dtype):
    (count, width), hidden = x.shape, hidden_of(shards)
    tile = tile_of(count)
    wide = pl.BlockSpec((tile, hidden), lambda i: (i, 0))
    return pl.pallas_call(
        hidden_kernel,
        grid=(count // tile,),
        in_specs=[pl.BlockSpec((tile, width), lambda i: (i, 0)), wide] + shard_specs(shards),
        out_specs=[wide, wide, pl.BlockSpec((tile, width), lambda i: (i, 0))],
        out_shape=[jax.ShapeDtypeStruct((count, hidden), bf16)] * 2
        + [jax.ShapeDtypeStruct((count, width), dtype)],
        compiler_params=PARAMS,
        cost_estimate=cost(6 * count * hidden * width),
        name="hidden_pass",
    )(x, grad_activ, *shards)


def down_kernel(a_ref, *refs):
    refs[-1][...] = product_of(a_ref, refs[:-1]).astype(refs[-1].dtype)


def down_pass(activ, shards, dtype):
    (count, hidden), width = activ.shape, shards[0].shape[1]
    tile = tile_of(count)
    return pl.pallas_call(
        down_kernel,
        grid=(count // tile,),
        in_specs=[pl.BlockSpec((tile, hidden), lambda i: (i, 0))] + shard_specs(shards),
        out_specs=pl.BlockSpec((tile, width), lambda i: (i, 0)),
        out_shape=jax.ShapeDtypeStruct((count, width), dtype),
        compiler_params=PARAMS,
        cost_estimate=cost(2 * count * hidden * width),
        name="down_pass",
    )(activ, *shards)


def summed(lefts, rights):
    total = mm(lefts[0][...], rights[0][...], TN)
    for left, right in zip(lefts[1:], rights[1:]):
        total = total + mm(left[...], right[...], TN)
    return total


def weight_grad_kernel(*refs):
    count = len(refs) // 2
    refs[-1][...] = summed(refs[:count], refs[count:-1]).astype(bf16)


def weight_grad_pass(lefts, rights):
    hidden, width = lefts[0].shape[1], rights[0].shape[1]
    tile = min(256, hidden)
    return pl.pallas_call(
        weight_grad_kernel,
        grid=(hidden // tile,),
        in_specs=[pl.BlockSpec((v.shape[0], tile), lambda i: (0, i)) for v in lefts]
        + [pl.BlockSpec(v.shape, lambda i: (0, 0)) for v in rights],
        out_specs=pl.BlockSpec((tile, width), lambda i: (i, 0)),
        out_shape=jax.ShapeDtypeStruct((hidden, width), bf16),
        compiler_params=PARAMS,
        cost_estimate=cost(2 * lefts[0].size * width * len(lefts)),
        name="weight_grad_pass",
    )(*lefts, *rights)


def split_grad_kernel(order_ref, *refs, tile):
    count = (len(refs) - 2) // 2
    total = None
    for left, right in zip(refs[:count], refs[count:-2]):
        middle = left.shape[1] // tile // 2
        places = [order_ref[pl.program_id(0) * middle + n] for n in range(middle)]
        chosen = jnp.concatenate(
            [left[:, pl.ds(pl.multiple_of(place * tile, tile), tile)] for place in places], axis=1
        )
        part = mm(chosen, right[...], TN)
        total = part if total is None else total + part

    @pl.when(pl.program_id(0) == 0)
    def _():
        refs[-2][...] = total.astype(bf16)

    @pl.when(pl.program_id(0) == 1)
    def _():
        refs[-1][...] = total.astype(bf16)


def split_grad_pass(order, lefts, rights, tile):
    hidden, width = lefts[0].shape[1], rights[0].shape[1]
    whole = [pl.BlockSpec(v.shape, lambda i, o: (0, 0)) for v in (*lefts, *rights)]
    out = jax.ShapeDtypeStruct((hidden // 2, width), bf16)
    return pl.pallas_call(
        functools.partial(split_grad_kernel, tile=tile),
        grid_spec=pltpu.PrefetchScalarGridSpec(
            num_scalar_prefetch=1,
            grid=(2,),
            in_specs=whole,
            out_specs=[pl.BlockSpec(out.shape, lambda i, o: (0, 0))] * 2,
        ),
        out_shape=[out, out],
        compiler_params=PARAMS,
        cost_estimate=cost(3 * lefts[0].size * width * len(lefts)),
        name="split_grad_pass",
    )(order, *lefts, *rights)


def expert_grad_kernel(sub_ref, *refs, count, pieces, per):
    total = summed(refs[:count], refs[count : 2 * count])
    step = pl.program_id(0)
    for n in range(pieces):

        @pl.when((step >= n * per) & (step < (n + 1) * per))
        def _(n=n):
            refs[2 * count + n][...] = total.astype(bf16)

    @pl.when(step >= pieces * per)
    def _():
        refs[-1][0] = total


def expert_grad_pass(sub, lefts, rights, experts, parts):
    hidden, width = lefts[0].shape[1], rights[0].shape[1]
    shard = hidden // experts
    tile = min(256, shard // parts)
    pieces, per, own = (experts - 1) * parts, shard // parts // tile, shard // tile
    far = pieces * per

    def piece_spec(n):
        return pl.BlockSpec((tile, width), lambda i, s: (jnp.clip(i - n * per, 0, per - 1), 0))

    return pl.pallas_call(
        functools.partial(expert_grad_kernel, count=len(lefts), pieces=pieces, per=per),
        grid_spec=pltpu.PrefetchScalarGridSpec(
            num_scalar_prefetch=1,
            grid=(far + own,),
            in_specs=[
                pl.BlockSpec(
                    (v.shape[0], tile), lambda i, s: (0, jnp.where(i < far, i + own, i - far))
                )
                for v in lefts
            ]
            + [pl.BlockSpec(v.shape, lambda i, s: (0, 0)) for v in rights],
            out_specs=[piece_spec(n) for n in range(pieces)]
            + [
                pl.BlockSpec(
                    (1, tile, width), lambda i, s: (s[0], jnp.clip(i - far, 0, own - 1), 0)
                )
            ],
        ),
        out_shape=[jax.ShapeDtypeStruct((shard // parts, width), bf16)] * pieces
        + [jax.ShapeDtypeStruct((experts, shard, width), f32)],
        compiler_params=PARAMS,
        cost_estimate=cost(2 * lefts[0].size * width * len(lefts)),
        name="expert_grad_pass",
    )(sub.reshape(1), *lefts, *rights)


def assemble_kernel(sub_ref, whole_ref, *refs):
    pieces, o_ref = refs[:-1], refs[-1]
    for n, piece in enumerate(pieces):

        @pl.when(pl.program_id(0) * pl.num_programs(1) + pl.program_id(1) == n)
        def _(piece=piece):
            o_ref[0] = piece[...].astype(f32)


def assemble(sub, whole, pieces):
    experts = whole.shape[0]
    parts = len(pieces) // (experts - 1)
    cut, width = pieces[0].shape

    def place(r, n, s):
        return (lax.rem(s[0] - r - 1 + experts, experts), n, 0)

    return pl.pallas_call(
        assemble_kernel,
        grid_spec=pltpu.PrefetchScalarGridSpec(
            num_scalar_prefetch=1,
            grid=(experts - 1, parts),
            in_specs=[pl.BlockSpec(memory_space=pl.ANY)]
            + [pl.BlockSpec((cut, width), lambda r, n, s: (0, 0)) for _ in pieces],
            out_specs=pl.BlockSpec((1, cut, width), place),
        ),
        out_shape=jax.ShapeDtypeStruct(whole.shape, f32),
        input_output_aliases={1: 0},
        compiler_params=PARAMS,
        cost_estimate=cost(2.0e9),
        name="assemble",
    )(sub.reshape(1), whole, *pieces)


def gelu_parts(pre):
    outer, inner = 0.7978845608028654, 0.044715
    square = pre * pre
    half = 0.5 + 0.5 * jnp.tanh(pre * (outer + outer * inner * square))
    value = pre * half
    slope = half + value * (1.0 - half) * (2.0 * outer + 6.0 * outer * inner * square)
    return value, slope


def dispatch_kernel(*refs):
    o_ref, count = refs[-1], len(refs) // 2
    tile = o_ref.shape[0]
    total = None
    for t_ref, v_ref in zip(refs[:count], refs[count:-1]):
        rows = v_ref.shape[0]
        slot = lax.broadcasted_iota(jnp.int32, (tile, rows), 0) + pl.program_id(0) * tile
        chosen = jnp.where(t_ref[...] == slot, 1.0, 0.0).astype(bf16)
        part = mm(chosen, v_ref[...])
        total = part if total is None else total + part
    o_ref[...] = total.astype(bf16)


def dispatch(targets, values, slots):
    tile, width = tile_of(slots), values[0].shape[1]
    return pl.pallas_call(
        dispatch_kernel,
        grid=(slots // tile,),
        in_specs=[pl.BlockSpec((1, v.shape[0]), lambda i: (0, 0)) for v in values]
        + [pl.BlockSpec(v.shape, lambda i: (0, 0)) for v in values],
        out_specs=pl.BlockSpec((tile, width), lambda i: (i, 0)),
        out_shape=jax.ShapeDtypeStruct((slots, width), bf16),
        compiler_params=PARAMS,
        cost_estimate=cost(2 * slots * width * sum(v.shape[0] for v in values)),
        name="dispatch",
    )(*[t.reshape(1, -1) for t in targets], *values)


def returned_rows(target, rows_ref):
    slots = rows_ref.shape[0]
    slot = lax.broadcasted_iota(jnp.int32, (target.shape[0], slots), 1)
    return mm(jnp.where(target == slot, 1.0, 0.0).astype(bf16), rows_ref[...])


def combine_kernel(t_ref, rows_ref, h_ref, o_ref):
    o_ref[...] = (h_ref[...] + returned_rows(t_ref[...], rows_ref)).astype(bf16)


def combine(target, rows, hidden):
    count, width = hidden.shape
    tile = tile_of(count, 256)
    return pl.pallas_call(
        combine_kernel,
        grid=(count // tile,),
        in_specs=[
            pl.BlockSpec((tile, 1), lambda i: (i, 0)),
            pl.BlockSpec(rows.shape, lambda i: (0, 0)),
            pl.BlockSpec((tile, width), lambda i: (i, 0)),
        ],
        out_specs=pl.BlockSpec((tile, width), lambda i: (i, 0)),
        out_shape=jax.ShapeDtypeStruct((count, width), bf16),
        compiler_params=PARAMS,
        cost_estimate=cost(2 * count * width * rows.shape[0]),
        name="combine",
    )(target.reshape(-1, 1), rows, hidden)


def project_kernel(a_ref, b_ref, t_ref, w_ref, gain_ref, shift_ref, h_ref, s_ref, m_ref):
    mixed = jnp.concatenate([a_ref[0, 0], a_ref[0, 1], b_ref[0, 0], b_ref[0, 1]], axis=1)
    m_ref[...] = mixed
    hidden = t_ref[0, 0].astype(f32) + mm(mixed, w_ref[...])
    h_ref[...] = hidden
    normal, _ = norm_parts(hidden)
    s_ref[...] = (normal * gain_ref[...] + shift_ref[...]).astype(bf16)


def project_norm(parts, tokens, seq, weight, gain, shift):
    chips, cores, span, cols = parts[0].shape
    width = tokens.shape[3]
    block = pl.BlockSpec((1, cores, span, cols), lambda j: (j, 0, 0, 0))
    row = pl.BlockSpec((1, width), lambda j: (0, 0))
    out = pl.BlockSpec((span, width), lambda j: (j, 0))
    return pl.pallas_call(
        project_kernel,
        grid=(chips,),
        in_specs=[
            block,
            block,
            pl.BlockSpec((1, 1, span, width), lambda j: (j, seq, 0, 0)),
            pl.BlockSpec((width, width), lambda j: (0, 0)),
            row,
            row,
        ],
        out_specs=[out] * 3,
        out_shape=[
            jax.ShapeDtypeStruct((chips * span, width), dtype) for dtype in (f32, bf16, bf16)
        ],
        compiler_params=PARAMS,
        cost_estimate=cost(2 * chips * span * width * width),
        name="project_norm",
    )(*parts, tokens, weight, gain.reshape(1, -1), shift.reshape(1, -1))


def project_back_kernel(
    t_ref, rows_ref, h_ref, c_ref, w_ref, gain_ref, gh_ref, gb_ref, gm_ref, small_ref
):
    grad = returned_rows(t_ref[...], rows_ref)
    normal, inverse = norm_parts(h_ref[...])
    grad_hidden = c_ref[0, 0].astype(f32) + norm_back(grad, normal, inverse, gain_ref[...])
    gh_ref[...] = grad_hidden
    branch = grad_hidden.astype(bf16)
    gb_ref[...] = branch
    mixed = mm(branch, w_ref[...], NT).astype(bf16)
    cols = gm_ref.shape[3] // 2
    for half in range(2):
        for k in range(CORES):
            at = (half * CORES + k) * cols
            gm_ref[0, k, :, half * cols : (half + 1) * cols] = mixed[:, at : at + cols]
    sums = jnp.concatenate(
        [
            jnp.sum(grad * normal, axis=0, keepdims=True),
            jnp.sum(grad, axis=0, keepdims=True),
        ],
        axis=0,
    )

    @pl.when(pl.program_id(0) == 0)
    def _():
        small_ref[...] = sums

    @pl.when(pl.program_id(0) > 0)
    def _():
        small_ref[...] += sums


def project_back(target, rows, hidden, cotangent, seq, weight, gain):
    chips, _, span, width = cotangent.shape
    out = pl.BlockSpec((span, width), lambda j: (j, 0))
    return pl.pallas_call(
        project_back_kernel,
        grid=(chips,),
        in_specs=[
            pl.BlockSpec((span, 1), lambda j: (j, 0)),
            pl.BlockSpec(rows.shape, lambda j: (0, 0)),
            out,
            pl.BlockSpec((1, 1, span, width), lambda j: (j, seq, 0, 0)),
            pl.BlockSpec((width, width), lambda j: (0, 0)),
            pl.BlockSpec((1, width), lambda j: (0, 0)),
        ],
        out_specs=[
            out,
            out,
            pl.BlockSpec((1, CORES, span, width // CORES), lambda j: (j, 0, 0, 0)),
            pl.BlockSpec((2, width), lambda j: (0, 0)),
        ],
        out_shape=[
            jax.ShapeDtypeStruct((chips * span, width), f32),
            jax.ShapeDtypeStruct((chips * span, width), bf16),
            jax.ShapeDtypeStruct((chips, CORES, span, width // CORES), bf16),
            jax.ShapeDtypeStruct((2, width), f32),
        ],
        compiler_params=PARAMS,
        cost_estimate=cost(6 * chips * span * width * width),
        name="project_back",
    )(target.reshape(-1, 1), rows, hidden, cotangent, weight, gain.reshape(1, -1))


def norm_parts(values):
    average = jnp.mean(values, axis=-1, keepdims=True)
    centered = values - average
    variance = jnp.mean(centered * centered, axis=-1, keepdims=True)
    inverse = lax.rsqrt(variance + eps_norm)
    return centered * inverse, inverse


def norm_back(grad, normal, inverse, gain):
    inner = grad * gain
    mean_one = jnp.mean(inner, axis=-1, keepdims=True)
    mean_two = jnp.mean(inner * normal, axis=-1, keepdims=True)
    return inverse * (inner - mean_one - normal * mean_two)


def body(
    tokens,
    lengths,
    expert_ids,
    cotangent,
    query_weight,
    key_weight,
    value_weight,
    output_weight,
    gain_one,
    shift_one,
    gain_two,
    shift_two,
    expert_in,
    expert_out,
):
    seq_local, span, width = tokens.shape
    rows = seq_local * span
    n_ctx, n_exp = lax.axis_size("ctx"), lax.axis_size("exp")
    ctx = lax.axis_index("ctx")
    chips = n_ctx // CORES
    chip, core = ctx // CORES, ctx % CORES
    seqs = seq_local // chips
    full = span * n_ctx
    half = width // CORES
    experts = expert_in.shape[0]
    group = n_ctx // experts
    sub, member = ctx // group, ctx % group
    shard = expert_in.shape[1]
    all_experts = experts * n_exp
    capacity = max(2, rows * 5 // (4 * all_experts))
    devices = n_exp * n_ctx
    everyone = ("exp", "ctx")

    def ctx_send(value, target):
        return lax.ppermute(value, "ctx", [(c, target(c)) for c in range(n_ctx)])

    def other_core(value):
        return ctx_send(value, lambda c: c ^ 1)

    def to_chip(value, shift):
        return ctx_send(value, lambda c: ((c // CORES + shift) % chips) * CORES + c % CORES)

    def pick(value, index):
        return lax.dynamic_index_in_dim(value, index, 0, keepdims=False)

    def in_order(found, mine, size):
        out = []
        for place in range(size):
            chosen = found[0]
            for r in range(1, size):
                chosen = jnp.where((mine - place) % size == r, found[r], chosen)
            out.append(chosen)
        return jnp.stack(out)

    def chip_exchange(value):
        if chips == 1:
            return value
        found = [pick(value, chip)]
        for r in range(1, chips):
            found.append(to_chip(pick(value, (chip + r) % chips), r))
        return in_order(found, chip, chips)

    def by_core(mine, other, axis=0):
        first = jnp.where(core == 0, mine, other)
        second = jnp.where(core == 0, other, mine)
        return jnp.stack([first, second], axis=axis)

    def exchange_all(value):
        return lax.all_to_all(value, everyone, split_axis=0, concat_axis=0, tiled=True)

    def by_pair(weight):
        return weight.astype(bf16).reshape(weight.shape[0], width // LANES, 1, LANES)

    exp_bits = [b for b in (2, 4, 8, 16) if b < n_exp]
    chip_bits = [b for b in (1, 2, 4, 8) if b < chips]

    def double(state, axis, bit):
        value, keys = state
        if axis == "exp":
            other = lax.ppermute(value, "exp", [(e, e ^ bit) for e in range(n_exp)])
            index, key = lax.axis_index("exp"), (0, -bit)
        else:
            other = ctx_send(value, lambda c: c ^ (bit * CORES))
            index, key = chip, (1, -bit)
        keys = sorted(keys + [key])
        at = keys.index(key)
        upper = (index & bit) != 0
        low, high = jnp.where(upper, other, value), jnp.where(upper, value, other)
        return jnp.stack([low, high], axis=at), keys

    def gather_start(weight):
        kept = lax.dynamic_index_in_dim(weight, core, 1, keepdims=False)
        away = lax.dynamic_index_in_dim(weight, 1 - core, 1, keepdims=False)
        state = (by_core(kept, other_core(away)), [(2, 0)])
        for bit in exp_bits:
            state = double(state, "exp", bit)
        return state

    def gather_end(state, exp_first):
        steps = [("exp", 1)], [("ctx", bit) for bit in chip_bits]
        for axis, bit in steps[0] + steps[1] if exp_first else steps[1] + steps[0]:
            state = double(state, axis, bit)
        value = state[0]
        return value.reshape(width, value.shape[-1])

    local_qkv = jnp.concatenate(
        [by_pair(query_weight), by_pair(key_weight), by_pair(value_weight)], axis=2
    ).reshape(query_weight.shape[0], CORES, 3 * half)
    parts = 3 * half // 2

    ids_flat = expert_ids.reshape(rows)
    positions = ctx * span + jnp.arange(span)
    live = (positions[None, :] < lengths[:, None]).reshape(rows)
    onehot = ((ids_flat[:, None] == jnp.arange(all_experts)[None, :]) & live[:, None]).astype(
        jnp.int32
    )
    running = jnp.cumsum(onehot, axis=0)
    ranks = jnp.sum(onehot * (running - 1), axis=1)
    keep = live & (ranks < capacity)
    target = jnp.where(keep, ids_flat * capacity + ranks, -1)
    targets = target.reshape(chips, seqs, span)
    targets = [targets[:, s].reshape(chips * span) for s in range(seqs)]
    slots = all_experts * capacity

    inputs = tokens.astype(f32).reshape(rows, width)
    normal_one, inverse_one = norm_parts(inputs)
    act = (normal_one * gain_one + shift_one).astype(bf16).reshape(chips, seqs, span, width)
    tokens_four = tokens.reshape(chips, seqs, span, width)
    cotangent_four = cotangent.reshape(chips, seqs, span, width)
    acts = []
    for s in range(seqs):
        act_chip = chip_exchange(act[:, s])
        acts.append(by_core(act_chip, other_core(act_chip), axis=1).reshape(full, width))

    def sub_send(value, shift):
        return ctx_send(value, lambda c: ((c // group + shift) % experts) * group + c % group)

    def group_send(value, shift):
        return ctx_send(value, lambda c: (c // group) * group + (c % group + shift) % group)

    def casts(weight):
        own, *others = [pick(weight, (sub + r) % experts).astype(bf16) for r in range(experts)]
        return own, others

    def swap(others, parts):
        cut = shard // parts
        return [
            sub_send(low[n * cut : (n + 1) * cut], r)
            for r, low in enumerate(others, 1)
            for n in range(parts)
        ]

    second_own, second_low = casts(expert_out)
    second_far = swap(second_low, 2)
    gathered, keys = gather_start(local_qkv)
    gathered, expert_in, cotangent_late, second_far[0] = hold(
        (gathered, expert_in, cotangent, second_far[0])
    )
    grad_send = dispatch([target], [cotangent_late.reshape(rows, width)], slots)
    first_own, first_low = casts(expert_in)
    qkv_weights = [
        gather_end((gathered[..., :parts], keys), True),
        gather_end((gathered[..., parts:], keys), False),
    ]
    out_low = output_weight.astype(bf16)
    acts, qkv_weights, grad_send, first_own, first_low, second_own, out_low = hold(
        (acts, qkv_weights, grad_send, first_own, first_low, second_own, out_low)
    )
    grad_arrived = exchange_all(grad_send)
    out_all = lax.all_gather(out_low, everyone, axis=0, tiled=True)
    first_far = swap(first_low, 2)

    lens = lax.dynamic_slice_in_dim(lengths, chip * seqs, seqs)
    halves = range(2)
    calls = 2 * seqs
    qkvs, mixed_parts = [], []
    for s in range(seqs):
        qkvs.append([mm(acts[s], weight).astype(bf16) for weight in qkv_weights])
        for h in halves:
            call = s * 2 + h
            if call == calls // 2:
                qkvs[s][h], second_far = hold((qkvs[s][h], second_far))
            if call == calls - 1:
                qkvs[s][h], first_far[0] = hold((qkvs[s][h], first_far[0]))
            mixed_chip = attention_forward(lens[s : s + 1], qkvs[s][h], full)
            if call == calls - 1:
                mixed_chip, grad_arrived = hold((mixed_chip, grad_arrived))
            mixed_chip = mixed_chip.reshape(chips, CORES, span, half // 2)
            mixed_own = lax.dynamic_index_in_dim(mixed_chip, core, 1, keepdims=False)
            mixed_away = lax.dynamic_index_in_dim(mixed_chip, 1 - core, 1, keepdims=False)
            mixed_parts.append(
                chip_exchange(jnp.stack([mixed_own, other_core(mixed_away)], axis=1))
            )

    second_low = [second_own] + second_far
    g_parts = [grad_arrived] + [group_send(grad_arrived, r) for r in range(1, group)]
    out_weight = out_all.reshape(CORES, 2, half // 2, width)
    out_weight = jnp.stack([pick(out_weight, core), pick(out_weight, 1 - core)], axis=1)
    out_weight = out_weight.reshape(width, width)
    hiddens, sents, mixeds = zip(
        *[
            project_norm(
                mixed_parts[2 * s : 2 * s + 2], tokens_four, s, out_weight, gain_two, shift_two
            )
            for s in range(seqs)
        ]
    )
    arrived = exchange_all(dispatch(targets, sents, slots))

    grad_activs = [grad_activ_pass(part, second_low) for part in g_parts]
    arrived, grad_activs, first_far = hold((arrived, grad_activs, first_far))
    first_low = [first_own] + first_far
    mine = arrived.shape[0]
    x_parts = [arrived] + [group_send(arrived, r) for r in range(1, group)]
    passes = [
        hidden_pass(x_parts[r], grad_activs[r], first_low, f32 if r == 0 else bf16)
        for r in range(group)
    ]

    def sum_group(terms):
        total = terms[0]
        for r in range(1, group):
            total = total + group_send(terms[r], group - r).astype(f32)
        return total.astype(bf16)

    activ_parts, grad_pre_parts, sent_terms = zip(*passes)
    grad_sent_rows = sum_group(sent_terms)
    grad_back = exchange_all(grad_sent_rows)
    grad_sent_rows, activ_parts, grad_pre_parts = hold(
        (grad_sent_rows, activ_parts, grad_pre_parts)
    )

    def send_grad(far, n, parts):
        return sub_send(far[n], experts - 1 - n // parts)

    def own_grads(whole, arriving, parts):
        order = [(experts - 1 - r) * parts + n for r in range(1, experts) for n in range(parts)]
        return assemble(sub, whole, [arriving[n] for n in order])

    cuts = 2
    *second_away, second_whole = expert_grad_pass(sub, activ_parts, g_parts, experts, cuts)
    activ_parts, second_away = hold((activ_parts, second_away))
    early = (experts - 1) * cuts // 2
    second_sent = [send_grad(second_away, n, cuts) for n in range(early)]
    terms = [down_pass(activ_parts[r], second_low, bf16) for r in range(1, group)]
    result_rows = sum_group([down_pass(activ_parts[0], second_low, f32)] + terms)
    grad_back, result_rows, second_sent = hold((grad_back, result_rows, second_sent))

    grad_hiddens, branches, grad_mixeds, small_two = zip(
        *[
            project_back(
                targets[s], grad_back, hiddens[s], cotangent_four, s, out_weight, gain_two
            )
            for s in range(seqs)
        ]
    )
    gm_chip = [chip_exchange(part) for part in grad_mixeds]

    own = width // devices
    pairs = n_exp // 2
    exp = lax.axis_index("exp")
    odd = exp % 2
    alike = [
        [e * n_ctx + c for e in range(n_exp) if e % 2 == which for c in range(n_ctx)]
        for which in range(2)
    ]
    tile = width // n_exp
    split = tile % LANES == 0

    def halve(order, lefts, rights):
        columns = rights[0].shape[1]
        if split:
            away, kept = split_grad_pass(order, lefts, rights, tile)
        else:
            terms = weight_grad_pass(lefts, rights).reshape(n_exp, tile, columns)[order]
            away, kept = (half_of.reshape(-1, columns) for half_of in (terms[:pairs], terms[pairs:]))
        other = lax.ppermute(away, "exp", [(e, e ^ 1) for e in range(n_exp)])
        total = (kept.astype(f32) + other.astype(f32)).astype(bf16)
        return total.reshape(pairs * n_ctx, own, columns)

    def to_owner(terms):
        got = lax.all_to_all(
            terms, everyone, split_axis=0, concat_axis=0, tiled=True, axis_index_groups=alike
        )
        return got.astype(f32)

    def by_core_cols(got):
        got = jnp.sum(got.reshape(-1, CORES, own, got.shape[2]), axis=0)
        return jnp.transpose(got, (1, 0, 2))

    evens = jnp.arange(pairs, dtype=jnp.int32) * 2
    plain = jnp.concatenate([evens + 1 - odd, evens + odd])
    steps = n_exp // 4
    true_core, true_half, place = plain // (2 * steps), plain // steps % 2, plain % steps
    mixed_order = (true_half * CORES + (true_core + core) % CORES) * steps + place
    wo_terms = halve(mixed_order, mixeds, branches)
    branches, grad_pre_parts = hold((branches, grad_pre_parts))
    *first_away, first_whole = expert_grad_pass(sub, grad_pre_parts, x_parts, experts, cuts)
    gm_chip, first_away, result_rows, second_away = hold(
        (gm_chip, first_away, result_rows, second_away)
    )
    gm_parts = [
        by_core(part[:, 0], other_core(part[:, 1]), axis=1).reshape(full, half) for part in gm_chip
    ]
    returned = exchange_all(result_rows)
    second_sent += [send_grad(second_away, n, cuts) for n in range(early, len(second_away))]

    grad_qkvs = [[None, None] for s in range(seqs)]
    grad_act_parts, w_terms, first_sent = [], [], []
    call = 0
    for h in halves:
        for s in range(seqs):
            cols = slice(h * half // 2, (h + 1) * half // 2)
            gm_part = gm_parts[s][:, cols]
            if call == 0:
                first_sent = [send_grad(first_away, n, cuts) for n in range(len(first_away))]
            if call == calls - 2:
                gm_part, second_sent, wo_terms = hold((gm_part, second_sent, wo_terms))
            if call == calls - 1:
                gm_part, returned, first_sent[0] = hold((gm_part, returned, first_sent[0]))
            grad_qkvs[s][h] = attention_backward(lens[s : s + 1], qkvs[s][h], gm_part, full)
            if call == calls - 1:
                grad_qkvs[s][h], first_sent = hold((grad_qkvs[s][h], first_sent))
            call += 1
            if h == 1:
                part = sum(mm(grad_qkvs[s][i], qkv_weights[i], NT) for i in halves)
                part = part.astype(bf16).reshape(chips, CORES, span, width)
                kept = lax.dynamic_index_in_dim(part, core, 1, keepdims=False)
                away = lax.dynamic_index_in_dim(part, 1 - core, 1, keepdims=False)
                total = kept.astype(f32) + other_core(away).astype(f32)
                grad_act_parts.append(chip_exchange(total.astype(bf16)))
        grad_half = [grad_qkvs[s][h] for s in range(seqs)]
        w_terms.append(halve(plain, acts, grad_half))
    grad_expert_out = own_grads(second_whole, second_sent, cuts)
    grad_expert_in = own_grads(first_whole, first_sent, cuts)
    first_sum = to_owner(jnp.concatenate([w_terms[0], wo_terms], axis=2))
    first_sum, w_terms[1] = hold((first_sum, w_terms[1]))
    second_sum = by_core_cols(to_owner(w_terms[1]))
    grad_output = jnp.sum(first_sum[:, :, parts:], axis=0)
    grad_w = jnp.concatenate([by_core_cols(first_sum[:, :, :parts]), second_sum], axis=2)
    grad_w = grad_w.reshape(own, width // LANES, 3, LANES)
    grad_query, grad_key, grad_value = (grad_w[:, :, t].reshape(own, width) for t in range(3))

    def by_seq(values):
        return jnp.stack([value.reshape(chips, span, width) for value in values], axis=1)

    blocks = [combine(targets[s], returned, hiddens[s]) for s in range(seqs)]
    block_out = by_seq(blocks).reshape(tokens.shape)

    grad_act_own = jnp.stack(grad_act_parts, axis=1).reshape(rows, width).astype(f32)
    grad_gain_one = jnp.sum(grad_act_own * normal_one, axis=0)
    grad_shift_one = jnp.sum(grad_act_own, axis=0)
    grad_hidden = by_seq(grad_hiddens).reshape(rows, width)
    grad_tokens = grad_hidden + norm_back(grad_act_own, normal_one, inverse_one, gain_one)
    grad_tokens = grad_tokens.astype(bf16).reshape(tokens.shape)
    small_two = sum(small_two)
    small = jnp.stack(
        [
            value.reshape(devices, own)
            for value in (grad_gain_one, grad_shift_one, small_two[0], small_two[1])
        ],
        axis=1,
    )
    second_sum, small = hold((second_sum, small))
    small = jnp.sum(exchange_all(small), axis=0)
    return (
        block_out,
        grad_tokens,
        grad_query,
        grad_key,
        grad_value,
        grad_output,
        small[0],
        small[1],
        small[2],
        small[3],
        grad_expert_in,
        grad_expert_out,
    )


def solution(mesh):
    rows = P("exp", "ctx", None)
    weight = P(("exp", "ctx"), None)
    vector = P(("exp", "ctx"))
    return jax.shard_map(
        body,
        mesh=mesh,
        in_specs=(
            rows,
            P("exp"),
            P("ctx", "exp", None, None),
            rows,
            weight,
            weight,
            weight,
            weight,
            P(),
            P(),
            P(),
            P(),
            rows,
            rows,
        ),
        out_specs=(rows, rows, weight, weight, weight, weight)
        + (vector, vector, vector, vector)
        + (rows, rows),
        check_vma=False,
    )
```

```python
import functools

import jax
import jax.numpy as jnp
from jax import lax
from jax.experimental import pallas as pl
from jax.experimental.pallas import tpu as pltpu
from jax.sharding import PartitionSpec as P

HEAD_DIM = 64
LANES = 128
PAIR = 3 * LANES
BLOCK = 256
LOG2E = 1.4426950408889634
CORES = 2

eps_norm = 1e-05
masked_score = -1e30
f32 = jnp.float32
bf16 = jnp.bfloat16
NN = (((1,), (0,)), ((), ()))
NT = (((1,), (1,)), ((), ()))
TN = (((0,), (0,)), ((), ()))
VMEM_LIMIT = 56 * 1024 * 1024
PARAMS = pltpu.CompilerParams(vmem_limit_bytes=VMEM_LIMIT)


def cost(flops):
    return pl.CostEstimate(flops=int(flops / 10), bytes_accessed=1024, transcendentals=0)


hold = lax.optimization_barrier


def after(value, *others):
    return hold((value, others))[0]


def mm(a, b, dims=NN):
    return lax.dot_general(a, b, dims, preferred_element_type=f32)


def head_operands(length, q, k):
    full = q.shape[0]
    lane = lax.broadcasted_iota(jnp.int32, (full, LANES), 1)
    pos = lax.broadcasted_iota(jnp.int32, (full, LANES), 0)
    bias = jnp.where(pos < length, 0.0, masked_score).astype(f32)
    inside, q_aug, k_aug = [], [], []
    for head in range(2):
        own = (lane // HEAD_DIM) == head
        spare = lane == HEAD_DIM * (1 - head)
        inside.append(own)
        q_aug.append(jnp.where(own, q, jnp.where(spare, 1.0, 0.0)).astype(bf16))
        k_aug.append(jnp.where(own, k, jnp.where(spare, bias, 0.0)).astype(bf16))
    return inside, q_aug, k_aug


def attention_forward_kernel(len_ref, x_ref, o_ref):
    full = x_ref.shape[0]
    q, k, v = (x_ref[:, LANES * t : LANES * (t + 1)].astype(f32) for t in range(3))
    inside, q_aug, k_aug = head_operands(len_ref[pl.program_id(0)], q, k)
    v_own = [jnp.where(own, v, 0.0).astype(bf16) for own in inside]
    to_log2 = HEAD_DIM**-0.5 * LOG2E
    row = lax.broadcasted_iota(jnp.int32, (BLOCK, BLOCK), 0)
    col = lax.broadcasted_iota(jnp.int32, (BLOCK, BLOCK), 1)
    causal = col <= row
    for i in range(full // BLOCK):
        here, before = slice(i * BLOCK, (i + 1) * BLOCK), slice(0, i * BLOCK)
        total = jnp.zeros((BLOCK, LANES), f32)
        for head in range(2):
            qi = q_aug[head][here]
            s_here = jnp.where(causal, mm(qi, k_aug[head][here], NT) * to_log2, masked_score)
            top = jnp.max(s_here, axis=1, keepdims=True)
            if i:
                s_before = mm(qi, k_aug[head][before], NT) * to_log2
                top = jnp.maximum(top, jnp.max(s_before, axis=1, keepdims=True))
            p_here = jnp.exp2(s_here - top)
            mass = jnp.sum(p_here, axis=1, keepdims=True)
            if i:
                p_before = jnp.exp2(s_before - top)
                mass = mass + jnp.sum(p_before, axis=1, keepdims=True)
            inverse = 1.0 / mass
            total = total + mm((p_here * inverse).astype(bf16), v_own[head][here])
            if i:
                total = total + mm((p_before * inverse).astype(bf16), v_own[head][before])
        o_ref[here, :] = total.astype(bf16)


def attention_forward(lens, qkv, full):
    n_seq, pairs = qkv.shape[0] // full, qkv.shape[1] // PAIR
    return pl.pallas_call(
        attention_forward_kernel,
        grid_spec=pltpu.PrefetchScalarGridSpec(
            num_scalar_prefetch=1,
            grid=(n_seq, pairs),
            in_specs=[pl.BlockSpec((full, PAIR), lambda s, p, l: (s, p))],
            out_specs=pl.BlockSpec((full, LANES), lambda s, p, l: (s, p)),
        ),
        out_shape=jax.ShapeDtypeStruct((n_seq * full, pairs * LANES), bf16),
        compiler_params=PARAMS,
        cost_estimate=cost(n_seq * pairs * 2.5e9),
        name="attention_forward",
    )(lens, qkv)


def attention_probs_kernel(len_ref, x_ref, p_ref):
    full = x_ref.shape[0]
    q, k = (x_ref[:, LANES * t : LANES * (t + 1)].astype(f32) for t in range(2))
    _, q_aug, k_aug = head_operands(len_ref[pl.program_id(0)], q, k)
    to_log2 = HEAD_DIM**-0.5 * LOG2E
    row = lax.broadcasted_iota(jnp.int32, (BLOCK, BLOCK), 0)
    col = lax.broadcasted_iota(jnp.int32, (BLOCK, BLOCK), 1)
    causal = row <= col
    for i in range(full // BLOCK):
        here, before = slice(i * BLOCK, (i + 1) * BLOCK), slice(0, i * BLOCK)
        for head in range(2):
            qi = q_aug[head][here]
            s_here = jnp.where(causal, mm(k_aug[head][here], qi, NT) * to_log2, masked_score)
            top = jnp.max(s_here, axis=0, keepdims=True)
            if i:
                s_before = mm(k_aug[head][before], qi, NT) * to_log2
                top = jnp.maximum(top, jnp.max(s_before, axis=0, keepdims=True))
            p_here = jnp.exp2(s_here - top)
            mass = jnp.sum(p_here, axis=0, keepdims=True)
            if i:
                p_before = jnp.exp2(s_before - top)
                mass = mass + jnp.sum(p_before, axis=0, keepdims=True)
            inverse = 1.0 / mass
            p_ref[head, here, here] = (p_here * inverse).astype(bf16)
            if i:
                p_ref[head, before, here] = (p_before * inverse).astype(bf16)


def attention_probs(lens, qkv, full):
    n_seq, pairs = qkv.shape[0] // full, qkv.shape[1] // PAIR
    return pl.pallas_call(
        attention_probs_kernel,
        grid_spec=pltpu.PrefetchScalarGridSpec(
            num_scalar_prefetch=1,
            grid=(n_seq, pairs),
            in_specs=[pl.BlockSpec((full, PAIR), lambda s, p, l: (s, p))],
            out_specs=pl.BlockSpec((2, full, full), lambda s, p, l: (s * pairs + p, 0, 0)),
        ),
        out_shape=jax.ShapeDtypeStruct((n_seq * pairs * 2, full, full), bf16),
        compiler_params=PARAMS,
        cost_estimate=cost(n_seq * pairs * 2.0e9),
        name="attention_probs",
    )(lens, qkv)


def attention_backward_kernel(x_ref, g_ref, p_ref, o_ref, d_scr):
    full = x_ref.shape[0]
    q, k = (x_ref[:, LANES * t : LANES * (t + 1)].astype(f32) for t in range(2))
    v = x_ref[:, 2 * LANES : 3 * LANES]
    g = g_ref[...].astype(f32)
    head_of = lax.broadcasted_iota(jnp.int32, (full, LANES), 1) // HEAD_DIM
    inside = [head_of == head for head in range(2)]
    q_own = [jnp.where(own, q, 0.0).astype(bf16) for own in inside]
    k_own = [jnp.where(own, k, 0.0).astype(bf16) for own in inside]
    g_own = [jnp.where(own, g, 0.0).astype(bf16) for own in inside]
    scale = HEAD_DIM**-0.5
    count = full // BLOCK
    for i in range(count):
        here, until = slice(i * BLOCK, (i + 1) * BLOCK), slice(0, (i + 1) * BLOCK)
        dq = jnp.zeros((BLOCK, LANES), f32)
        for head in range(2):
            probs = p_ref[head, until, here].astype(f32)
            grad = mm(v[until], g_own[head][here], NT)
            delta = jnp.sum(grad * probs, axis=0, keepdims=True)
            d_score = (probs * (grad - delta)).astype(bf16)
            d_scr[head, until, here] = d_score
            dq = dq + mm(d_score, k_own[head][until], TN)
        o_ref[here, 0:LANES] = (dq * scale).astype(bf16)
    for j in range(count):
        here, after_ = slice(j * BLOCK, (j + 1) * BLOCK), slice(j * BLOCK, full)
        dk = mm(d_scr[0, here, after_], q_own[0][after_]) + mm(
            d_scr[1, here, after_], q_own[1][after_]
        )
        dv = mm(p_ref[0, here, after_], g_own[0][after_]) + mm(
            p_ref[1, here, after_], g_own[1][after_]
        )
        o_ref[here, LANES : 2 * LANES] = (dk * scale).astype(bf16)
        o_ref[here, 2 * LANES : 3 * LANES] = dv.astype(bf16)


def attention_backward(qkv, g, probs):
    full = probs.shape[1]
    n_seq, pairs = qkv.shape[0] // full, qkv.shape[1] // PAIR
    return pl.pallas_call(
        attention_backward_kernel,
        grid=(n_seq, pairs),
        in_specs=[
            pl.BlockSpec((full, PAIR), lambda s, p: (s, p)),
            pl.BlockSpec((full, LANES), lambda s, p: (s, p)),
            pl.BlockSpec((2, full, full), lambda s, p: (s * pairs + p, 0, 0)),
        ],
        out_specs=pl.BlockSpec((full, PAIR), lambda s, p: (s, p)),
        scratch_shapes=[pltpu.VMEM((2, full, full), bf16)],
        out_shape=jax.ShapeDtypeStruct(qkv.shape, bf16),
        compiler_params=PARAMS,
        cost_estimate=cost(n_seq * pairs * 3.0e9),
        name="attention_backward",
    )(qkv, g, probs)


def tile_of(count, most=320):
    return max(t for t in range(16, most + 1, 16) if count % t == 0)


def pieces_of(shards):
    start = 0
    for ref in shards:
        size = min(512, ref.shape[0])
        for h in range(0, ref.shape[0], size):
            yield ref, slice(h, h + size), slice(start, start + size)
            start += size


def shard_specs(shards):
    return [pl.BlockSpec(w.shape, lambda i: (0, 0)) for w in shards]


def hidden_of(shards):
    return sum(w.shape[0] for w in shards)


def grad_activ_kernel(g_ref, *refs):
    for w_ref, part, cols in pieces_of(refs[:-1]):
        refs[-1][:, cols] = mm(g_ref[...], w_ref[part, :], NT).astype(bf16)


def grad_activ_pass(g, shards):
    (count, width), hidden = g.shape, hidden_of(shards)
    tile = tile_of(count)
    return pl.pallas_call(
        grad_activ_kernel,
        grid=(count // tile,),
        in_specs=[pl.BlockSpec((tile, width), lambda i: (i, 0))] + shard_specs(shards),
        out_specs=pl.BlockSpec((tile, hidden), lambda i: (i, 0)),
        out_shape=jax.ShapeDtypeStruct((count, hidden), bf16),
        compiler_params=PARAMS,
        cost_estimate=cost(count * hidden * width / 2),
        name="grad_activ_pass",
    )(g, *shards)


def hidden_kernel(x_ref, ga_ref, *refs, before):
    shards, (a_ref, gp_ref, gs_ref) = refs[before:-3], refs[-3:]
    for w_ref, part, cols in pieces_of(shards):
        activ, slope = gelu_parts(mm(x_ref[...], w_ref[part, :], NT))
        a_ref[:, cols] = activ.astype(bf16)
        gp_ref[:, cols] = (ga_ref[:, cols].astype(f32) * slope).astype(bf16)
    total = product_of(gp_ref, shards)
    if before:
        total = total + refs[0][...]
    gs_ref[...] = total.astype(gs_ref.dtype)


def product_of(rows_ref, shards):
    total, start = None, 0
    for w_ref in shards:
        cols = slice(start, start + w_ref.shape[0])
        part = mm(rows_ref[:, cols], w_ref[...])
        total = part if total is None else total + part
        start += w_ref.shape[0]
    return total


def hidden_pass(x, grad_activ, shards, dtype, before=None):
    (count, width), hidden = x.shape, hidden_of(shards)
    tile = tile_of(count)
    wide = pl.BlockSpec((tile, hidden), lambda i: (i, 0))
    thin = pl.BlockSpec((tile, width), lambda i: (i, 0))
    more = [] if before is None else [before]
    return pl.pallas_call(
        functools.partial(hidden_kernel, before=len(more)),
        grid=(count // tile,),
        in_specs=[thin, wide] + [thin] * len(more) + shard_specs(shards),
        out_specs=[wide, wide, thin],
        out_shape=[jax.ShapeDtypeStruct((count, hidden), bf16)] * 2
        + [jax.ShapeDtypeStruct((count, width), dtype)],
        compiler_params=PARAMS,
        cost_estimate=cost(2 * count * hidden * width),
        name="hidden_pass",
    )(x, grad_activ, *more, *shards)


def down_kernel(*refs, own):
    total = product_of(refs[0], refs[2 : 2 + own]) + product_of(refs[1], refs[2 + own : -1])
    refs[-1][...] = total.astype(refs[-1].dtype)


def down_pass(activs, groups, dtype):
    count, width = activs[0].shape[0], groups[0][0].shape[1]
    tile = tile_of(count)
    shards = list(groups[0]) + list(groups[1])
    return pl.pallas_call(
        functools.partial(down_kernel, own=len(groups[0])),
        grid=(count // tile,),
        in_specs=[pl.BlockSpec((tile, a.shape[1]), lambda i: (i, 0)) for a in activs]
        + shard_specs(shards),
        out_specs=pl.BlockSpec((tile, width), lambda i: (i, 0)),
        out_shape=jax.ShapeDtypeStruct((count, width), dtype),
        compiler_params=PARAMS,
        cost_estimate=cost(2 * count * hidden_of(shards) * width),
        name="down_pass",
    )(*activs, *shards)


def summed(lefts, rights):
    total = mm(lefts[0][...], rights[0][...], TN)
    for left, right in zip(lefts[1:], rights[1:]):
        total = total + mm(left[...], right[...], TN)
    return total


def weight_grad_kernel(*refs):
    count = len(refs) // 2
    refs[-1][...] = summed(refs[:count], refs[count:-1]).astype(bf16)


def weight_grad_pass(lefts, rights):
    hidden, width = lefts[0].shape[1], rights[0].shape[1]
    tile = min(256, hidden)
    return pl.pallas_call(
        weight_grad_kernel,
        grid=(hidden // tile,),
        in_specs=[pl.BlockSpec((v.shape[0], tile), lambda i: (0, i)) for v in lefts]
        + [pl.BlockSpec(v.shape, lambda i: (0, 0)) for v in rights],
        out_specs=pl.BlockSpec((tile, width), lambda i: (i, 0)),
        out_shape=jax.ShapeDtypeStruct((hidden, width), bf16),
        compiler_params=PARAMS,
        cost_estimate=cost(2 * lefts[0].size * width * len(lefts)),
        name="weight_grad_pass",
    )(*lefts, *rights)


def split_grad_kernel(order_ref, *refs, tile, counts):
    values, start, col = refs[:-2], 0, 0
    steps = order_ref.shape[0] // len(counts)
    totals = []
    for group, count in enumerate(counts):
        lefts, rights = values[start : start + count], values[start + count : start + 2 * count]
        first = group * steps + pl.program_id(0) * (steps // 2)
        places = [order_ref[first + n] for n in range(steps // 2)]
        total = None
        for left, right in zip(lefts, rights):
            chosen = jnp.concatenate(
                [left[:, pl.ds(pl.multiple_of(place * tile, tile), tile)] for place in places],
                axis=1,
            )
            part = mm(chosen, right[...], TN)
            total = part if total is None else total + part
        totals.append((slice(col, col + total.shape[1]), total.astype(bf16)))
        start += 2 * count
        col += total.shape[1]

    for which in range(2):

        @pl.when(pl.program_id(0) == which)
        def _(which=which):
            for cols, total in totals:
                refs[which - 2][:, cols] = total


def split_grad_pass(groups, tile):
    hidden = groups[0][1][0].shape[1]
    width = sum(rights[0].shape[1] for _, _, rights in groups)
    values = [v for _, lefts, rights in groups for v in (*lefts, *rights)]
    out = jax.ShapeDtypeStruct((hidden // 2, width), bf16)
    return pl.pallas_call(
        functools.partial(split_grad_kernel, tile=tile, counts=[len(g[1]) for g in groups]),
        grid_spec=pltpu.PrefetchScalarGridSpec(
            num_scalar_prefetch=1,
            grid=(2,),
            in_specs=[pl.BlockSpec(v.shape, lambda i, o: (0, 0)) for v in values],
            out_specs=[pl.BlockSpec(out.shape, lambda i, o: (0, 0))] * 2,
        ),
        out_shape=[out, out],
        compiler_params=PARAMS,
        cost_estimate=cost(2 * width * sum(v.size for v in groups[0][1])),
        name="split_grad_pass",
    )(jnp.concatenate([order for order, _, _ in groups]), *values)


def add_terms_kernel(*refs):
    col = 0
    for one, two in zip(refs[0:-1:2], refs[1:-1:2]):
        cols = slice(col, col + one.shape[1])
        refs[-1][:, cols] = (one[...].astype(f32) + two[...].astype(f32)).astype(bf16)
        col = cols.stop


def add_terms(pairs):
    count = pairs[0][0].shape[0]
    tile = min(128, count)
    values = [v for pair in pairs for v in pair]
    width = sum(pair[0].shape[1] for pair in pairs)
    return pl.pallas_call(
        add_terms_kernel,
        grid=(count // tile,),
        in_specs=[pl.BlockSpec((tile, v.shape[1]), lambda i: (i, 0)) for v in values],
        out_specs=pl.BlockSpec((tile, width), lambda i: (i, 0)),
        out_shape=jax.ShapeDtypeStruct((count, width), bf16),
        compiler_params=PARAMS,
        cost_estimate=cost(3.0e10),
        name="add_terms",
    )(*values)


def expert_grad_kernel(sub_ref, *refs, count, pieces, per):
    step = pl.program_id(0)
    rights = refs[2 * count : 3 * count]

    @pl.when(step < pieces * per)
    def _():
        total = summed(refs[count : 2 * count], rights).astype(bf16)
        for n in range(pieces):

            @pl.when((step >= n * per) & (step < (n + 1) * per))
            def _(n=n):
                refs[3 * count + n][...] = total

    @pl.when(step >= pieces * per)
    def _():
        refs[-1][0] = summed(refs[:count], rights)


def expert_grad_pass(sub, owns, others, rights, experts, parts):
    shard, width = owns[0].shape[1], rights[0].shape[1]
    tile = min(256, shard // parts)
    pieces, per, own = (experts - 1) * parts, shard // parts // tile, shard // tile
    far = pieces * per

    def piece_spec(n):
        return pl.BlockSpec((tile, width), lambda i, s: (jnp.clip(i - n * per, 0, per - 1), 0))

    return pl.pallas_call(
        functools.partial(expert_grad_kernel, count=len(owns), pieces=pieces, per=per),
        grid_spec=pltpu.PrefetchScalarGridSpec(
            num_scalar_prefetch=1,
            grid=(far + own,),
            in_specs=[
                pl.BlockSpec((v.shape[0], tile), lambda i, s: (0, jnp.clip(i - far, 0, own - 1)))
                for v in owns
            ]
            + [
                pl.BlockSpec((v.shape[0], tile), lambda i, s: (0, jnp.clip(i, 0, far - 1)))
                for v in others
            ]
            + [pl.BlockSpec(v.shape, lambda i, s: (0, 0)) for v in rights],
            out_specs=[piece_spec(n) for n in range(pieces)]
            + [
                pl.BlockSpec(
                    (1, tile, width), lambda i, s: (s[0], jnp.clip(i - far, 0, own - 1), 0)
                )
            ],
        ),
        out_shape=[jax.ShapeDtypeStruct((shard // parts, width), bf16)] * pieces
        + [jax.ShapeDtypeStruct((experts, shard, width), f32)],
        compiler_params=PARAMS,
        cost_estimate=cost(2 * experts * owns[0].size * width * len(owns)),
        name="expert_grad_pass",
    )(sub.reshape(1), *owns, *others, *rights)


def assemble_kernel(sub_ref, whole_ref, *refs):
    pieces, o_ref = refs[:-1], refs[-1]
    for n, piece in enumerate(pieces):

        @pl.when(pl.program_id(0) * pl.num_programs(1) + pl.program_id(1) == n)
        def _(piece=piece):
            o_ref[0] = piece[...].astype(f32)


def assemble(sub, whole, pieces):
    experts = whole.shape[0]
    parts = len(pieces) // (experts - 1)
    cut, width = pieces[0].shape

    def place(r, n, s):
        return (lax.rem(s[0] - r - 1 + experts, experts), n, 0)

    return pl.pallas_call(
        assemble_kernel,
        grid_spec=pltpu.PrefetchScalarGridSpec(
            num_scalar_prefetch=1,
            grid=(experts - 1, parts),
            in_specs=[pl.BlockSpec(memory_space=pl.ANY)]
            + [pl.BlockSpec((cut, width), lambda r, n, s: (0, 0)) for _ in pieces],
            out_specs=pl.BlockSpec((1, cut, width), place),
        ),
        out_shape=jax.ShapeDtypeStruct(whole.shape, f32),
        input_output_aliases={1: 0},
        compiler_params=PARAMS,
        cost_estimate=cost(3.0e10),
        name="assemble",
    )(sub.reshape(1), whole, *pieces)


def gelu_parts(pre):
    outer, inner = 0.7978845608028654, 0.044715
    square = pre * pre
    half = 0.5 + 0.5 * jnp.tanh(pre * (outer + outer * inner * square))
    value = pre * half
    slope = half + value * (1.0 - half) * (2.0 * outer + 6.0 * outer * inner * square)
    return value, slope


def dispatch_kernel(*refs):
    o_ref, count = refs[-1], len(refs) // 2
    tile = o_ref.shape[0]
    total = None
    for t_ref, v_ref in zip(refs[:count], refs[count:-1]):
        rows = v_ref.shape[0]
        slot = lax.broadcasted_iota(jnp.int32, (tile, rows), 0) + pl.program_id(0) * tile
        chosen = jnp.where(t_ref[...] == slot, 1.0, 0.0).astype(bf16)
        part = mm(chosen, v_ref[...])
        total = part if total is None else total + part
    o_ref[...] = total.astype(bf16)


def dispatch(targets, values, slots):
    tile, width = tile_of(slots), values[0].shape[1]
    return pl.pallas_call(
        dispatch_kernel,
        grid=(slots // tile,),
        in_specs=[pl.BlockSpec((1, v.shape[0]), lambda i: (0, 0)) for v in values]
        + [pl.BlockSpec(v.shape, lambda i: (0, 0)) for v in values],
        out_specs=pl.BlockSpec((tile, width), lambda i: (i, 0)),
        out_shape=jax.ShapeDtypeStruct((slots, width), bf16),
        compiler_params=PARAMS,
        cost_estimate=cost(2 * slots * width * sum(v.shape[0] for v in values)),
        name="dispatch",
    )(*[t.reshape(1, -1) for t in targets], *values)


def returned_rows(target, rows_ref):
    slots = rows_ref.shape[0]
    slot = lax.broadcasted_iota(jnp.int32, (target.shape[0], slots), 1)
    return mm(jnp.where(target == slot, 1.0, 0.0).astype(bf16), rows_ref[...])


def combine_kernel(t_ref, rows_ref, h_ref, o_ref):
    o_ref[...] = (h_ref[...] + returned_rows(t_ref[...], rows_ref)).astype(bf16)


def combine(target, rows, hidden):
    count, width = hidden.shape
    tile = tile_of(count, 256)
    return pl.pallas_call(
        combine_kernel,
        grid=(count // tile,),
        in_specs=[
            pl.BlockSpec((tile, 1), lambda i: (i, 0)),
            pl.BlockSpec(rows.shape, lambda i: (0, 0)),
            pl.BlockSpec((tile, width), lambda i: (i, 0)),
        ],
        out_specs=pl.BlockSpec((tile, width), lambda i: (i, 0)),
        out_shape=jax.ShapeDtypeStruct((count, width), bf16),
        compiler_params=PARAMS,
        cost_estimate=cost(20 * count * width * rows.shape[0]),
        name="combine",
    )(target.reshape(-1, 1), rows, hidden)


def project_kernel(a_ref, b_ref, t_ref, w_ref, gain_ref, shift_ref, h_ref, s_ref, m_ref):
    mixed = jnp.concatenate([a_ref[0, 0], a_ref[0, 1], b_ref[0, 0], b_ref[0, 1]], axis=1)
    m_ref[...] = mixed
    hidden = t_ref[0, 0].astype(f32) + mm(mixed, w_ref[...])
    h_ref[...] = hidden
    normal, _ = norm_parts(hidden)
    s_ref[...] = (normal * gain_ref[...] + shift_ref[...]).astype(bf16)


def project_norm(parts, tokens, seq, weight, gain, shift):
    chips, cores, span, cols = parts[0].shape
    width = tokens.shape[3]
    block = pl.BlockSpec((1, cores, span, cols), lambda j: (j, 0, 0, 0))
    row = pl.BlockSpec((1, width), lambda j: (0, 0))
    out = pl.BlockSpec((span, width), lambda j: (j, 0))
    return pl.pallas_call(
        project_kernel,
        grid=(chips,),
        in_specs=[
            block,
            block,
            pl.BlockSpec((1, 1, span, width), lambda j: (j, seq, 0, 0)),
            pl.BlockSpec((width, width), lambda j: (0, 0)),
            row,
            row,
        ],
        out_specs=[out] * 3,
        out_shape=[
            jax.ShapeDtypeStruct((chips * span, width), dtype) for dtype in (f32, bf16, bf16)
        ],
        compiler_params=PARAMS,
        cost_estimate=cost(2 * chips * span * width * width),
        name="project_norm",
    )(*parts, tokens, weight, gain.reshape(1, -1), shift.reshape(1, -1))


def project_back_kernel(
    t_ref, rows_ref, h_ref, c_ref, w_ref, gain_ref, gh_ref, gb_ref, gm_ref, small_ref
):
    grad = returned_rows(t_ref[...], rows_ref)
    normal, inverse = norm_parts(h_ref[...])
    grad_hidden = c_ref[0, 0].astype(f32) + norm_back(grad, normal, inverse, gain_ref[...])
    gh_ref[...] = grad_hidden
    branch = grad_hidden.astype(bf16)
    gb_ref[...] = branch
    mixed = mm(branch, w_ref[...], NT).astype(bf16)
    cols = gm_ref.shape[3] // 2
    for half in range(2):
        for k in range(CORES):
            at = (half * CORES + k) * cols
            gm_ref[0, k, :, half * cols : (half + 1) * cols] = mixed[:, at : at + cols]
    sums = jnp.concatenate(
        [
            jnp.sum(grad * normal, axis=0, keepdims=True),
            jnp.sum(grad, axis=0, keepdims=True),
        ],
        axis=0,
    )

    @pl.when(pl.program_id(0) == 0)
    def _():
        small_ref[...] = sums

    @pl.when(pl.program_id(0) > 0)
    def _():
        small_ref[...] += sums


def project_back(target, rows, hidden, cotangent, seq, weight, gain):
    chips, _, span, width = cotangent.shape
    out = pl.BlockSpec((span, width), lambda j: (j, 0))
    return pl.pallas_call(
        project_back_kernel,
        grid=(chips,),
        in_specs=[
            pl.BlockSpec((span, 1), lambda j: (j, 0)),
            pl.BlockSpec(rows.shape, lambda j: (0, 0)),
            out,
            pl.BlockSpec((1, 1, span, width), lambda j: (j, seq, 0, 0)),
            pl.BlockSpec((width, width), lambda j: (0, 0)),
            pl.BlockSpec((1, width), lambda j: (0, 0)),
        ],
        out_specs=[
            out,
            out,
            pl.BlockSpec((1, CORES, span, width // CORES), lambda j: (j, 0, 0, 0)),
            pl.BlockSpec((2, width), lambda j: (0, 0)),
        ],
        out_shape=[
            jax.ShapeDtypeStruct((chips * span, width), f32),
            jax.ShapeDtypeStruct((chips * span, width), bf16),
            jax.ShapeDtypeStruct((chips, CORES, span, width // CORES), bf16),
            jax.ShapeDtypeStruct((2, width), f32),
        ],
        compiler_params=PARAMS,
        cost_estimate=cost(6 * chips * span * width * width),
        name="project_back",
    )(target.reshape(-1, 1), rows, hidden, cotangent, weight, gain.reshape(1, -1))


def grad_act_kernel(core_ref, *refs):
    count = (len(refs) - 2) // 2
    total = None
    for d_ref, w_ref in zip(refs[:count], refs[count:-2]):
        part = mm(d_ref[...], w_ref[...], NT)
        total = part if total is None else total + part
    for which in range(2):

        @pl.when(pl.program_id(0) == which)
        def _(which=which):
            refs[which - 2][0] = total.astype(bf16)


def grad_act_pass(core, grads, weights, chips):
    width = weights[0].shape[0]
    span = grads[0].shape[0] // (chips * CORES)
    out = jax.ShapeDtypeStruct((chips, span, width), bf16)

    def rows(which, j, c):
        return (j * CORES + jnp.where(which == 0, 1 - c[0], c[0]), 0)

    return pl.pallas_call(
        grad_act_kernel,
        grid_spec=pltpu.PrefetchScalarGridSpec(
            num_scalar_prefetch=1,
            grid=(2, chips),
            in_specs=[pl.BlockSpec((span, g.shape[1]), rows) for g in grads]
            + [pl.BlockSpec(w.shape, lambda which, j, c: (0, 0)) for w in weights],
            out_specs=[
                pl.BlockSpec(
                    (1, span, width), lambda which, j, c: (jnp.where(which == 0, j, chips - 1), 0, 0)
                ),
                pl.BlockSpec(
                    (1, span, width), lambda which, j, c: (jnp.where(which == 1, j, 0), 0, 0)
                ),
            ],
        ),
        out_shape=[out, out],
        compiler_params=PARAMS,
        cost_estimate=cost(2 * sum(g.size for g in grads) * width),
        name="grad_act_pass",
    )(core.reshape(1), *grads, *weights)


def norm_parts(values):
    average = jnp.mean(values, axis=-1, keepdims=True)
    centered = values - average
    variance = jnp.mean(centered * centered, axis=-1, keepdims=True)
    inverse = lax.rsqrt(variance + eps_norm)
    return centered * inverse, inverse


def norm_back(grad, normal, inverse, gain):
    inner = grad * gain
    mean_one = jnp.mean(inner, axis=-1, keepdims=True)
    mean_two = jnp.mean(inner * normal, axis=-1, keepdims=True)
    return inverse * (inner - mean_one - normal * mean_two)


def body(
    tokens,
    lengths,
    expert_ids,
    cotangent,
    query_weight,
    key_weight,
    value_weight,
    output_weight,
    gain_one,
    shift_one,
    gain_two,
    shift_two,
    expert_in,
    expert_out,
):
    seq_local, span, width = tokens.shape
    rows = seq_local * span
    n_ctx, n_exp = lax.axis_size("ctx"), lax.axis_size("exp")
    ctx = lax.axis_index("ctx")
    chips = n_ctx // CORES
    chip, core = ctx // CORES, ctx % CORES
    seqs = seq_local // chips
    full = span * n_ctx
    half = width // CORES
    experts = expert_in.shape[0]
    group = n_ctx // experts
    sub, member = ctx // group, ctx % group
    shard = expert_in.shape[1]
    all_experts = experts * n_exp
    capacity = max(2, rows * 5 // (4 * all_experts))
    devices = n_exp * n_ctx
    everyone = ("exp", "ctx")

    def ctx_send(value, target):
        return lax.ppermute(value, "ctx", [(c, target(c)) for c in range(n_ctx)])

    def other_core(value):
        return ctx_send(value, lambda c: c ^ 1)

    def to_chip(value, shift):
        return ctx_send(value, lambda c: ((c // CORES + shift) % chips) * CORES + c % CORES)

    def pick(value, index):
        return lax.dynamic_index_in_dim(value, index, 0, keepdims=False)

    def in_order(found, mine, size):
        out = []
        for place in range(size):
            chosen = found[0]
            for r in range(1, size):
                chosen = jnp.where((mine - place) % size == r, found[r], chosen)
            out.append(chosen)
        return jnp.stack(out)

    def chip_send(value):
        return [pick(value, chip)] + [
            to_chip(pick(value, (chip + r) % chips), r) for r in range(1, chips)
        ]

    def chip_join(found):
        return in_order(found, chip, chips)

    def chip_exchange(value):
        return chip_join(chip_send(value))

    def by_core(mine, other, axis=0):
        first = jnp.where(core == 0, mine, other)
        second = jnp.where(core == 0, other, mine)
        return jnp.stack([first, second], axis=axis)

    def exchange_all(value):
        return lax.all_to_all(value, everyone, split_axis=0, concat_axis=0, tiled=True)

    def by_pair(weight):
        return weight.astype(bf16).reshape(weight.shape[0], width // LANES, 1, LANES)

    exp_bits = [b for b in (2, 4, 8, 16) if b < n_exp]
    chip_bits = [b for b in (1, 2, 4, 8) if b < chips]

    def double(state, axis, bit):
        value, keys = state
        if axis == "exp":
            other = lax.ppermute(value, "exp", [(e, e ^ bit) for e in range(n_exp)])
            index, key = lax.axis_index("exp"), (0, -bit)
        else:
            other = ctx_send(value, lambda c: c ^ (bit * CORES))
            index, key = chip, (1, -bit)
        keys = sorted(keys + [key])
        at = keys.index(key)
        upper = (index & bit) != 0
        low, high = jnp.where(upper, other, value), jnp.where(upper, value, other)
        return jnp.stack([low, high], axis=at), keys

    def gather_cores(weight):
        kept = lax.dynamic_index_in_dim(weight, core, 1, keepdims=False)
        away = lax.dynamic_index_in_dim(weight, 1 - core, 1, keepdims=False)
        return by_core(kept, other_core(away)), [(2, 0)]

    def gather(state, steps):
        for axis, bit in steps:
            state = double(state, axis, bit)
        return state

    first_steps = [("exp", bit) for bit in exp_bits]
    last_steps = [("exp", 1)] + [("ctx", bit) for bit in chip_bits]

    local_qkv = jnp.concatenate(
        [by_pair(query_weight), by_pair(key_weight), by_pair(value_weight)], axis=2
    ).reshape(query_weight.shape[0], CORES, 3 * half)
    parts = 3 * half // 2

    gathered, keys = gather_cores(local_qkv)
    gathered, tokens, expert_ids, expert_out, cotangent = hold(
        (gathered, tokens, expert_ids, expert_out, cotangent)
    )

    ids_flat = expert_ids.reshape(rows)
    positions = ctx * span + jnp.arange(span)
    live = (positions[None, :] < lengths[:, None]).reshape(rows)
    onehot = ((ids_flat[:, None] == jnp.arange(all_experts)[None, :]) & live[:, None]).astype(
        jnp.int32
    )
    running = jnp.cumsum(onehot, axis=0)
    ranks = jnp.sum(onehot * (running - 1), axis=1)
    keep = live & (ranks < capacity)
    target = jnp.where(keep, ids_flat * capacity + ranks, -1)
    targets = target.reshape(chips, seqs, span)
    targets = [targets[:, s].reshape(chips * span) for s in range(seqs)]
    slots = all_experts * capacity

    inputs = tokens.astype(f32).reshape(rows, width)
    normal_one, inverse_one = norm_parts(inputs)
    act = (normal_one * gain_one + shift_one).astype(bf16).reshape(chips, seqs, span, width)
    tokens_four = tokens.reshape(chips, seqs, span, width)
    cotangent_four = cotangent.reshape(chips, seqs, span, width)
    acts = []
    for s in range(seqs):
        act_chip = chip_exchange(act[:, s])
        acts.append(by_core(act_chip, other_core(act_chip), axis=1).reshape(full, width))

    def sub_send(value, shift):
        return ctx_send(value, lambda c: ((c // group + shift) % experts) * group + c % group)

    def group_send(value, shift):
        return ctx_send(value, lambda c: (c // group) * group + (c % group + shift) % group)

    def casts(weight):
        own, *others = [pick(weight, (sub + r) % experts).astype(bf16) for r in range(experts)]
        return own, others

    def swap(others, parts):
        cut = shard // parts
        return [
            sub_send(low[n * cut : (n + 1) * cut], r)
            for r, low in enumerate(others, 1)
            for n in range(parts)
        ]

    state = gather((gathered, keys), first_steps)
    streams = [
        ((state[0][..., :parts], state[1]), last_steps),
        ((state[0][..., parts:], state[1]), last_steps[::-1]),
    ]
    streams = [(gather(part, steps[:1]), steps[1:]) for part, steps in streams]
    values = [part[0] for part, _ in streams]
    values, expert_in, expert_out, cotangent_late = hold(
        (values, expert_in, expert_out, cotangent)
    )
    grad_send = dispatch([target], [cotangent_late.reshape(rows, width)], slots)
    first_own, first_low = casts(expert_in)
    second_own, second_low = casts(expert_out)
    qkv_weights = [
        gather((value, part[1]), steps)[0].reshape(width, parts)
        for value, (part, steps) in zip(values, streams)
    ]
    out_low = output_weight.astype(bf16)
    acts, qkv_weights, grad_send, second_low, out_low = hold(
        (acts, qkv_weights, grad_send, second_low, out_low)
    )
    grad_arrived = exchange_all(grad_send)
    out_all = lax.all_gather(out_low, everyone, axis=0, tiled=True)
    second_far = swap(second_low, 4)

    lens = lax.dynamic_slice_in_dim(lengths, chip * seqs, seqs)
    halves = range(2)
    calls = 2 * seqs
    qkvs, mixed_parts, previous = [], [], None
    for s in range(seqs):
        qkvs.append([mm(acts[s], weight).astype(bf16) for weight in qkv_weights])
        for h in halves:
            call = s * 2 + h
            if call > 1:
                n = slice(call - 2, call - 1)
                qkvs[s][h], second_far[n] = hold((qkvs[s][h], second_far[n]))
            if call:
                qkvs[s][h], previous = hold((qkvs[s][h], previous))
            mixed_chip = attention_forward(lens[s : s + 1], qkvs[s][h], full)
            previous = mixed_chip
            if call == calls - 1:
                mixed_chip, grad_arrived, mixed_parts = hold(
                    (mixed_chip, grad_arrived, mixed_parts)
                )
            mixed_chip = mixed_chip.reshape(chips, CORES, span, half // 2)
            mixed_own = lax.dynamic_index_in_dim(mixed_chip, core, 1, keepdims=False)
            mixed_away = lax.dynamic_index_in_dim(mixed_chip, 1 - core, 1, keepdims=False)
            mixed_parts.append(chip_send(jnp.stack([mixed_own, other_core(mixed_away)], axis=1)))
    mixed_parts = [chip_join(found) for found in mixed_parts]

    g_parts = [grad_arrived] + [group_send(grad_arrived, r) for r in range(1, group)]

    out_weight = out_all.reshape(CORES, 2, half // 2, width)
    out_weight = jnp.stack([pick(out_weight, core), pick(out_weight, 1 - core)], axis=1)
    out_weight = out_weight.reshape(width, width)
    hiddens, sents, mixeds = zip(
        *[
            project_norm(
                mixed_parts[2 * s : 2 * s + 2], tokens_four, s, out_weight, gain_two, shift_two
            )
            for s in range(seqs)
        ]
    )
    arrived = exchange_all(dispatch(targets, sents, slots))

    sents, first_low = hold((sents, first_low))
    first_far = swap(first_low, 2)
    seconds, firsts = [[second_own], second_far], [[first_own], first_far]
    probs = []
    for h in halves:
        for s in range(seqs):
            part, _ = hold((qkvs[s][h], sents))
            probs.append(attention_probs(lens[s : s + 1], part, full))
    g_parts, probs = hold((g_parts, probs))
    activs_own = [grad_activ_pass(part, [second_own]) for part in g_parts]
    g_late = after(g_parts, activs_own)
    activs_far = [grad_activ_pass(part, seconds[1]) for part in g_late]
    arrived, activs_own, activs_far, first_own, probs = hold(
        (arrived, activs_own, activs_far, first_own, probs)
    )
    x_parts = [arrived] + [group_send(arrived, r) for r in range(1, group)]
    owns = [hidden_pass(arrived, activs_own[0], firsts[0], f32)]
    x_parts[-1], owns, first_far[0] = hold((x_parts[-1], owns, first_far[0]))
    for r in range(1, group):
        owns.append(hidden_pass(x_parts[r], activs_own[r], firsts[0], f32))
    fars = [None] * group
    for r in list(range(1, group)) + [0]:
        fars[r] = hidden_pass(
            x_parts[r], activs_far[r], firsts[1], f32 if r == 0 else bf16, owns[r][2]
        )

    def sum_group(terms):
        total = terms[0]
        for r in range(1, group):
            total = total + group_send(terms[r], group - r).astype(f32)
        return total.astype(bf16)

    activ_parts = [[one[0] for one in owns], [one[0] for one in fars]]
    grad_pre_parts = [[one[1] for one in owns], [one[1] for one in fars]]
    grad_sent_rows = sum_group([one[2] for one in fars])
    grad_back = exchange_all(grad_sent_rows)
    grad_sent_rows, activ_parts, grad_pre_parts = hold(
        (grad_sent_rows, activ_parts, grad_pre_parts)
    )

    def send_grad(far, n, parts):
        return sub_send(far[n], experts - 1 - n // parts)

    def own_grads(whole, arriving, parts):
        order = [(experts - 1 - r) * parts + n for r in range(1, experts) for n in range(parts)]
        return assemble(sub, whole, [arriving[n] for n in order])

    cuts = 2
    *second_away, second_whole = expert_grad_pass(
        sub, *activ_parts, g_parts, experts, cuts
    )
    activ_parts, second_away = hold((activ_parts, second_away))
    early = (experts - 1) * cuts // 2
    second_sent = [send_grad(second_away, n, cuts) for n in range(early)]
    by_rows = list(zip(*activ_parts))
    terms = [down_pass(by_rows[r], seconds, bf16) for r in range(1, group)]
    result_rows = sum_group([down_pass(by_rows[0], seconds, f32)] + terms)
    *first_away, first_whole = expert_grad_pass(
        sub, *grad_pre_parts, x_parts, experts, cuts
    )
    grad_back, second_sent, first_away = hold((grad_back, second_sent, first_away))

    grad_hiddens, branches, grad_mixeds, small_two = zip(
        *[
            project_back(
                targets[s], grad_back, hiddens[s], cotangent_four, s, out_weight, gain_two
            )
            for s in range(seqs)
        ]
    )
    gm_chip = [chip_exchange(part) for part in grad_mixeds]

    own = width // devices
    pairs = n_exp // 2
    exp = lax.axis_index("exp")
    odd = exp % 2
    alike = [
        [e * n_ctx + c for e in range(n_exp) if e % 2 == which for c in range(n_ctx)]
        for which in range(2)
    ]
    tile = width // n_exp
    split = tile % LANES == 0

    def blocks_of(groups):
        if split:
            return split_grad_pass(groups, tile)
        terms = jnp.concatenate(
            [
                weight_grad_pass(lefts, rights).reshape(n_exp, tile, -1)[order]
                for order, lefts, rights in groups
            ],
            axis=2,
        )
        return [terms[:pairs].reshape(width // 2, -1), terms[pairs:].reshape(width // 2, -1)]

    def halve(away, kept):
        return kept, lax.ppermute(away, "exp", [(e, e ^ 1) for e in range(n_exp)])

    def joined(halved):
        total = add_terms(halved)
        return total.reshape(pairs * n_ctx, own, total.shape[1])

    def to_owner(terms):
        got = lax.all_to_all(
            terms, everyone, split_axis=0, concat_axis=0, tiled=True, axis_index_groups=alike
        )
        return got.astype(f32)

    def by_core_cols(got):
        got = jnp.sum(got.reshape(-1, CORES, own, got.shape[2]), axis=0)
        return jnp.transpose(got, (1, 0, 2))

    evens = jnp.arange(pairs, dtype=jnp.int32) * 2
    plain = jnp.concatenate([evens + 1 - odd, evens + odd])
    steps = n_exp // 4
    true_core, true_half, place = plain // (2 * steps), plain // steps % 2, plain % steps
    mixed_order = (true_half * CORES + (true_core + core) % CORES) * steps + place
    gm_chip, result_rows, second_away, first_away = hold(
        (gm_chip, result_rows, second_away, first_away)
    )
    gm_parts = [
        by_core(part[:, 0], other_core(part[:, 1]), axis=1).reshape(full, half) for part in gm_chip
    ]
    returned = exchange_all(result_rows)
    second_sent += [send_grad(second_away, n, cuts) for n in range(early, len(second_away))]

    wo_terms = halve(*blocks_of([(mixed_order, mixeds, branches)]))
    grad_qkvs = [[None, None] for s in range(seqs)]
    found_parts, w_terms, first_sent, previous = [], [], [], None
    call = 0
    for h in halves:
        for s in range(seqs):
            cols = slice(h * half // 2, (h + 1) * half // 2)
            gm_part = gm_parts[s][:, cols]
            if call == 0:
                first_sent = [send_grad(first_away, n, cuts) for n in range(len(first_away))]
            if call:
                gm_part, previous = hold((gm_part, previous))
            if call == calls - 2:
                gm_part, second_sent, wo_terms = hold((gm_part, second_sent, wo_terms))
            if call == calls - 1:
                gm_part, returned = hold((gm_part, returned))
            previous = attention_backward(qkvs[s][h], gm_part, probs[call])
            grad_qkvs[s][h] = previous
            call += 1
            if s == seqs - 1:
                terms = blocks_of([(plain, acts, [grad_qkvs[i][h] for i in range(seqs)])])
                previous, terms = hold((grad_qkvs[s][h], terms))
                grad_qkvs[s][h] = previous
                w_terms.append(halve(*terms))
            if h == 1:
                if call == calls - 1:
                    grad_qkvs[s][h], w_terms[0], first_sent[0] = hold(
                        (grad_qkvs[s][h], w_terms[0], first_sent[0])
                    )
                if call == calls:
                    grad_qkvs[s][h], found_parts = hold((grad_qkvs[s][h], found_parts))
                away, kept = grad_act_pass(core, grad_qkvs[s], qkv_weights, chips)
                previous, kept = hold((previous, kept))
                total = (kept.astype(f32) + other_core(away).astype(f32)).astype(bf16)
                if call == calls:
                    total, w_terms[1] = hold((total, w_terms[1]))
                found_parts.append(chip_send(total))
                grad_qkvs[s][h] = previous
    returned, second_whole, first_whole = (
        after(value, previous) for value in (returned, second_whole, first_whole)
    )
    value = joined([w_terms[1]])
    columns = value.shape[2]
    first = True
    upper_bits = [b for b in (2, 4, 8, 16) if b < n_exp]
    axes = [("exp", b) for b in upper_bits[::-1]] + [("ctx", b) for b in chip_bits[::-1]]
    value = value.reshape((2,) * len(axes) + (CORES, own, columns))
    for step in axes[::-1]:
        axis, bit = step
        at = axes.index(step)
        index = exp if axis == "exp" else chip
        upper = jnp.where((index & bit) != 0, 1, 0)
        kept = lax.dynamic_index_in_dim(value, upper, at, keepdims=False)
        away = lax.dynamic_index_in_dim(value, 1 - upper, at, keepdims=False)
        if axis == "exp":
            other = lax.ppermute(away, "exp", [(e, e ^ bit) for e in range(n_exp)])
        else:
            other = ctx_send(away, lambda c: c ^ (bit * CORES))
        if first:
            other, first_sent[1:], found_parts = hold((other, first_sent[1:], found_parts))
            first = False
        value = (kept.astype(f32) + other.astype(f32)).astype(bf16)
        axes.remove(step)
    second_sum = by_core(
        pick(value, core), other_core(pick(value, 1 - core)), axis=1
    ).astype(f32)
    grad_act_parts = [chip_join(found) for found in found_parts]
    grad_expert_out = own_grads(second_whole, second_sent, cuts)
    grad_expert_in = own_grads(first_whole, first_sent, cuts)
    first_sum = to_owner(joined([w_terms[0], wo_terms]))
    grad_output = jnp.sum(first_sum[:, :, parts:], axis=0)
    grad_w = jnp.concatenate([by_core_cols(first_sum[:, :, :parts]), second_sum], axis=2)
    grad_w = grad_w.reshape(own, width // LANES, 3, LANES)
    grad_query, grad_key, grad_value = (grad_w[:, :, t].reshape(own, width) for t in range(3))

    def by_seq(values):
        return jnp.stack([value.reshape(chips, span, width) for value in values], axis=1)

    blocks = [combine(targets[s], returned, hiddens[s]) for s in range(seqs)]
    block_out = by_seq(blocks).reshape(tokens.shape)

    grad_act_own = jnp.stack(grad_act_parts, axis=1).reshape(rows, width).astype(f32)
    grad_gain_one = jnp.sum(grad_act_own * normal_one, axis=0)
    grad_shift_one = jnp.sum(grad_act_own, axis=0)
    grad_hidden = by_seq(grad_hiddens).reshape(rows, width)
    grad_tokens = grad_hidden + norm_back(grad_act_own, normal_one, inverse_one, gain_one)
    grad_tokens = grad_tokens.astype(bf16).reshape(tokens.shape)
    small_two = sum(small_two)
    small = jnp.stack(
        [
            value.reshape(devices, own)
            for value in (grad_gain_one, grad_shift_one, small_two[0], small_two[1])
        ],
        axis=1,
    )
    small = jnp.sum(exchange_all(small), axis=0)
    return (
        block_out,
        grad_tokens,
        grad_query,
        grad_key,
        grad_value,
        grad_output,
        small[0],
        small[1],
        small[2],
        small[3],
        grad_expert_in,
        grad_expert_out,
    )


def solution(mesh):
    rows = P("exp", "ctx", None)
    weight = P(("exp", "ctx"), None)
    vector = P(("exp", "ctx"))
    return jax.shard_map(
        body,
        mesh=mesh,
        in_specs=(
            rows,
            P("exp"),
            P("ctx", "exp", None, None),
            rows,
            weight,
            weight,
            weight,
            weight,
            P(),
            P(),
            P(),
            P(),
            rows,
            rows,
        ),
        out_specs=(rows, rows, weight, weight, weight, weight)
        + (vector, vector, vector, vector)
        + (rows, rows),
        check_vma=False,
    )
```

```python
import functools

import jax
import jax.numpy as jnp
from jax import lax
from jax.experimental import pallas as pl
from jax.experimental.pallas import tpu as pltpu
from jax.sharding import PartitionSpec as P

HEAD_DIM = 64
LANES = 128
PAIR = 3 * LANES
BLOCK = 256
LOG2E = 1.4426950408889634
CORES = 2

eps_norm = 1e-05
masked_score = -1e30
f32 = jnp.float32
bf16 = jnp.bfloat16
NN = (((1,), (0,)), ((), ()))
NT = (((1,), (1,)), ((), ()))
TN = (((0,), (0,)), ((), ()))
VMEM_LIMIT = 56 * 1024 * 1024
PARAMS = pltpu.CompilerParams(vmem_limit_bytes=VMEM_LIMIT)


def cost(flops):
    return pl.CostEstimate(flops=int(flops / 10), bytes_accessed=1024, transcendentals=0)


hold = lax.optimization_barrier


def after(value, *others):
    return hold((value, others))[0]


def mm(a, b, dims=NN):
    return lax.dot_general(a, b, dims, preferred_element_type=f32)


def head_operands(length, q, k):
    full = q.shape[0]
    lane = lax.broadcasted_iota(jnp.int32, (full, LANES), 1)
    pos = lax.broadcasted_iota(jnp.int32, (full, LANES), 0)
    bias = jnp.where(pos < length, 0.0, masked_score).astype(f32)
    inside, q_aug, k_aug = [], [], []
    for head in range(2):
        own = (lane // HEAD_DIM) == head
        spare = lane == HEAD_DIM * (1 - head)
        inside.append(own)
        q_aug.append(jnp.where(own, q, jnp.where(spare, 1.0, 0.0)).astype(bf16))
        k_aug.append(jnp.where(own, k, jnp.where(spare, bias, 0.0)).astype(bf16))
    return inside, q_aug, k_aug


def attention_forward_kernel(len_ref, x_ref, o_ref):
    full = x_ref.shape[0]
    q, k, v = (x_ref[:, LANES * t : LANES * (t + 1)].astype(f32) for t in range(3))
    inside, q_aug, k_aug = head_operands(len_ref[pl.program_id(0)], q, k)
    v_own = [jnp.where(own, v, 0.0).astype(bf16) for own in inside]
    to_log2 = HEAD_DIM**-0.5 * LOG2E
    row = lax.broadcasted_iota(jnp.int32, (BLOCK, BLOCK), 0)
    col = lax.broadcasted_iota(jnp.int32, (BLOCK, BLOCK), 1)
    causal = col <= row
    for i in range(full // BLOCK):
        here, before = slice(i * BLOCK, (i + 1) * BLOCK), slice(0, i * BLOCK)
        total = jnp.zeros((BLOCK, LANES), f32)
        for head in range(2):
            qi = q_aug[head][here]
            s_here = jnp.where(causal, mm(qi, k_aug[head][here], NT) * to_log2, masked_score)
            top = jnp.max(s_here, axis=1, keepdims=True)
            if i:
                s_before = mm(qi, k_aug[head][before], NT) * to_log2
                top = jnp.maximum(top, jnp.max(s_before, axis=1, keepdims=True))
            p_here = jnp.exp2(s_here - top)
            mass = jnp.sum(p_here, axis=1, keepdims=True)
            if i:
                p_before = jnp.exp2(s_before - top)
                mass = mass + jnp.sum(p_before, axis=1, keepdims=True)
            inverse = 1.0 / mass
            total = total + mm((p_here * inverse).astype(bf16), v_own[head][here])
            if i:
                total = total + mm((p_before * inverse).astype(bf16), v_own[head][before])
        o_ref[here, :] = total.astype(bf16)


def attention_forward(lens, qkv, full):
    n_seq, pairs = qkv.shape[0] // full, qkv.shape[1] // PAIR
    return pl.pallas_call(
        attention_forward_kernel,
        grid_spec=pltpu.PrefetchScalarGridSpec(
            num_scalar_prefetch=1,
            grid=(n_seq, pairs),
            in_specs=[pl.BlockSpec((full, PAIR), lambda s, p, l: (s, p))],
            out_specs=pl.BlockSpec((full, LANES), lambda s, p, l: (s, p)),
        ),
        out_shape=jax.ShapeDtypeStruct((n_seq * full, pairs * LANES), bf16),
        compiler_params=PARAMS,
        cost_estimate=cost(n_seq * pairs * 2.5e9),
        name="attention_forward",
    )(lens, qkv)


def attention_probs_kernel(len_ref, x_ref, p_ref):
    full = x_ref.shape[0]
    q, k = (x_ref[:, LANES * t : LANES * (t + 1)].astype(f32) for t in range(2))
    _, q_aug, k_aug = head_operands(len_ref[pl.program_id(0)], q, k)
    to_log2 = HEAD_DIM**-0.5 * LOG2E
    row = lax.broadcasted_iota(jnp.int32, (BLOCK, BLOCK), 0)
    col = lax.broadcasted_iota(jnp.int32, (BLOCK, BLOCK), 1)
    causal = row <= col
    for i in range(full // BLOCK):
        here, before = slice(i * BLOCK, (i + 1) * BLOCK), slice(0, i * BLOCK)
        for head in range(2):
            qi = q_aug[head][here]
            s_here = jnp.where(causal, mm(k_aug[head][here], qi, NT) * to_log2, masked_score)
            top = jnp.max(s_here, axis=0, keepdims=True)
            if i:
                s_before = mm(k_aug[head][before], qi, NT) * to_log2
                top = jnp.maximum(top, jnp.max(s_before, axis=0, keepdims=True))
            p_here = jnp.exp2(s_here - top)
            mass = jnp.sum(p_here, axis=0, keepdims=True)
            if i:
                p_before = jnp.exp2(s_before - top)
                mass = mass + jnp.sum(p_before, axis=0, keepdims=True)
            inverse = 1.0 / mass
            p_ref[head, here, here] = (p_here * inverse).astype(bf16)
            if i:
                p_ref[head, before, here] = (p_before * inverse).astype(bf16)


def attention_probs(lens, qkv, full):
    n_seq, pairs = qkv.shape[0] // full, qkv.shape[1] // PAIR
    return pl.pallas_call(
        attention_probs_kernel,
        grid_spec=pltpu.PrefetchScalarGridSpec(
            num_scalar_prefetch=1,
            grid=(n_seq, pairs),
            in_specs=[pl.BlockSpec((full, PAIR), lambda s, p, l: (s, p))],
            out_specs=pl.BlockSpec((2, full, full), lambda s, p, l: (s * pairs + p, 0, 0)),
        ),
        out_shape=jax.ShapeDtypeStruct((n_seq * pairs * 2, full, full), bf16),
        compiler_params=PARAMS,
        cost_estimate=cost(n_seq * pairs * 2.0e9),
        name="attention_probs",
    )(lens, qkv)


def attention_backward_kernel(x_ref, g_ref, p_ref, o_ref, d_scr):
    full = x_ref.shape[0]
    q, k = (x_ref[:, LANES * t : LANES * (t + 1)].astype(f32) for t in range(2))
    v = x_ref[:, 2 * LANES : 3 * LANES]
    g = g_ref[...].astype(f32)
    head_of = lax.broadcasted_iota(jnp.int32, (full, LANES), 1) // HEAD_DIM
    inside = [head_of == head for head in range(2)]
    q_own = [jnp.where(own, q, 0.0).astype(bf16) for own in inside]
    k_own = [jnp.where(own, k, 0.0).astype(bf16) for own in inside]
    g_own = [jnp.where(own, g, 0.0).astype(bf16) for own in inside]
    scale = HEAD_DIM**-0.5
    count = full // BLOCK
    for i in range(count):
        here, until = slice(i * BLOCK, (i + 1) * BLOCK), slice(0, (i + 1) * BLOCK)
        dq = jnp.zeros((BLOCK, LANES), f32)
        for head in range(2):
            probs = p_ref[head, until, here].astype(f32)
            grad = mm(v[until], g_own[head][here], NT)
            delta = jnp.sum(grad * probs, axis=0, keepdims=True)
            d_score = (probs * (grad - delta)).astype(bf16)
            d_scr[head, until, here] = d_score
            dq = dq + mm(d_score, k_own[head][until], TN)
        o_ref[here, 0:LANES] = (dq * scale).astype(bf16)
    for j in range(count):
        here, after_ = slice(j * BLOCK, (j + 1) * BLOCK), slice(j * BLOCK, full)
        dk = mm(d_scr[0, here, after_], q_own[0][after_]) + mm(
            d_scr[1, here, after_], q_own[1][after_]
        )
        dv = mm(p_ref[0, here, after_], g_own[0][after_]) + mm(
            p_ref[1, here, after_], g_own[1][after_]
        )
        o_ref[here, LANES : 2 * LANES] = (dk * scale).astype(bf16)
        o_ref[here, 2 * LANES : 3 * LANES] = dv.astype(bf16)


def attention_backward(qkv, g, probs):
    full = probs.shape[1]
    n_seq, pairs = qkv.shape[0] // full, qkv.shape[1] // PAIR
    return pl.pallas_call(
        attention_backward_kernel,
        grid=(n_seq, pairs),
        in_specs=[
            pl.BlockSpec((full, PAIR), lambda s, p: (s, p)),
            pl.BlockSpec((full, LANES), lambda s, p: (s, p)),
            pl.BlockSpec((2, full, full), lambda s, p: (s * pairs + p, 0, 0)),
        ],
        out_specs=pl.BlockSpec((full, PAIR), lambda s, p: (s, p)),
        scratch_shapes=[pltpu.VMEM((2, full, full), bf16)],
        out_shape=jax.ShapeDtypeStruct(qkv.shape, bf16),
        compiler_params=PARAMS,
        cost_estimate=cost(n_seq * pairs * 3.0e9),
        name="attention_backward",
    )(qkv, g, probs)


def tile_of(count, most=320):
    return max(t for t in range(16, most + 1, 16) if count % t == 0)


def pieces_of(shards):
    start = 0
    for ref in shards:
        size = min(512, ref.shape[0])
        for h in range(0, ref.shape[0], size):
            yield ref, slice(h, h + size), slice(start, start + size)
            start += size


def shard_specs(shards):
    return [pl.BlockSpec(w.shape, lambda i: (0, 0)) for w in shards]


def hidden_of(shards):
    return sum(w.shape[0] for w in shards)


def grad_activ_kernel(g_ref, *refs):
    for w_ref, part, cols in pieces_of(refs[:-1]):
        refs[-1][:, cols] = mm(g_ref[...], w_ref[part, :], NT).astype(bf16)


def grad_activ_pass(g, shards):
    (count, width), hidden = g.shape, hidden_of(shards)
    tile = tile_of(count)
    return pl.pallas_call(
        grad_activ_kernel,
        grid=(count // tile,),
        in_specs=[pl.BlockSpec((tile, width), lambda i: (i, 0))] + shard_specs(shards),
        out_specs=pl.BlockSpec((tile, hidden), lambda i: (i, 0)),
        out_shape=jax.ShapeDtypeStruct((count, hidden), bf16),
        compiler_params=PARAMS,
        cost_estimate=cost(count * hidden * width / 2),
        name="grad_activ_pass",
    )(g, *shards)


def hidden_kernel(x_ref, ga_ref, *refs, before):
    shards, (a_ref, gp_ref, gs_ref) = refs[before:-3], refs[-3:]
    for w_ref, part, cols in pieces_of(shards):
        activ, slope = gelu_parts(mm(x_ref[...], w_ref[part, :], NT))
        a_ref[:, cols] = activ.astype(bf16)
        gp_ref[:, cols] = (ga_ref[:, cols].astype(f32) * slope).astype(bf16)
    total = product_of(gp_ref, shards)
    if before:
        total = total + refs[0][...]
    gs_ref[...] = total.astype(gs_ref.dtype)


def product_of(rows_ref, shards):
    total, start = None, 0
    for w_ref in shards:
        cols = slice(start, start + w_ref.shape[0])
        part = mm(rows_ref[:, cols], w_ref[...])
        total = part if total is None else total + part
        start += w_ref.shape[0]
    return total


def hidden_pass(x, grad_activ, shards, dtype, before=None):
    (count, width), hidden = x.shape, hidden_of(shards)
    tile = tile_of(count)
    wide = pl.BlockSpec((tile, hidden), lambda i: (i, 0))
    thin = pl.BlockSpec((tile, width), lambda i: (i, 0))
    more = [] if before is None else [before]
    return pl.pallas_call(
        functools.partial(hidden_kernel, before=len(more)),
        grid=(count // tile,),
        in_specs=[thin, wide] + [thin] * len(more) + shard_specs(shards),
        out_specs=[wide, wide, thin],
        out_shape=[jax.ShapeDtypeStruct((count, hidden), bf16)] * 2
        + [jax.ShapeDtypeStruct((count, width), dtype)],
        compiler_params=PARAMS,
        cost_estimate=cost(2 * count * hidden * width),
        name="hidden_pass",
    )(x, grad_activ, *more, *shards)


def down_kernel(*refs, own, more):
    last = len(refs) - 1 - more
    total = product_of(refs[0], refs[2 : 2 + own]) + product_of(refs[1], refs[2 + own : last])
    for term in refs[last:-1]:
        total = total + term[...].astype(f32)
    refs[-1][...] = total.astype(bf16)


def down_pass(activs, groups, terms=()):
    count, width = activs[0].shape[0], groups[0][0].shape[1]
    tile = tile_of(count)
    shards = list(groups[0]) + list(groups[1])
    return pl.pallas_call(
        functools.partial(down_kernel, own=len(groups[0]), more=len(terms)),
        grid=(count // tile,),
        in_specs=[pl.BlockSpec((tile, a.shape[1]), lambda i: (i, 0)) for a in activs]
        + shard_specs(shards)
        + [pl.BlockSpec((tile, width), lambda i: (i, 0)) for _ in terms],
        out_specs=pl.BlockSpec((tile, width), lambda i: (i, 0)),
        out_shape=jax.ShapeDtypeStruct((count, width), bf16),
        compiler_params=PARAMS,
        cost_estimate=cost(2 * count * hidden_of(shards) * width),
        name="down_pass",
    )(*activs, *shards, *terms)


def summed(lefts, rights):
    total = mm(lefts[0][...], rights[0][...], TN)
    for left, right in zip(lefts[1:], rights[1:]):
        total = total + mm(left[...], right[...], TN)
    return total


def weight_grad_kernel(*refs):
    count = len(refs) // 2
    refs[-1][...] = summed(refs[:count], refs[count:-1]).astype(bf16)


def weight_grad_pass(lefts, rights):
    hidden, width = lefts[0].shape[1], rights[0].shape[1]
    tile = min(256, hidden)
    return pl.pallas_call(
        weight_grad_kernel,
        grid=(hidden // tile,),
        in_specs=[pl.BlockSpec((v.shape[0], tile), lambda i: (0, i)) for v in lefts]
        + [pl.BlockSpec(v.shape, lambda i: (0, 0)) for v in rights],
        out_specs=pl.BlockSpec((tile, width), lambda i: (i, 0)),
        out_shape=jax.ShapeDtypeStruct((hidden, width), bf16),
        compiler_params=PARAMS,
        cost_estimate=cost(2 * lefts[0].size * width * len(lefts)),
        name="weight_grad_pass",
    )(*lefts, *rights)


def split_grad_kernel(order_ref, *refs, tile, counts):
    values, start, col = refs[:-2], 0, 0
    steps = order_ref.shape[0] // len(counts)
    totals = []
    for group, count in enumerate(counts):
        lefts, rights = values[start : start + count], values[start + count : start + 2 * count]
        first = group * steps + pl.program_id(0) * (steps // 2)
        places = [order_ref[first + n] for n in range(steps // 2)]
        total = None
        for left, right in zip(lefts, rights):
            chosen = jnp.concatenate(
                [left[:, pl.ds(pl.multiple_of(place * tile, tile), tile)] for place in places],
                axis=1,
            )
            part = mm(chosen, right[...], TN)
            total = part if total is None else total + part
        totals.append((slice(col, col + total.shape[1]), total.astype(bf16)))
        start += 2 * count
        col += total.shape[1]

    for which in range(2):

        @pl.when(pl.program_id(0) == which)
        def _(which=which):
            for cols, total in totals:
                refs[which - 2][:, cols] = total


def split_grad_pass(groups, tile):
    hidden = groups[0][1][0].shape[1]
    width = sum(rights[0].shape[1] for _, _, rights in groups)
    values = [v for _, lefts, rights in groups for v in (*lefts, *rights)]
    out = jax.ShapeDtypeStruct((hidden // 2, width), bf16)
    return pl.pallas_call(
        functools.partial(split_grad_kernel, tile=tile, counts=[len(g[1]) for g in groups]),
        grid_spec=pltpu.PrefetchScalarGridSpec(
            num_scalar_prefetch=1,
            grid=(2,),
            in_specs=[pl.BlockSpec(v.shape, lambda i, o: (0, 0)) for v in values],
            out_specs=[pl.BlockSpec(out.shape, lambda i, o: (0, 0))] * 2,
        ),
        out_shape=[out, out],
        compiler_params=PARAMS,
        cost_estimate=cost(2 * width * sum(v.size for v in groups[0][1])),
        name="split_grad_pass",
    )(jnp.concatenate([order for order, _, _ in groups]), *values)


def add_terms_kernel(*refs):
    col = 0
    for one, two in zip(refs[0:-1:2], refs[1:-1:2]):
        cols = slice(col, col + one.shape[1])
        refs[-1][:, cols] = (one[...].astype(f32) + two[...].astype(f32)).astype(bf16)
        col = cols.stop


def add_terms(pairs):
    count = pairs[0][0].shape[0]
    tile = min(128, count)
    values = [v for pair in pairs for v in pair]
    width = sum(pair[0].shape[1] for pair in pairs)
    return pl.pallas_call(
        add_terms_kernel,
        grid=(count // tile,),
        in_specs=[pl.BlockSpec((tile, v.shape[1]), lambda i: (i, 0)) for v in values],
        out_specs=pl.BlockSpec((tile, width), lambda i: (i, 0)),
        out_shape=jax.ShapeDtypeStruct((count, width), bf16),
        compiler_params=PARAMS,
        cost_estimate=cost(3.0e10),
        name="add_terms",
    )(*values)


def expert_grad_kernel(sub_ref, *refs, count, pieces, per):
    step = pl.program_id(0)
    rights = refs[2 * count : 3 * count]

    @pl.when(step < pieces * per)
    def _():
        total = summed(refs[count : 2 * count], rights).astype(bf16)
        for n in range(pieces):

            @pl.when((step >= n * per) & (step < (n + 1) * per))
            def _(n=n):
                refs[3 * count + n][...] = total

    @pl.when(step >= pieces * per)
    def _():
        refs[-1][0] = summed(refs[:count], rights)


def expert_grad_pass(sub, owns, others, rights, experts, parts):
    shard, width = owns[0].shape[1], rights[0].shape[1]
    tile = min(256, shard // parts)
    pieces, per, own = (experts - 1) * parts, shard // parts // tile, shard // tile
    far = pieces * per

    def piece_spec(n):
        return pl.BlockSpec((tile, width), lambda i, s: (jnp.clip(i - n * per, 0, per - 1), 0))

    return pl.pallas_call(
        functools.partial(expert_grad_kernel, count=len(owns), pieces=pieces, per=per),
        grid_spec=pltpu.PrefetchScalarGridSpec(
            num_scalar_prefetch=1,
            grid=(far + own,),
            in_specs=[
                pl.BlockSpec((v.shape[0], tile), lambda i, s: (0, jnp.clip(i - far, 0, own - 1)))
                for v in owns
            ]
            + [
                pl.BlockSpec((v.shape[0], tile), lambda i, s: (0, jnp.clip(i, 0, far - 1)))
                for v in others
            ]
            + [pl.BlockSpec(v.shape, lambda i, s: (0, 0)) for v in rights],
            out_specs=[piece_spec(n) for n in range(pieces)]
            + [
                pl.BlockSpec(
                    (1, tile, width), lambda i, s: (s[0], jnp.clip(i - far, 0, own - 1), 0)
                )
            ],
        ),
        out_shape=[jax.ShapeDtypeStruct((shard // parts, width), bf16)] * pieces
        + [jax.ShapeDtypeStruct((experts, shard, width), f32)],
        compiler_params=PARAMS,
        cost_estimate=cost(2 * experts * owns[0].size * width * len(owns)),
        name="expert_grad_pass",
    )(sub.reshape(1), *owns, *others, *rights)


def assemble_kernel(sub_ref, whole_ref, *refs):
    pieces, o_ref = refs[:-1], refs[-1]
    for n, piece in enumerate(pieces):

        @pl.when(pl.program_id(0) * pl.num_programs(1) + pl.program_id(1) == n)
        def _(piece=piece):
            o_ref[0] = piece[...].astype(f32)


def assemble(sub, whole, pieces):
    experts = whole.shape[0]
    parts = len(pieces) // (experts - 1)
    cut, width = pieces[0].shape

    def place(r, n, s):
        return (lax.rem(s[0] - r - 1 + experts, experts), n, 0)

    return pl.pallas_call(
        assemble_kernel,
        grid_spec=pltpu.PrefetchScalarGridSpec(
            num_scalar_prefetch=1,
            grid=(experts - 1, parts),
            in_specs=[pl.BlockSpec(memory_space=pl.ANY)]
            + [pl.BlockSpec((cut, width), lambda r, n, s: (0, 0)) for _ in pieces],
            out_specs=pl.BlockSpec((1, cut, width), place),
        ),
        out_shape=jax.ShapeDtypeStruct(whole.shape, f32),
        input_output_aliases={1: 0},
        compiler_params=PARAMS,
        cost_estimate=cost(3.0e10),
        name="assemble",
    )(sub.reshape(1), whole, *pieces)


def gelu_parts(pre):
    outer, inner = 0.7978845608028654, 0.044715
    square = pre * pre
    half = 0.5 + 0.5 * jnp.tanh(pre * (outer + outer * inner * square))
    value = pre * half
    slope = half + value * (1.0 - half) * (2.0 * outer + 6.0 * outer * inner * square)
    return value, slope


def dispatch_kernel(*refs):
    o_ref, count = refs[-1], len(refs) // 2
    tile = o_ref.shape[0]
    total = None
    for t_ref, v_ref in zip(refs[:count], refs[count:-1]):
        rows = v_ref.shape[0]
        slot = lax.broadcasted_iota(jnp.int32, (tile, rows), 0) + pl.program_id(0) * tile
        chosen = jnp.where(t_ref[...] == slot, 1.0, 0.0).astype(bf16)
        part = mm(chosen, v_ref[...])
        total = part if total is None else total + part
    o_ref[...] = total.astype(bf16)


def dispatch(targets, values, slots):
    tile, width = tile_of(slots), values[0].shape[1]
    return pl.pallas_call(
        dispatch_kernel,
        grid=(slots // tile,),
        in_specs=[pl.BlockSpec((1, v.shape[0]), lambda i: (0, 0)) for v in values]
        + [pl.BlockSpec(v.shape, lambda i: (0, 0)) for v in values],
        out_specs=pl.BlockSpec((tile, width), lambda i: (i, 0)),
        out_shape=jax.ShapeDtypeStruct((slots, width), bf16),
        compiler_params=PARAMS,
        cost_estimate=cost(2 * slots * width * sum(v.shape[0] for v in values)),
        name="dispatch",
    )(*[t.reshape(1, -1) for t in targets], *values)


def returned_rows(target, rows_ref):
    slots = rows_ref.shape[0]
    slot = lax.broadcasted_iota(jnp.int32, (target.shape[0], slots), 1)
    return mm(jnp.where(target == slot, 1.0, 0.0).astype(bf16), rows_ref[...])


def combine_kernel(t_ref, rows_ref, h_ref, *refs):
    refs[-1][0, 0] = (h_ref[...] + returned_rows(t_ref[...], rows_ref)).astype(bf16)


def into_whole(whole, place):
    if whole is None:
        return [], [], {}
    return [pl.BlockSpec(memory_space=pl.ANY)], [whole], {place: 0}


def combine(target, rows, hidden, shape, seq, whole):
    chips, _, span, width = shape
    specs, arrays, aliases = into_whole(whole, 3)
    return pl.pallas_call(
        combine_kernel,
        grid=(chips,),
        in_specs=[
            pl.BlockSpec((span, 1), lambda j: (j, 0)),
            pl.BlockSpec(rows.shape, lambda j: (0, 0)),
            pl.BlockSpec((span, width), lambda j: (j, 0)),
        ]
        + specs,
        out_specs=pl.BlockSpec((1, 1, span, width), lambda j: (j, seq, 0, 0)),
        out_shape=jax.ShapeDtypeStruct(shape, bf16),
        input_output_aliases=aliases,
        compiler_params=PARAMS,
        cost_estimate=cost(20 * chips * span * width * rows.shape[0]),
        name="combine",
    )(target.reshape(-1, 1), rows, hidden, *arrays)


def project_kernel(a_ref, b_ref, t_ref, w_ref, gain_ref, shift_ref, h_ref, s_ref, m_ref):
    mixed = jnp.concatenate([a_ref[0, 0], a_ref[0, 1], b_ref[0, 0], b_ref[0, 1]], axis=1)
    m_ref[...] = mixed
    hidden = t_ref[0, 0].astype(f32) + mm(mixed, w_ref[...])
    h_ref[...] = hidden
    normal, _ = norm_parts(hidden)
    s_ref[...] = (normal * gain_ref[...] + shift_ref[...]).astype(bf16)


def project_norm(parts, tokens, seq, weight, gain, shift):
    chips, cores, span, cols = parts[0].shape
    width = tokens.shape[3]
    block = pl.BlockSpec((1, cores, span, cols), lambda j: (j, 0, 0, 0))
    row = pl.BlockSpec((1, width), lambda j: (0, 0))
    out = pl.BlockSpec((span, width), lambda j: (j, 0))
    return pl.pallas_call(
        project_kernel,
        grid=(chips,),
        in_specs=[
            block,
            block,
            pl.BlockSpec((1, 1, span, width), lambda j: (j, seq, 0, 0)),
            pl.BlockSpec((width, width), lambda j: (0, 0)),
            row,
            row,
        ],
        out_specs=[out] * 3,
        out_shape=[
            jax.ShapeDtypeStruct((chips * span, width), dtype) for dtype in (f32, bf16, bf16)
        ],
        compiler_params=PARAMS,
        cost_estimate=cost(2 * chips * span * width * width),
        name="project_norm",
    )(*parts, tokens, weight, gain.reshape(1, -1), shift.reshape(1, -1))


def project_back_kernel(
    t_ref, rows_ref, h_ref, c_ref, w_ref, gain_ref, gh_ref, gb_ref, gm_ref, small_ref
):
    grad = returned_rows(t_ref[...], rows_ref)
    normal, inverse = norm_parts(h_ref[...])
    grad_hidden = c_ref[0, 0].astype(f32) + norm_back(grad, normal, inverse, gain_ref[...])
    gh_ref[...] = grad_hidden
    branch = grad_hidden.astype(bf16)
    gb_ref[...] = branch
    mixed = mm(branch, w_ref[...], NT).astype(bf16)
    cols = gm_ref.shape[3] // 2
    for half in range(2):
        for k in range(CORES):
            at = (half * CORES + k) * cols
            gm_ref[0, k, :, half * cols : (half + 1) * cols] = mixed[:, at : at + cols]
    sums = jnp.concatenate(
        [
            jnp.sum(grad * normal, axis=0, keepdims=True),
            jnp.sum(grad, axis=0, keepdims=True),
        ],
        axis=0,
    )

    @pl.when(pl.program_id(0) == 0)
    def _():
        small_ref[...] = sums

    @pl.when(pl.program_id(0) > 0)
    def _():
        small_ref[...] += sums


def project_back(target, rows, hidden, cotangent, seq, weight, gain):
    chips, _, span, width = cotangent.shape
    out = pl.BlockSpec((span, width), lambda j: (j, 0))
    return pl.pallas_call(
        project_back_kernel,
        grid=(chips,),
        in_specs=[
            pl.BlockSpec((span, 1), lambda j: (j, 0)),
            pl.BlockSpec(rows.shape, lambda j: (0, 0)),
            out,
            pl.BlockSpec((1, 1, span, width), lambda j: (j, seq, 0, 0)),
            pl.BlockSpec((width, width), lambda j: (0, 0)),
            pl.BlockSpec((1, width), lambda j: (0, 0)),
        ],
        out_specs=[
            out,
            out,
            pl.BlockSpec((1, CORES, span, width // CORES), lambda j: (j, 0, 0, 0)),
            pl.BlockSpec((2, width), lambda j: (0, 0)),
        ],
        out_shape=[
            jax.ShapeDtypeStruct((chips * span, width), f32),
            jax.ShapeDtypeStruct((chips * span, width), bf16),
            jax.ShapeDtypeStruct((chips, CORES, span, width // CORES), bf16),
            jax.ShapeDtypeStruct((2, width), f32),
        ],
        compiler_params=PARAMS,
        cost_estimate=cost(6 * chips * span * width * width),
        name="project_back",
    )(target.reshape(-1, 1), rows, hidden, cotangent, weight, gain.reshape(1, -1))


def grad_act_kernel(core_ref, *refs):
    count = (len(refs) - 2) // 2
    total = None
    for d_ref, w_ref in zip(refs[:count], refs[count:-2]):
        part = mm(d_ref[...], w_ref[...], NT)
        total = part if total is None else total + part
    for which in range(2):

        @pl.when(pl.program_id(0) == which)
        def _(which=which):
            refs[which - 2][0] = total.astype(bf16)


def grad_act_pass(core, grads, weights, chips):
    width = weights[0].shape[0]
    span = grads[0].shape[0] // (chips * CORES)
    out = jax.ShapeDtypeStruct((chips, span, width), bf16)

    def rows(which, j, c):
        return (j * CORES + jnp.where(which == 0, 1 - c[0], c[0]), 0)

    return pl.pallas_call(
        grad_act_kernel,
        grid_spec=pltpu.PrefetchScalarGridSpec(
            num_scalar_prefetch=1,
            grid=(2, chips),
            in_specs=[pl.BlockSpec((span, g.shape[1]), rows) for g in grads]
            + [pl.BlockSpec(w.shape, lambda which, j, c: (0, 0)) for w in weights],
            out_specs=[
                pl.BlockSpec(
                    (1, span, width), lambda which, j, c: (jnp.where(which == 0, j, chips - 1), 0, 0)
                ),
                pl.BlockSpec(
                    (1, span, width), lambda which, j, c: (jnp.where(which == 1, j, 0), 0, 0)
                ),
            ],
        ),
        out_shape=[out, out],
        compiler_params=PARAMS,
        cost_estimate=cost(2 * sum(g.size for g in grads) * width),
        name="grad_act_pass",
    )(core.reshape(1), *grads, *weights)


def finish_kernel(chip_ref, *refs, chips):
    found, (t_ref, gh_ref, gain_ref) = refs[:chips], refs[chips : chips + 3]
    o_ref, small_ref, grad_ref = refs[-3:]
    step = pl.program_id(0)
    place = lax.rem(chip_ref[0] - step + chips, chips)
    for n, part in enumerate(found):

        @pl.when(place == n)
        def _(part=part):
            grad_ref[...] = part[...].astype(f32)

    grad = grad_ref[...]
    normal, inverse = norm_parts(t_ref[0, 0].astype(f32))
    o_ref[0, 0] = (gh_ref[...] + norm_back(grad, normal, inverse, gain_ref[...])).astype(bf16)
    sums = jnp.concatenate(
        [
            jnp.sum(grad * normal, axis=0, keepdims=True),
            jnp.sum(grad, axis=0, keepdims=True),
        ],
        axis=0,
    )

    @pl.when(step == 0)
    def _():
        small_ref[...] = sums

    @pl.when(step > 0)
    def _():
        small_ref[...] += sums


def finish(chip, found, tokens, grad_hidden, gain, seq, whole):
    chips, _, span, width = tokens.shape
    specs, arrays, aliases = into_whole(whole, chips + 4)
    return pl.pallas_call(
        functools.partial(finish_kernel, chips=chips),
        grid_spec=pltpu.PrefetchScalarGridSpec(
            num_scalar_prefetch=1,
            grid=(chips,),
            in_specs=[pl.BlockSpec((span, width), lambda j, c: (0, 0)) for _ in found]
            + [
                pl.BlockSpec((1, 1, span, width), lambda j, c: (j, seq, 0, 0)),
                pl.BlockSpec((span, width), lambda j, c: (j, 0)),
                pl.BlockSpec((1, width), lambda j, c: (0, 0)),
            ]
            + specs,
            out_specs=[
                pl.BlockSpec((1, 1, span, width), lambda j, c: (j, seq, 0, 0)),
                pl.BlockSpec((2, width), lambda j, c: (0, 0)),
            ],
            scratch_shapes=[pltpu.VMEM((span, width), f32)],
        ),
        out_shape=[
            jax.ShapeDtypeStruct(tokens.shape, bf16),
            jax.ShapeDtypeStruct((2, width), f32),
        ],
        input_output_aliases=aliases,
        compiler_params=PARAMS,
        cost_estimate=cost(2.0e10),
        name="finish",
    )(chip.reshape(1), *found, tokens, grad_hidden, gain.reshape(1, -1), *arrays)


def norm_parts(values):
    average = jnp.mean(values, axis=-1, keepdims=True)
    centered = values - average
    variance = jnp.mean(centered * centered, axis=-1, keepdims=True)
    inverse = lax.rsqrt(variance + eps_norm)
    return centered * inverse, inverse


def norm_back(grad, normal, inverse, gain):
    inner = grad * gain
    mean_one = jnp.mean(inner, axis=-1, keepdims=True)
    mean_two = jnp.mean(inner * normal, axis=-1, keepdims=True)
    return inverse * (inner - mean_one - normal * mean_two)


def body(
    tokens,
    lengths,
    expert_ids,
    cotangent,
    query_weight,
    key_weight,
    value_weight,
    output_weight,
    gain_one,
    shift_one,
    gain_two,
    shift_two,
    expert_in,
    expert_out,
):
    seq_local, span, width = tokens.shape
    rows = seq_local * span
    n_ctx, n_exp = lax.axis_size("ctx"), lax.axis_size("exp")
    ctx = lax.axis_index("ctx")
    chips = n_ctx // CORES
    chip, core = ctx // CORES, ctx % CORES
    seqs = seq_local // chips
    full = span * n_ctx
    half = width // CORES
    experts = expert_in.shape[0]
    group = n_ctx // experts
    sub, member = ctx // group, ctx % group
    shard = expert_in.shape[1]
    all_experts = experts * n_exp
    capacity = max(2, rows * 5 // (4 * all_experts))
    devices = n_exp * n_ctx
    everyone = ("exp", "ctx")

    def ctx_send(value, target):
        return lax.ppermute(value, "ctx", [(c, target(c)) for c in range(n_ctx)])

    def other_core(value):
        return ctx_send(value, lambda c: c ^ 1)

    def to_chip(value, shift):
        return ctx_send(value, lambda c: ((c // CORES + shift) % chips) * CORES + c % CORES)

    def pick(value, index):
        return lax.dynamic_index_in_dim(value, index, 0, keepdims=False)

    def in_order(found, mine, size):
        out = []
        for place in range(size):
            chosen = found[0]
            for r in range(1, size):
                chosen = jnp.where((mine - place) % size == r, found[r], chosen)
            out.append(chosen)
        return jnp.stack(out)

    def chip_send(value):
        return [pick(value, chip)] + [
            to_chip(pick(value, (chip + r) % chips), r) for r in range(1, chips)
        ]

    def chip_join(found):
        return in_order(found, chip, chips)

    def chip_exchange(value):
        return chip_join(chip_send(value))

    def by_core(mine, other, axis=0):
        first = jnp.where(core == 0, mine, other)
        second = jnp.where(core == 0, other, mine)
        return jnp.stack([first, second], axis=axis)

    def exchange_all(value):
        return lax.all_to_all(value, everyone, split_axis=0, concat_axis=0, tiled=True)

    def by_pair(weight):
        return weight.astype(bf16).reshape(weight.shape[0], width // LANES, 1, LANES)

    exp_bits = [b for b in (2, 4, 8, 16) if b < n_exp]
    chip_bits = [b for b in (1, 2, 4, 8) if b < chips]

    def double(state, axis, bit):
        value, keys = state
        if axis == "exp":
            other = lax.ppermute(value, "exp", [(e, e ^ bit) for e in range(n_exp)])
            index, key = lax.axis_index("exp"), (0, -bit)
        else:
            other = ctx_send(value, lambda c: c ^ (bit * CORES))
            index, key = chip, (1, -bit)
        keys = sorted(keys + [key])
        at = keys.index(key)
        upper = (index & bit) != 0
        low, high = jnp.where(upper, other, value), jnp.where(upper, value, other)
        return jnp.stack([low, high], axis=at), keys

    def gather_cores(weight):
        kept = lax.dynamic_index_in_dim(weight, core, 1, keepdims=False)
        away = lax.dynamic_index_in_dim(weight, 1 - core, 1, keepdims=False)
        return by_core(kept, other_core(away)), [(2, 0)]

    def gather(state, steps):
        for axis, bit in steps:
            state = double(state, axis, bit)
        return state

    first_steps = [("exp", bit) for bit in exp_bits]
    last_steps = [("exp", 1)] + [("ctx", bit) for bit in chip_bits]

    local_qkv = jnp.concatenate(
        [by_pair(query_weight), by_pair(key_weight), by_pair(value_weight)], axis=2
    ).reshape(query_weight.shape[0], CORES, 3 * half)
    parts = 3 * half // 2

    gathered, keys = gather_cores(local_qkv)
    gathered, tokens, expert_ids, expert_out, cotangent = hold(
        (gathered, tokens, expert_ids, expert_out, cotangent)
    )

    ids_flat = expert_ids.reshape(rows)
    positions = ctx * span + jnp.arange(span)
    live = (positions[None, :] < lengths[:, None]).reshape(rows)
    onehot = ((ids_flat[:, None] == jnp.arange(all_experts)[None, :]) & live[:, None]).astype(
        jnp.int32
    )
    running = jnp.cumsum(onehot, axis=0)
    ranks = jnp.sum(onehot * (running - 1), axis=1)
    keep = live & (ranks < capacity)
    target = jnp.where(keep, ids_flat * capacity + ranks, -1)
    targets = target.reshape(chips, seqs, span)
    targets = [targets[:, s].reshape(chips * span) for s in range(seqs)]
    slots = all_experts * capacity

    inputs = tokens.astype(f32).reshape(rows, width)
    normal_one, inverse_one = norm_parts(inputs)
    act = (normal_one * gain_one + shift_one).astype(bf16).reshape(chips, seqs, span, width)
    tokens_four = tokens.reshape(chips, seqs, span, width)
    cotangent_four = cotangent.reshape(chips, seqs, span, width)
    acts = []
    for s in range(seqs):
        act_chip = chip_exchange(act[:, s])
        acts.append(by_core(act_chip, other_core(act_chip), axis=1).reshape(full, width))

    def sub_send(value, shift):
        return ctx_send(value, lambda c: ((c // group + shift) % experts) * group + c % group)

    def group_send(value, shift):
        return ctx_send(value, lambda c: (c // group) * group + (c % group + shift) % group)

    def casts(weight):
        own, *others = [pick(weight, (sub + r) % experts).astype(bf16) for r in range(experts)]
        return own, others

    def swap(others, parts):
        cut = shard // parts
        return [
            sub_send(low[n * cut : (n + 1) * cut], r)
            for r, low in enumerate(others, 1)
            for n in range(parts)
        ]

    state = gather((gathered, keys), first_steps)
    streams = [
        ((state[0][..., :parts], state[1]), last_steps),
        ((state[0][..., parts:], state[1]), last_steps[::-1]),
    ]
    streams = [(gather(part, steps[:1]), steps[1:]) for part, steps in streams]
    values = [part[0] for part, _ in streams]
    values, expert_in, expert_out, cotangent_late = hold(
        (values, expert_in, expert_out, cotangent)
    )
    grad_send = dispatch([target], [cotangent_late.reshape(rows, width)], slots)
    first_own, first_low = casts(expert_in)
    second_own, second_low = casts(expert_out)
    qkv_weights = [
        gather((value, part[1]), steps)[0].reshape(width, parts)
        for value, (part, steps) in zip(values, streams)
    ]
    out_low = output_weight.astype(bf16)
    acts, qkv_weights, grad_send, second_low, out_low = hold(
        (acts, qkv_weights, grad_send, second_low, out_low)
    )
    grad_arrived = exchange_all(grad_send)
    out_all = lax.all_gather(out_low, everyone, axis=0, tiled=True)
    second_far = swap(second_low, 4)

    lens = lax.dynamic_slice_in_dim(lengths, chip * seqs, seqs)
    halves = range(2)
    calls = 2 * seqs
    qkvs, mixed_parts, previous = [], [], None
    for s in range(seqs):
        qkvs.append([mm(acts[s], weight).astype(bf16) for weight in qkv_weights])
        for h in halves:
            call = s * 2 + h
            if call > 1:
                n = slice(call - 2, call - 1)
                qkvs[s][h], second_far[n] = hold((qkvs[s][h], second_far[n]))
            if call:
                qkvs[s][h], previous = hold((qkvs[s][h], previous))
            mixed_chip = attention_forward(lens[s : s + 1], qkvs[s][h], full)
            previous = mixed_chip
            if call == calls - 1:
                mixed_chip, grad_arrived, mixed_parts = hold(
                    (mixed_chip, grad_arrived, mixed_parts)
                )
            mixed_chip = mixed_chip.reshape(chips, CORES, span, half // 2)
            mixed_own = lax.dynamic_index_in_dim(mixed_chip, core, 1, keepdims=False)
            mixed_away = lax.dynamic_index_in_dim(mixed_chip, 1 - core, 1, keepdims=False)
            mixed_parts.append(chip_send(jnp.stack([mixed_own, other_core(mixed_away)], axis=1)))
    mixed_parts = [chip_join(found) for found in mixed_parts]

    g_parts = [grad_arrived] + [group_send(grad_arrived, r) for r in range(1, group)]

    out_weight = out_all.reshape(CORES, 2, half // 2, width)
    out_weight = jnp.stack([pick(out_weight, core), pick(out_weight, 1 - core)], axis=1)
    out_weight = out_weight.reshape(width, width)
    hiddens, sents, mixeds = zip(
        *[
            project_norm(
                mixed_parts[2 * s : 2 * s + 2], tokens_four, s, out_weight, gain_two, shift_two
            )
            for s in range(seqs)
        ]
    )
    arrived = exchange_all(dispatch(targets, sents, slots))

    sents, first_low = hold((sents, first_low))
    first_far = swap(first_low, 2)
    seconds, firsts = [[second_own], second_far], [[first_own], first_far]
    probs = []
    for h in halves:
        for s in range(seqs):
            part, _ = hold((qkvs[s][h], sents))
            probs.append(attention_probs(lens[s : s + 1], part, full))
    g_parts, probs = hold((g_parts, probs))
    activs_own = [grad_activ_pass(part, [second_own]) for part in g_parts]
    g_late, first_far[0] = hold((after(g_parts, activs_own), first_far[0]))
    activs_far = [grad_activ_pass(part, seconds[1]) for part in g_late]
    arrived, activs_own, activs_far, first_own, probs = hold(
        (arrived, activs_own, activs_far, first_own, probs)
    )
    x_parts = [arrived] + [group_send(arrived, r) for r in range(1, group)]
    owns = [hidden_pass(arrived, activs_own[0], firsts[0], f32)]
    x_parts[-1], owns = hold((x_parts[-1], owns))
    for r in range(1, group):
        owns.append(hidden_pass(x_parts[r], activs_own[r], firsts[0], f32))
    fars = [None] * group
    for r in list(range(1, group)) + [0]:
        fars[r] = hidden_pass(
            x_parts[r], activs_far[r], firsts[1], f32 if r == 0 else bf16, owns[r][2]
        )

    def sum_group(terms):
        total = terms[0]
        for r in range(1, group):
            total = total + group_send(terms[r], group - r).astype(f32)
        return total.astype(bf16)

    activ_parts = [[one[0] for one in owns], [one[0] for one in fars]]
    grad_pre_parts = [[one[1] for one in owns], [one[1] for one in fars]]
    grad_sent_rows = sum_group([one[2] for one in fars])
    grad_back = exchange_all(grad_sent_rows)
    grad_sent_rows, activ_parts, grad_pre_parts = hold(
        (grad_sent_rows, activ_parts, grad_pre_parts)
    )

    def send_grad(far, n, parts):
        return sub_send(far[n], experts - 1 - n // parts)

    def own_grads(whole, arriving, parts):
        order = [(experts - 1 - r) * parts + n for r in range(1, experts) for n in range(parts)]
        return assemble(sub, whole, [arriving[n] for n in order])

    cuts = 2
    *second_away, second_whole = expert_grad_pass(
        sub, *activ_parts, g_parts, experts, cuts
    )
    activ_parts, second_away = hold((activ_parts, second_away))
    early = (experts - 1) * cuts // 2
    second_sent = [send_grad(second_away, n, cuts) for n in range(early)]
    by_rows = list(zip(*activ_parts))
    terms = [
        group_send(down_pass(by_rows[r], seconds), group - r) for r in range(1, group)
    ]
    *first_away, first_whole = expert_grad_pass(
        sub, *grad_pre_parts, x_parts, experts, cuts
    )
    own_rows, terms, first_away = hold((by_rows[0], terms, first_away))
    result_rows = down_pass(own_rows, seconds, terms)
    grad_back, second_sent, first_away = hold((grad_back, second_sent, first_away))

    grad_hiddens, branches, grad_mixeds, small_two = zip(
        *[
            project_back(
                targets[s], grad_back, hiddens[s], cotangent_four, s, out_weight, gain_two
            )
            for s in range(seqs)
        ]
    )
    gm_chip = [chip_exchange(part) for part in grad_mixeds]

    own = width // devices
    pairs = n_exp // 2
    exp = lax.axis_index("exp")
    odd = exp % 2
    alike = [
        [e * n_ctx + c for e in range(n_exp) if e % 2 == which for c in range(n_ctx)]
        for which in range(2)
    ]
    tile = width // n_exp
    split = tile % LANES == 0

    def blocks_of(groups):
        if split:
            return split_grad_pass(groups, tile)
        terms = jnp.concatenate(
            [
                weight_grad_pass(lefts, rights).reshape(n_exp, tile, -1)[order]
                for order, lefts, rights in groups
            ],
            axis=2,
        )
        return [terms[:pairs].reshape(width // 2, -1), terms[pairs:].reshape(width // 2, -1)]

    def halve(away, kept):
        return kept, lax.ppermute(away, "exp", [(e, e ^ 1) for e in range(n_exp)])

    def joined(halved):
        total = add_terms(halved)
        return total.reshape(pairs * n_ctx, own, total.shape[1])

    def to_owner(terms):
        got = lax.all_to_all(
            terms, everyone, split_axis=0, concat_axis=0, tiled=True, axis_index_groups=alike
        )
        return got.astype(f32)

    def by_core_cols(got):
        got = jnp.sum(got.reshape(-1, CORES, own, got.shape[2]), axis=0)
        return jnp.transpose(got, (1, 0, 2))

    evens = jnp.arange(pairs, dtype=jnp.int32) * 2
    plain = jnp.concatenate([evens + 1 - odd, evens + odd])
    steps = n_exp // 4
    true_core, true_half, place = plain // (2 * steps), plain // steps % 2, plain % steps
    mixed_order = (true_half * CORES + (true_core + core) % CORES) * steps + place
    gm_chip, result_rows, second_away, first_away = hold(
        (gm_chip, result_rows, second_away, first_away)
    )
    gm_parts = [
        by_core(part[:, 0], other_core(part[:, 1]), axis=1).reshape(full, half) for part in gm_chip
    ]
    returned = exchange_all(result_rows)
    second_sent += [send_grad(second_away, n, cuts) for n in range(early, len(second_away))]

    wo_terms = halve(*blocks_of([(mixed_order, mixeds, branches)]))
    grad_qkvs = [[None, None] for s in range(seqs)]
    found_parts, w_terms, first_sent, previous = [], [], [], None
    call = 0
    for h in halves:
        for s in range(seqs):
            cols = slice(h * half // 2, (h + 1) * half // 2)
            gm_part = gm_parts[s][:, cols]
            if call == 0:
                first_sent = [send_grad(first_away, n, cuts) for n in range(len(first_away))]
            if call:
                gm_part, previous = hold((gm_part, previous))
            if call == calls - 2:
                gm_part, wo_terms = hold((gm_part, wo_terms))
            if call == calls - 1:
                gm_part, returned = hold((gm_part, returned))
            previous = attention_backward(qkvs[s][h], gm_part, probs[call])
            grad_qkvs[s][h] = previous
            call += 1
            if s == seqs - 1:
                terms = blocks_of([(plain, acts, [grad_qkvs[i][h] for i in range(seqs)])])
                previous, terms = hold((grad_qkvs[s][h], terms))
                grad_qkvs[s][h] = previous
                w_terms.append(halve(*terms))
            if h == 1:
                if call == calls - 1:
                    grad_qkvs[s][h], w_terms[0], second_sent, first_sent[0] = hold(
                        (grad_qkvs[s][h], w_terms[0], second_sent, first_sent[0])
                    )
                if call == calls:
                    grad_qkvs[s][h], found_parts, first_sent[1:] = hold(
                        (grad_qkvs[s][h], found_parts, first_sent[1:])
                    )
                away, kept = grad_act_pass(core, grad_qkvs[s], qkv_weights, chips)
                previous, kept = hold((previous, kept))
                total = (kept.astype(f32) + other_core(away).astype(f32)).astype(bf16)
                if call == calls:
                    total, w_terms[1] = hold((total, w_terms[1]))
                found_parts.append(chip_send(total))
                grad_qkvs[s][h] = previous
    returned, second_whole, first_whole = (
        after(value, previous) for value in (returned, second_whole, first_whole)
    )
    value = joined([w_terms[1]])
    columns = value.shape[2]
    first = True
    upper_bits = [b for b in (2, 4, 8, 16) if b < n_exp]
    axes = [("exp", b) for b in upper_bits[::-1]] + [("ctx", b) for b in chip_bits[::-1]]
    value = value.reshape((2,) * len(axes) + (CORES, own, columns))
    for step in axes[::-1]:
        axis, bit = step
        at = axes.index(step)
        index = exp if axis == "exp" else chip
        upper = jnp.where((index & bit) != 0, 1, 0)
        kept = lax.dynamic_index_in_dim(value, upper, at, keepdims=False)
        away = lax.dynamic_index_in_dim(value, 1 - upper, at, keepdims=False)
        if axis == "exp":
            other = lax.ppermute(away, "exp", [(e, e ^ bit) for e in range(n_exp)])
        else:
            other = ctx_send(away, lambda c: c ^ (bit * CORES))
        if first:
            other, found_parts[-1] = hold((other, found_parts[-1]))
            first = False
        value = (kept.astype(f32) + other.astype(f32)).astype(bf16)
        axes.remove(step)
    second_sum = by_core(
        pick(value, core), other_core(pick(value, 1 - core)), axis=1
    ).astype(f32)
    grad_tokens, small_one = None, []
    for s in range(seqs):
        grad_tokens, sums = finish(
            chip, found_parts[s], tokens_four, grad_hiddens[s], gain_one, s, grad_tokens
        )
        small_one.append(sums)
    small_one = sum(small_one)
    grad_tokens = grad_tokens.reshape(tokens.shape)
    grad_expert_out = own_grads(second_whole, second_sent, cuts)
    grad_expert_in = own_grads(first_whole, first_sent, cuts)
    first_sum = to_owner(joined([w_terms[0], wo_terms]))
    grad_output = jnp.sum(first_sum[:, :, parts:], axis=0)
    grad_w = jnp.concatenate([by_core_cols(first_sum[:, :, :parts]), second_sum], axis=2)
    grad_w = grad_w.reshape(own, width // LANES, 3, LANES)
    grad_query, grad_key, grad_value = (grad_w[:, :, t].reshape(own, width) for t in range(3))

    block_out = None
    for s in range(seqs):
        block_out = combine(
            targets[s], returned, hiddens[s], tokens_four.shape, s, block_out
        )
    block_out = block_out.reshape(tokens.shape)
    small_two = sum(small_two)
    small = jnp.stack(
        [
            value.reshape(devices, own)
            for value in (small_one[0], small_one[1], small_two[0], small_two[1])
        ],
        axis=1,
    )
    small = jnp.sum(exchange_all(small), axis=0)
    return (
        block_out,
        grad_tokens,
        grad_query,
        grad_key,
        grad_value,
        grad_output,
        small[0],
        small[1],
        small[2],
        small[3],
        grad_expert_in,
        grad_expert_out,
    )


def solution(mesh):
    rows = P("exp", "ctx", None)
    weight = P(("exp", "ctx"), None)
    vector = P(("exp", "ctx"))
    return jax.shard_map(
        body,
        mesh=mesh,
        in_specs=(
            rows,
            P("exp"),
            P("ctx", "exp", None, None),
            rows,
            weight,
            weight,
            weight,
            weight,
            P(),
            P(),
            P(),
            P(),
            rows,
            rows,
        ),
        out_specs=(rows, rows, weight, weight, weight, weight)
        + (vector, vector, vector, vector)
        + (rows, rows),
        check_vma=False,
    )
```

```python
import functools

import jax
import jax.numpy as jnp
from jax import lax
from jax.experimental import pallas as pl
from jax.experimental.pallas import tpu as pltpu
from jax.sharding import PartitionSpec as P

HEAD_DIM = 64
LANES = 128
PAIR = 3 * LANES
BLOCK = 256
LOG2E = 1.4426950408889634
CORES = 2

eps_norm = 1e-05
masked_score = -1e30
f32 = jnp.float32
bf16 = jnp.bfloat16
NN = (((1,), (0,)), ((), ()))
NT = (((1,), (1,)), ((), ()))
TN = (((0,), (0,)), ((), ()))
VMEM_LIMIT = 56 * 1024 * 1024
PARAMS = pltpu.CompilerParams(vmem_limit_bytes=VMEM_LIMIT)


def cost(flops):
    return pl.CostEstimate(flops=int(flops / 10), bytes_accessed=1024, transcendentals=0)


hold = lax.optimization_barrier


def after(value, *others):
    return hold((value, others))[0]


def mm(a, b, dims=NN):
    return lax.dot_general(a, b, dims, preferred_element_type=f32)


def head_operands(length, q, k):
    full = q.shape[0]
    lane = lax.broadcasted_iota(jnp.int32, (full, LANES), 1)
    pos = lax.broadcasted_iota(jnp.int32, (full, LANES), 0)
    bias = jnp.where(pos < length, 0.0, masked_score).astype(f32)
    inside, q_aug, k_aug = [], [], []
    for head in range(2):
        own = (lane // HEAD_DIM) == head
        spare = lane == HEAD_DIM * (1 - head)
        inside.append(own)
        q_aug.append(jnp.where(own, q, jnp.where(spare, 1.0, 0.0)).astype(bf16))
        k_aug.append(jnp.where(own, k, jnp.where(spare, bias, 0.0)).astype(bf16))
    return inside, q_aug, k_aug


def attention_forward_kernel(len_ref, x_ref, o_ref):
    full = x_ref.shape[0]
    q, k, v = (x_ref[:, LANES * t : LANES * (t + 1)].astype(f32) for t in range(3))
    inside, q_aug, k_aug = head_operands(len_ref[pl.program_id(0)], q, k)
    v_own = [jnp.where(own, v, 0.0).astype(bf16) for own in inside]
    to_log2 = HEAD_DIM**-0.5 * LOG2E
    row = lax.broadcasted_iota(jnp.int32, (BLOCK, BLOCK), 0)
    col = lax.broadcasted_iota(jnp.int32, (BLOCK, BLOCK), 1)
    causal = col <= row
    for i in range(full // BLOCK):
        here, before = slice(i * BLOCK, (i + 1) * BLOCK), slice(0, i * BLOCK)
        total = jnp.zeros((BLOCK, LANES), f32)
        for head in range(2):
            qi = q_aug[head][here]
            s_here = jnp.where(causal, mm(qi, k_aug[head][here], NT) * to_log2, masked_score)
            top = jnp.max(s_here, axis=1, keepdims=True)
            if i:
                s_before = mm(qi, k_aug[head][before], NT) * to_log2
                top = jnp.maximum(top, jnp.max(s_before, axis=1, keepdims=True))
            p_here = jnp.exp2(s_here - top)
            mass = jnp.sum(p_here, axis=1, keepdims=True)
            if i:
                p_before = jnp.exp2(s_before - top)
                mass = mass + jnp.sum(p_before, axis=1, keepdims=True)
            inverse = 1.0 / mass
            total = total + mm((p_here * inverse).astype(bf16), v_own[head][here])
            if i:
                total = total + mm((p_before * inverse).astype(bf16), v_own[head][before])
        o_ref[here, :] = total.astype(bf16)


def attention_forward(lens, qkv, full):
    n_seq, pairs = qkv.shape[0] // full, qkv.shape[1] // PAIR
    return pl.pallas_call(
        attention_forward_kernel,
        grid_spec=pltpu.PrefetchScalarGridSpec(
            num_scalar_prefetch=1,
            grid=(n_seq, pairs),
            in_specs=[pl.BlockSpec((full, PAIR), lambda s, p, l: (s, p))],
            out_specs=pl.BlockSpec((full, LANES), lambda s, p, l: (s, p)),
        ),
        out_shape=jax.ShapeDtypeStruct((n_seq * full, pairs * LANES), bf16),
        compiler_params=PARAMS,
        cost_estimate=cost(n_seq * pairs * 2.5e9),
        name="attention_forward",
    )(lens, qkv)


def attention_probs_kernel(len_ref, x_ref, p_ref):
    full = x_ref.shape[0]
    q, k = (x_ref[:, LANES * t : LANES * (t + 1)].astype(f32) for t in range(2))
    _, q_aug, k_aug = head_operands(len_ref[pl.program_id(0)], q, k)
    to_log2 = HEAD_DIM**-0.5 * LOG2E
    row = lax.broadcasted_iota(jnp.int32, (BLOCK, BLOCK), 0)
    col = lax.broadcasted_iota(jnp.int32, (BLOCK, BLOCK), 1)
    causal = row <= col
    for i in range(full // BLOCK):
        here, before = slice(i * BLOCK, (i + 1) * BLOCK), slice(0, i * BLOCK)
        for head in range(2):
            qi = q_aug[head][here]
            s_here = jnp.where(causal, mm(k_aug[head][here], qi, NT) * to_log2, masked_score)
            top = jnp.max(s_here, axis=0, keepdims=True)
            if i:
                s_before = mm(k_aug[head][before], qi, NT) * to_log2
                top = jnp.maximum(top, jnp.max(s_before, axis=0, keepdims=True))
            p_here = jnp.exp2(s_here - top)
            mass = jnp.sum(p_here, axis=0, keepdims=True)
            if i:
                p_before = jnp.exp2(s_before - top)
                mass = mass + jnp.sum(p_before, axis=0, keepdims=True)
            inverse = 1.0 / mass
            p_ref[head, here, here] = (p_here * inverse).astype(bf16)
            if i:
                p_ref[head, before, here] = (p_before * inverse).astype(bf16)


def attention_probs(lens, qkv, full):
    n_seq, pairs = qkv.shape[0] // full, qkv.shape[1] // PAIR
    return pl.pallas_call(
        attention_probs_kernel,
        grid_spec=pltpu.PrefetchScalarGridSpec(
            num_scalar_prefetch=1,
            grid=(n_seq, pairs),
            in_specs=[pl.BlockSpec((full, PAIR), lambda s, p, l: (s, p))],
            out_specs=pl.BlockSpec((2, full, full), lambda s, p, l: (s * pairs + p, 0, 0)),
        ),
        out_shape=jax.ShapeDtypeStruct((n_seq * pairs * 2, full, full), bf16),
        compiler_params=PARAMS,
        cost_estimate=cost(n_seq * pairs * 2.0e9),
        name="attention_probs",
    )(lens, qkv)


def attention_backward_kernel(x_ref, g_ref, p_ref, o_ref, d_scr):
    full = x_ref.shape[0]
    q, k = (x_ref[:, LANES * t : LANES * (t + 1)].astype(f32) for t in range(2))
    v = x_ref[:, 2 * LANES : 3 * LANES]
    g = g_ref[...].astype(f32)
    head_of = lax.broadcasted_iota(jnp.int32, (full, LANES), 1) // HEAD_DIM
    inside = [head_of == head for head in range(2)]
    q_own = [jnp.where(own, q, 0.0).astype(bf16) for own in inside]
    k_own = [jnp.where(own, k, 0.0).astype(bf16) for own in inside]
    g_own = [jnp.where(own, g, 0.0).astype(bf16) for own in inside]
    scale = HEAD_DIM**-0.5
    count = full // BLOCK
    for i in range(count):
        here, until = slice(i * BLOCK, (i + 1) * BLOCK), slice(0, (i + 1) * BLOCK)
        dq = jnp.zeros((BLOCK, LANES), f32)
        for head in range(2):
            probs = p_ref[head, until, here].astype(f32)
            grad = mm(v[until], g_own[head][here], NT)
            delta = jnp.sum(grad * probs, axis=0, keepdims=True)
            d_score = (probs * (grad - delta)).astype(bf16)
            d_scr[head, until, here] = d_score
            dq = dq + mm(d_score, k_own[head][until], TN)
        o_ref[here, 0:LANES] = (dq * scale).astype(bf16)
    for j in range(count):
        here, after_ = slice(j * BLOCK, (j + 1) * BLOCK), slice(j * BLOCK, full)
        dk = mm(d_scr[0, here, after_], q_own[0][after_]) + mm(
            d_scr[1, here, after_], q_own[1][after_]
        )
        dv = mm(p_ref[0, here, after_], g_own[0][after_]) + mm(
            p_ref[1, here, after_], g_own[1][after_]
        )
        o_ref[here, LANES : 2 * LANES] = (dk * scale).astype(bf16)
        o_ref[here, 2 * LANES : 3 * LANES] = dv.astype(bf16)


def attention_backward(qkv, g, probs):
    full = probs.shape[1]
    n_seq, pairs = qkv.shape[0] // full, qkv.shape[1] // PAIR
    return pl.pallas_call(
        attention_backward_kernel,
        grid=(n_seq, pairs),
        in_specs=[
            pl.BlockSpec((full, PAIR), lambda s, p: (s, p)),
            pl.BlockSpec((full, LANES), lambda s, p: (s, p)),
            pl.BlockSpec((2, full, full), lambda s, p: (s * pairs + p, 0, 0)),
        ],
        out_specs=pl.BlockSpec((full, PAIR), lambda s, p: (s, p)),
        scratch_shapes=[pltpu.VMEM((2, full, full), bf16)],
        out_shape=jax.ShapeDtypeStruct(qkv.shape, bf16),
        compiler_params=PARAMS,
        cost_estimate=cost(n_seq * pairs * 3.0e9),
        name="attention_backward",
    )(qkv, g, probs)


def tile_of(count, most=320):
    return max(t for t in range(16, most + 1, 16) if count % t == 0)


def pieces_of(shards):
    start = 0
    for ref in shards:
        size = min(512, ref.shape[0])
        for h in range(0, ref.shape[0], size):
            yield ref, slice(h, h + size), slice(start, start + size)
            start += size


def shard_specs(shards):
    return [pl.BlockSpec(w.shape, lambda i: (0, 0)) for w in shards]


def hidden_of(shards):
    return sum(w.shape[0] for w in shards)


def grad_activ_kernel(g_ref, *refs):
    for w_ref, part, cols in pieces_of(refs[:-1]):
        refs[-1][:, cols] = mm(g_ref[...], w_ref[part, :], NT).astype(bf16)


def grad_activ_pass(g, shards):
    (count, width), hidden = g.shape, hidden_of(shards)
    tile = tile_of(count)
    return pl.pallas_call(
        grad_activ_kernel,
        grid=(count // tile,),
        in_specs=[pl.BlockSpec((tile, width), lambda i: (i, 0))] + shard_specs(shards),
        out_specs=pl.BlockSpec((tile, hidden), lambda i: (i, 0)),
        out_shape=jax.ShapeDtypeStruct((count, hidden), bf16),
        compiler_params=PARAMS,
        cost_estimate=cost(count * hidden * width / 2),
        name="grad_activ_pass",
    )(g, *shards)


def hidden_kernel(x_ref, ga_ref, *refs, before):
    shards, (a_ref, gp_ref, gs_ref) = refs[before:-3], refs[-3:]
    for w_ref, part, cols in pieces_of(shards):
        activ, slope = gelu_parts(mm(x_ref[...], w_ref[part, :], NT))
        a_ref[:, cols] = activ.astype(bf16)
        gp_ref[:, cols] = (ga_ref[:, cols].astype(f32) * slope).astype(bf16)
    total = product_of(gp_ref, shards)
    if before:
        total = total + refs[0][...]
    gs_ref[...] = total.astype(gs_ref.dtype)


def product_of(rows_ref, shards):
    total, start = None, 0
    for w_ref in shards:
        cols = slice(start, start + w_ref.shape[0])
        part = mm(rows_ref[:, cols], w_ref[...])
        total = part if total is None else total + part
        start += w_ref.shape[0]
    return total


def hidden_pass(x, grad_activ, shards, dtype, before=None):
    (count, width), hidden = x.shape, hidden_of(shards)
    tile = tile_of(count)
    wide = pl.BlockSpec((tile, hidden), lambda i: (i, 0))
    thin = pl.BlockSpec((tile, width), lambda i: (i, 0))
    more = [] if before is None else [before]
    return pl.pallas_call(
        functools.partial(hidden_kernel, before=len(more)),
        grid=(count // tile,),
        in_specs=[thin, wide] + [thin] * len(more) + shard_specs(shards),
        out_specs=[wide, wide, thin],
        out_shape=[jax.ShapeDtypeStruct((count, hidden), bf16)] * 2
        + [jax.ShapeDtypeStruct((count, width), dtype)],
        compiler_params=PARAMS,
        cost_estimate=cost(2 * count * hidden * width),
        name="hidden_pass",
    )(x, grad_activ, *more, *shards)


def down_kernel(*refs, own, more):
    last = len(refs) - 1 - more
    total = product_of(refs[0], refs[2 : 2 + own]) + product_of(refs[1], refs[2 + own : last])
    for term in refs[last:-1]:
        total = total + term[...].astype(f32)
    refs[-1][...] = total.astype(bf16)


def down_pass(activs, groups, terms=()):
    count, width = activs[0].shape[0], groups[0][0].shape[1]
    tile = tile_of(count)
    shards = list(groups[0]) + list(groups[1])
    return pl.pallas_call(
        functools.partial(down_kernel, own=len(groups[0]), more=len(terms)),
        grid=(count // tile,),
        in_specs=[pl.BlockSpec((tile, a.shape[1]), lambda i: (i, 0)) for a in activs]
        + shard_specs(shards)
        + [pl.BlockSpec((tile, width), lambda i: (i, 0)) for _ in terms],
        out_specs=pl.BlockSpec((tile, width), lambda i: (i, 0)),
        out_shape=jax.ShapeDtypeStruct((count, width), bf16),
        compiler_params=PARAMS,
        cost_estimate=cost(2 * count * hidden_of(shards) * width),
        name="down_pass",
    )(*activs, *shards, *terms)


def summed(lefts, rights):
    total = mm(lefts[0][...], rights[0][...], TN)
    for left, right in zip(lefts[1:], rights[1:]):
        total = total + mm(left[...], right[...], TN)
    return total


def weight_grad_kernel(*refs):
    count = len(refs) // 2
    refs[-1][...] = summed(refs[:count], refs[count:-1]).astype(bf16)


def weight_grad_pass(lefts, rights):
    hidden, width = lefts[0].shape[1], rights[0].shape[1]
    tile = min(256, hidden)
    return pl.pallas_call(
        weight_grad_kernel,
        grid=(hidden // tile,),
        in_specs=[pl.BlockSpec((v.shape[0], tile), lambda i: (0, i)) for v in lefts]
        + [pl.BlockSpec(v.shape, lambda i: (0, 0)) for v in rights],
        out_specs=pl.BlockSpec((tile, width), lambda i: (i, 0)),
        out_shape=jax.ShapeDtypeStruct((hidden, width), bf16),
        compiler_params=PARAMS,
        cost_estimate=cost(2 * lefts[0].size * width * len(lefts)),
        name="weight_grad_pass",
    )(*lefts, *rights)


def split_grad_kernel(order_ref, *refs, tile, counts):
    values, start, col = refs[:-2], 0, 0
    steps = order_ref.shape[0] // len(counts)
    totals = []
    for group, count in enumerate(counts):
        lefts, rights = values[start : start + count], values[start + count : start + 2 * count]
        first = group * steps + pl.program_id(0) * (steps // 2)
        places = [order_ref[first + n] for n in range(steps // 2)]
        total = None
        for left, right in zip(lefts, rights):
            chosen = jnp.concatenate(
                [left[:, pl.ds(pl.multiple_of(place * tile, tile), tile)] for place in places],
                axis=1,
            )
            part = mm(chosen, right[...], TN)
            total = part if total is None else total + part
        totals.append((slice(col, col + total.shape[1]), total.astype(bf16)))
        start += 2 * count
        col += total.shape[1]

    for which in range(2):

        @pl.when(pl.program_id(0) == which)
        def _(which=which):
            for cols, total in totals:
                refs[which - 2][:, cols] = total


def split_grad_pass(groups, tile):
    hidden = groups[0][1][0].shape[1]
    width = sum(rights[0].shape[1] for _, _, rights in groups)
    values = [v for _, lefts, rights in groups for v in (*lefts, *rights)]
    out = jax.ShapeDtypeStruct((hidden // 2, width), bf16)
    return pl.pallas_call(
        functools.partial(split_grad_kernel, tile=tile, counts=[len(g[1]) for g in groups]),
        grid_spec=pltpu.PrefetchScalarGridSpec(
            num_scalar_prefetch=1,
            grid=(2,),
            in_specs=[pl.BlockSpec(v.shape, lambda i, o: (0, 0)) for v in values],
            out_specs=[pl.BlockSpec(out.shape, lambda i, o: (0, 0))] * 2,
        ),
        out_shape=[out, out],
        compiler_params=PARAMS,
        cost_estimate=cost(2 * width * sum(v.size for v in groups[0][1])),
        name="split_grad_pass",
    )(jnp.concatenate([order for order, _, _ in groups]), *values)


def add_terms_kernel(*refs):
    col = 0
    for one, two in zip(refs[0:-1:2], refs[1:-1:2]):
        cols = slice(col, col + one.shape[1])
        refs[-1][:, cols] = (one[...].astype(f32) + two[...].astype(f32)).astype(bf16)
        col = cols.stop


def add_terms(pairs):
    count = pairs[0][0].shape[0]
    tile = min(128, count)
    values = [v for pair in pairs for v in pair]
    width = sum(pair[0].shape[1] for pair in pairs)
    return pl.pallas_call(
        add_terms_kernel,
        grid=(count // tile,),
        in_specs=[pl.BlockSpec((tile, v.shape[1]), lambda i: (i, 0)) for v in values],
        out_specs=pl.BlockSpec((tile, width), lambda i: (i, 0)),
        out_shape=jax.ShapeDtypeStruct((count, width), bf16),
        compiler_params=PARAMS,
        cost_estimate=cost(3.0e10),
        name="add_terms",
    )(*values)


def expert_grad_kernel(sub_ref, *refs, count, pieces, per):
    step = pl.program_id(0)
    rights = refs[2 * count : 3 * count]

    @pl.when(step < pieces * per)
    def _():
        total = summed(refs[count : 2 * count], rights).astype(bf16)
        for n in range(pieces):

            @pl.when((step >= n * per) & (step < (n + 1) * per))
            def _(n=n):
                refs[3 * count + n][...] = total

    @pl.when(step >= pieces * per)
    def _():
        refs[-1][0] = summed(refs[:count], rights)


def expert_grad_pass(sub, owns, others, rights, experts, parts):
    shard, width = owns[0].shape[1], rights[0].shape[1]
    tile = min(256, shard // parts)
    pieces, per, own = (experts - 1) * parts, shard // parts // tile, shard // tile
    far = pieces * per

    def piece_spec(n):
        return pl.BlockSpec((tile, width), lambda i, s: (jnp.clip(i - n * per, 0, per - 1), 0))

    return pl.pallas_call(
        functools.partial(expert_grad_kernel, count=len(owns), pieces=pieces, per=per),
        grid_spec=pltpu.PrefetchScalarGridSpec(
            num_scalar_prefetch=1,
            grid=(far + own,),
            in_specs=[
                pl.BlockSpec((v.shape[0], tile), lambda i, s: (0, jnp.clip(i - far, 0, own - 1)))
                for v in owns
            ]
            + [
                pl.BlockSpec((v.shape[0], tile), lambda i, s: (0, jnp.clip(i, 0, far - 1)))
                for v in others
            ]
            + [pl.BlockSpec(v.shape, lambda i, s: (0, 0)) for v in rights],
            out_specs=[piece_spec(n) for n in range(pieces)]
            + [
                pl.BlockSpec(
                    (1, tile, width), lambda i, s: (s[0], jnp.clip(i - far, 0, own - 1), 0)
                )
            ],
        ),
        out_shape=[jax.ShapeDtypeStruct((shard // parts, width), bf16)] * pieces
        + [jax.ShapeDtypeStruct((experts, shard, width), f32)],
        compiler_params=PARAMS,
        cost_estimate=cost(2 * experts * owns[0].size * width * len(owns)),
        name="expert_grad_pass",
    )(sub.reshape(1), *owns, *others, *rights)


def assemble_kernel(sub_ref, whole_ref, *refs):
    pieces, o_ref = refs[:-1], refs[-1]
    for n, piece in enumerate(pieces):

        @pl.when(pl.program_id(0) * pl.num_programs(1) + pl.program_id(1) == n)
        def _(piece=piece):
            o_ref[0] = piece[...].astype(f32)


def assemble(sub, whole, pieces):
    experts = whole.shape[0]
    parts = len(pieces) // (experts - 1)
    cut, width = pieces[0].shape

    def place(r, n, s):
        return (lax.rem(s[0] - r - 1 + experts, experts), n, 0)

    return pl.pallas_call(
        assemble_kernel,
        grid_spec=pltpu.PrefetchScalarGridSpec(
            num_scalar_prefetch=1,
            grid=(experts - 1, parts),
            in_specs=[pl.BlockSpec(memory_space=pl.ANY)]
            + [pl.BlockSpec((cut, width), lambda r, n, s: (0, 0)) for _ in pieces],
            out_specs=pl.BlockSpec((1, cut, width), place),
        ),
        out_shape=jax.ShapeDtypeStruct(whole.shape, f32),
        input_output_aliases={1: 0},
        compiler_params=PARAMS,
        cost_estimate=cost(3.0e10),
        name="assemble",
    )(sub.reshape(1), whole, *pieces)


def gelu_parts(pre):
    outer, inner = 0.7978845608028654, 0.044715
    square = pre * pre
    half = 0.5 + 0.5 * jnp.tanh(pre * (outer + outer * inner * square))
    value = pre * half
    slope = half + value * (1.0 - half) * (2.0 * outer + 6.0 * outer * inner * square)
    return value, slope


def dispatch_kernel(*refs):
    o_ref, count = refs[-1], len(refs) // 2
    tile = o_ref.shape[0]
    total = None
    for t_ref, v_ref in zip(refs[:count], refs[count:-1]):
        rows = v_ref.shape[0]
        slot = lax.broadcasted_iota(jnp.int32, (tile, rows), 0) + pl.program_id(0) * tile
        chosen = jnp.where(t_ref[...] == slot, 1.0, 0.0).astype(bf16)
        part = mm(chosen, v_ref[...])
        total = part if total is None else total + part
    o_ref[...] = total.astype(bf16)


def dispatch(targets, values, slots):
    tile, width = tile_of(slots), values[0].shape[1]
    return pl.pallas_call(
        dispatch_kernel,
        grid=(slots // tile,),
        in_specs=[pl.BlockSpec((1, v.shape[0]), lambda i: (0, 0)) for v in values]
        + [pl.BlockSpec(v.shape, lambda i: (0, 0)) for v in values],
        out_specs=pl.BlockSpec((tile, width), lambda i: (i, 0)),
        out_shape=jax.ShapeDtypeStruct((slots, width), bf16),
        compiler_params=PARAMS,
        cost_estimate=cost(2 * slots * width * sum(v.shape[0] for v in values)),
        name="dispatch",
    )(*[t.reshape(1, -1) for t in targets], *values)


def returned_rows(target, rows_ref):
    slots = rows_ref.shape[0]
    slot = lax.broadcasted_iota(jnp.int32, (target.shape[0], slots), 1)
    return mm(jnp.where(target == slot, 1.0, 0.0).astype(bf16), rows_ref[...])


def combine_kernel(t_ref, rows_ref, h_ref, *refs):
    refs[-1][0, 0] = (h_ref[...] + returned_rows(t_ref[...], rows_ref)).astype(bf16)


def into_whole(whole, place):
    if whole is None:
        return [], [], {}
    return [pl.BlockSpec(memory_space=pl.ANY)], [whole], {place: 0}


def combine(target, rows, hidden, shape, seq, whole):
    chips, _, span, width = shape
    specs, arrays, aliases = into_whole(whole, 3)
    return pl.pallas_call(
        combine_kernel,
        grid=(chips,),
        in_specs=[
            pl.BlockSpec((span, 1), lambda j: (j, 0)),
            pl.BlockSpec(rows.shape, lambda j: (0, 0)),
            pl.BlockSpec((span, width), lambda j: (j, 0)),
        ]
        + specs,
        out_specs=pl.BlockSpec((1, 1, span, width), lambda j: (j, seq, 0, 0)),
        out_shape=jax.ShapeDtypeStruct(shape, bf16),
        input_output_aliases=aliases,
        compiler_params=PARAMS,
        cost_estimate=cost(20 * chips * span * width * rows.shape[0]),
        name="combine",
    )(target.reshape(-1, 1), rows, hidden, *arrays)


def project_kernel(a_ref, b_ref, t_ref, w_ref, gain_ref, shift_ref, h_ref, s_ref, m_ref):
    mixed = jnp.concatenate([a_ref[0, 0], a_ref[0, 1], b_ref[0, 0], b_ref[0, 1]], axis=1)
    m_ref[...] = mixed
    hidden = t_ref[0, 0].astype(f32) + mm(mixed, w_ref[...])
    h_ref[...] = hidden
    normal, _ = norm_parts(hidden)
    s_ref[...] = (normal * gain_ref[...] + shift_ref[...]).astype(bf16)


def project_norm(parts, tokens, seq, weight, gain, shift):
    chips, cores, span, cols = parts[0].shape
    width = tokens.shape[3]
    block = pl.BlockSpec((1, cores, span, cols), lambda j: (j, 0, 0, 0))
    row = pl.BlockSpec((1, width), lambda j: (0, 0))
    out = pl.BlockSpec((span, width), lambda j: (j, 0))
    return pl.pallas_call(
        project_kernel,
        grid=(chips,),
        in_specs=[
            block,
            block,
            pl.BlockSpec((1, 1, span, width), lambda j: (j, seq, 0, 0)),
            pl.BlockSpec((width, width), lambda j: (0, 0)),
            row,
            row,
        ],
        out_specs=[out] * 3,
        out_shape=[
            jax.ShapeDtypeStruct((chips * span, width), dtype) for dtype in (f32, bf16, bf16)
        ],
        compiler_params=PARAMS,
        cost_estimate=cost(2 * chips * span * width * width),
        name="project_norm",
    )(*parts, tokens, weight, gain.reshape(1, -1), shift.reshape(1, -1))


def project_back_kernel(
    t_ref, rows_ref, h_ref, c_ref, w_ref, gain_ref, gh_ref, gb_ref, gm_ref, small_ref
):
    grad = returned_rows(t_ref[...], rows_ref)
    normal, inverse = norm_parts(h_ref[...])
    grad_hidden = c_ref[0, 0].astype(f32) + norm_back(grad, normal, inverse, gain_ref[...])
    gh_ref[...] = grad_hidden
    branch = grad_hidden.astype(bf16)
    gb_ref[...] = branch
    mixed = mm(branch, w_ref[...], NT).astype(bf16)
    cols = gm_ref.shape[3] // 2
    for half in range(2):
        for k in range(CORES):
            at = (half * CORES + k) * cols
            gm_ref[0, k, :, half * cols : (half + 1) * cols] = mixed[:, at : at + cols]
    sums = jnp.concatenate(
        [
            jnp.sum(grad * normal, axis=0, keepdims=True),
            jnp.sum(grad, axis=0, keepdims=True),
        ],
        axis=0,
    )

    @pl.when(pl.program_id(0) == 0)
    def _():
        small_ref[...] = sums

    @pl.when(pl.program_id(0) > 0)
    def _():
        small_ref[...] += sums


def project_back(target, rows, hidden, cotangent, seq, weight, gain):
    chips, _, span, width = cotangent.shape
    out = pl.BlockSpec((span, width), lambda j: (j, 0))
    return pl.pallas_call(
        project_back_kernel,
        grid=(chips,),
        in_specs=[
            pl.BlockSpec((span, 1), lambda j: (j, 0)),
            pl.BlockSpec(rows.shape, lambda j: (0, 0)),
            out,
            pl.BlockSpec((1, 1, span, width), lambda j: (j, seq, 0, 0)),
            pl.BlockSpec((width, width), lambda j: (0, 0)),
            pl.BlockSpec((1, width), lambda j: (0, 0)),
        ],
        out_specs=[
            out,
            out,
            pl.BlockSpec((1, CORES, span, width // CORES), lambda j: (j, 0, 0, 0)),
            pl.BlockSpec((2, width), lambda j: (0, 0)),
        ],
        out_shape=[
            jax.ShapeDtypeStruct((chips * span, width), f32),
            jax.ShapeDtypeStruct((chips * span, width), bf16),
            jax.ShapeDtypeStruct((chips, CORES, span, width // CORES), bf16),
            jax.ShapeDtypeStruct((2, width), f32),
        ],
        compiler_params=PARAMS,
        cost_estimate=cost(6 * chips * span * width * width),
        name="project_back",
    )(target.reshape(-1, 1), rows, hidden, cotangent, weight, gain.reshape(1, -1))


def grad_act_kernel(core_ref, *refs):
    count = (len(refs) - 2) // 2
    total = None
    for d_ref, w_ref in zip(refs[:count], refs[count:-2]):
        part = mm(d_ref[...], w_ref[...], NT)
        total = part if total is None else total + part
    for which in range(2):

        @pl.when(pl.program_id(0) == which)
        def _(which=which):
            refs[which - 2][0] = total.astype(bf16)


def grad_act_pass(core, grads, weights, chips):
    width = weights[0].shape[0]
    span = grads[0].shape[0] // (chips * CORES)
    out = jax.ShapeDtypeStruct((chips, span, width), bf16)

    def rows(which, j, c):
        return (j * CORES + jnp.where(which == 0, 1 - c[0], c[0]), 0)

    return pl.pallas_call(
        grad_act_kernel,
        grid_spec=pltpu.PrefetchScalarGridSpec(
            num_scalar_prefetch=1,
            grid=(2, chips),
            in_specs=[pl.BlockSpec((span, g.shape[1]), rows) for g in grads]
            + [pl.BlockSpec(w.shape, lambda which, j, c: (0, 0)) for w in weights],
            out_specs=[
                pl.BlockSpec(
                    (1, span, width), lambda which, j, c: (jnp.where(which == 0, j, chips - 1), 0, 0)
                ),
                pl.BlockSpec(
                    (1, span, width), lambda which, j, c: (jnp.where(which == 1, j, 0), 0, 0)
                ),
            ],
        ),
        out_shape=[out, out],
        compiler_params=PARAMS,
        cost_estimate=cost(2 * sum(g.size for g in grads) * width),
        name="grad_act_pass",
    )(core.reshape(1), *grads, *weights)


def finish_kernel(chip_ref, *refs, chips):
    found, (t_ref, gh_ref, gain_ref) = refs[:chips], refs[chips : chips + 3]
    o_ref, small_ref, grad_ref = refs[-3:]
    step = pl.program_id(0)
    place = lax.rem(chip_ref[0] - step + chips, chips)
    for n, part in enumerate(found):

        @pl.when(place == n)
        def _(part=part):
            grad_ref[...] = part[...].astype(f32)

    grad = grad_ref[...]
    normal, inverse = norm_parts(t_ref[0, 0].astype(f32))
    o_ref[0, 0] = (gh_ref[...] + norm_back(grad, normal, inverse, gain_ref[...])).astype(bf16)
    sums = jnp.concatenate(
        [
            jnp.sum(grad * normal, axis=0, keepdims=True),
            jnp.sum(grad, axis=0, keepdims=True),
        ],
        axis=0,
    )

    @pl.when(step == 0)
    def _():
        small_ref[...] = sums

    @pl.when(step > 0)
    def _():
        small_ref[...] += sums


def finish(chip, found, tokens, grad_hidden, gain, seq, whole):
    chips, _, span, width = tokens.shape
    specs, arrays, aliases = into_whole(whole, chips + 4)
    return pl.pallas_call(
        functools.partial(finish_kernel, chips=chips),
        grid_spec=pltpu.PrefetchScalarGridSpec(
            num_scalar_prefetch=1,
            grid=(chips,),
            in_specs=[pl.BlockSpec((span, width), lambda j, c: (0, 0)) for _ in found]
            + [
                pl.BlockSpec((1, 1, span, width), lambda j, c: (j, seq, 0, 0)),
                pl.BlockSpec((span, width), lambda j, c: (j, 0)),
                pl.BlockSpec((1, width), lambda j, c: (0, 0)),
            ]
            + specs,
            out_specs=[
                pl.BlockSpec((1, 1, span, width), lambda j, c: (j, seq, 0, 0)),
                pl.BlockSpec((2, width), lambda j, c: (0, 0)),
            ],
            scratch_shapes=[pltpu.VMEM((span, width), f32)],
        ),
        out_shape=[
            jax.ShapeDtypeStruct(tokens.shape, bf16),
            jax.ShapeDtypeStruct((2, width), f32),
        ],
        input_output_aliases=aliases,
        compiler_params=PARAMS,
        cost_estimate=cost(2.0e10),
        name="finish",
    )(chip.reshape(1), *found, tokens, grad_hidden, gain.reshape(1, -1), *arrays)


def norm_parts(values):
    average = jnp.mean(values, axis=-1, keepdims=True)
    centered = values - average
    variance = jnp.mean(centered * centered, axis=-1, keepdims=True)
    inverse = lax.rsqrt(variance + eps_norm)
    return centered * inverse, inverse


def norm_back(grad, normal, inverse, gain):
    inner = grad * gain
    mean_one = jnp.mean(inner, axis=-1, keepdims=True)
    mean_two = jnp.mean(inner * normal, axis=-1, keepdims=True)
    return inverse * (inner - mean_one - normal * mean_two)


def body(
    tokens,
    lengths,
    expert_ids,
    cotangent,
    query_weight,
    key_weight,
    value_weight,
    output_weight,
    gain_one,
    shift_one,
    gain_two,
    shift_two,
    expert_in,
    expert_out,
):
    seq_local, span, width = tokens.shape
    rows = seq_local * span
    n_ctx, n_exp = lax.axis_size("ctx"), lax.axis_size("exp")
    ctx = lax.axis_index("ctx")
    chips = n_ctx // CORES
    chip, core = ctx // CORES, ctx % CORES
    seqs = seq_local // chips
    full = span * n_ctx
    half = width // CORES
    experts = expert_in.shape[0]
    group = n_ctx // experts
    sub, member = ctx // group, ctx % group
    shard = expert_in.shape[1]
    all_experts = experts * n_exp
    capacity = max(2, rows * 5 // (4 * all_experts))
    devices = n_exp * n_ctx
    everyone = ("exp", "ctx")

    def ctx_send(value, target):
        return lax.ppermute(value, "ctx", [(c, target(c)) for c in range(n_ctx)])

    def other_core(value):
        return ctx_send(value, lambda c: c ^ 1)

    def to_chip(value, shift):
        return ctx_send(value, lambda c: ((c // CORES + shift) % chips) * CORES + c % CORES)

    def pick(value, index):
        return lax.dynamic_index_in_dim(value, index, 0, keepdims=False)

    def in_order(found, mine, size):
        out = []
        for place in range(size):
            chosen = found[0]
            for r in range(1, size):
                chosen = jnp.where((mine - place) % size == r, found[r], chosen)
            out.append(chosen)
        return jnp.stack(out)

    def chip_send(value):
        return [pick(value, chip)] + [
            to_chip(pick(value, (chip + r) % chips), r) for r in range(1, chips)
        ]

    def chip_join(found):
        return in_order(found, chip, chips)

    def chip_exchange(value):
        return chip_join(chip_send(value))

    def by_core(mine, other, axis=0):
        first = jnp.where(core == 0, mine, other)
        second = jnp.where(core == 0, other, mine)
        return jnp.stack([first, second], axis=axis)

    def exchange_all(value):
        return lax.all_to_all(value, everyone, split_axis=0, concat_axis=0, tiled=True)

    def by_pair(weight):
        return weight.astype(bf16).reshape(weight.shape[0], width // LANES, 1, LANES)

    exp_bits = [b for b in (2, 4, 8, 16) if b < n_exp]
    chip_bits = [b for b in (1, 2, 4, 8) if b < chips]

    def double(state, axis, bit):
        value, keys = state
        if axis == "exp":
            other = lax.ppermute(value, "exp", [(e, e ^ bit) for e in range(n_exp)])
            index, key = lax.axis_index("exp"), (0, -bit)
        else:
            other = ctx_send(value, lambda c: c ^ (bit * CORES))
            index, key = chip, (1, -bit)
        keys = sorted(keys + [key])
        at = keys.index(key)
        upper = (index & bit) != 0
        low, high = jnp.where(upper, other, value), jnp.where(upper, value, other)
        return jnp.stack([low, high], axis=at), keys

    def gather_cores(weight):
        kept = lax.dynamic_index_in_dim(weight, core, 1, keepdims=False)
        away = lax.dynamic_index_in_dim(weight, 1 - core, 1, keepdims=False)
        return by_core(kept, other_core(away)), [(2, 0)]

    def gather(state, steps):
        for axis, bit in steps:
            state = double(state, axis, bit)
        return state

    first_steps = [("exp", bit) for bit in exp_bits]
    last_steps = [("exp", 1)] + [("ctx", bit) for bit in chip_bits]

    local_qkv = jnp.concatenate(
        [by_pair(query_weight), by_pair(key_weight), by_pair(value_weight)], axis=2
    ).reshape(query_weight.shape[0], CORES, 3 * half)
    parts = 3 * half // 2

    gathered, keys = gather_cores(local_qkv)
    gathered, tokens, expert_ids, expert_out, cotangent = hold(
        (gathered, tokens, expert_ids, expert_out, cotangent)
    )

    ids_flat = expert_ids.reshape(rows)
    positions = ctx * span + jnp.arange(span)
    live = (positions[None, :] < lengths[:, None]).reshape(rows)
    onehot = ((ids_flat[:, None] == jnp.arange(all_experts)[None, :]) & live[:, None]).astype(
        jnp.int32
    )
    running = jnp.cumsum(onehot, axis=0)
    ranks = jnp.sum(onehot * (running - 1), axis=1)
    keep = live & (ranks < capacity)
    target = jnp.where(keep, ids_flat * capacity + ranks, -1)
    targets = target.reshape(chips, seqs, span)
    targets = [targets[:, s].reshape(chips * span) for s in range(seqs)]
    slots = all_experts * capacity

    inputs = tokens.astype(f32).reshape(rows, width)
    normal_one, inverse_one = norm_parts(inputs)
    act = (normal_one * gain_one + shift_one).astype(bf16).reshape(chips, seqs, span, width)
    tokens_four = tokens.reshape(chips, seqs, span, width)
    cotangent_four = cotangent.reshape(chips, seqs, span, width)
    acts = []
    for s in range(seqs):
        act_chip = chip_exchange(act[:, s])
        acts.append(by_core(act_chip, other_core(act_chip), axis=1).reshape(full, width))

    def sub_send(value, shift):
        return ctx_send(value, lambda c: ((c // group + shift) % experts) * group + c % group)

    def group_send(value, shift):
        return ctx_send(value, lambda c: (c // group) * group + (c % group + shift) % group)

    def casts(weight):
        own, *others = [pick(weight, (sub + r) % experts).astype(bf16) for r in range(experts)]
        return own, others

    def swap(others, parts):
        cut = shard // parts
        return [
            sub_send(low[n * cut : (n + 1) * cut], r)
            for r, low in enumerate(others, 1)
            for n in range(parts)
        ]

    state = gather((gathered, keys), first_steps)
    streams = [
        ((state[0][..., :parts], state[1]), last_steps),
        ((state[0][..., parts:], state[1]), last_steps[::-1]),
    ]
    streams = [(gather(part, steps[:1]), steps[1:]) for part, steps in streams]
    values = [part[0] for part, _ in streams]
    values, expert_in, expert_out, cotangent_late = hold(
        (values, expert_in, expert_out, cotangent)
    )
    grad_send = dispatch([target], [cotangent_late.reshape(rows, width)], slots)
    first_own, first_low = casts(expert_in)
    second_own, second_low = casts(expert_out)
    qkv_weights = [
        gather((value, part[1]), steps)[0].reshape(width, parts)
        for value, (part, steps) in zip(values, streams)
    ]
    out_low = output_weight.astype(bf16)
    acts, qkv_weights, grad_send, second_low, out_low = hold(
        (acts, qkv_weights, grad_send, second_low, out_low)
    )
    grad_arrived = exchange_all(grad_send)
    out_all = lax.all_gather(out_low, everyone, axis=0, tiled=True)
    second_far = swap(second_low, 4)

    lens = lax.dynamic_slice_in_dim(lengths, chip * seqs, seqs)
    halves = range(2)
    calls = 2 * seqs
    qkvs, mixed_parts, previous = [], [], None
    for s in range(seqs):
        qkvs.append([mm(acts[s], weight).astype(bf16) for weight in qkv_weights])
        for h in halves:
            call = s * 2 + h
            if call > 1:
                n = slice(call - 2, call - 1)
                qkvs[s][h], second_far[n] = hold((qkvs[s][h], second_far[n]))
            if call:
                qkvs[s][h], previous = hold((qkvs[s][h], previous))
            mixed_chip = attention_forward(lens[s : s + 1], qkvs[s][h], full)
            previous = mixed_chip
            if call == calls - 1:
                mixed_chip, grad_arrived, mixed_parts = hold(
                    (mixed_chip, grad_arrived, mixed_parts)
                )
            mixed_chip = mixed_chip.reshape(chips, CORES, span, half // 2)
            mixed_own = lax.dynamic_index_in_dim(mixed_chip, core, 1, keepdims=False)
            mixed_away = lax.dynamic_index_in_dim(mixed_chip, 1 - core, 1, keepdims=False)
            mixed_parts.append(chip_send(jnp.stack([mixed_own, other_core(mixed_away)], axis=1)))
    mixed_parts = [chip_join(found) for found in mixed_parts]

    g_parts = [grad_arrived] + [group_send(grad_arrived, r) for r in range(1, group)]

    out_weight = out_all.reshape(CORES, 2, half // 2, width)
    out_weight = jnp.stack([pick(out_weight, core), pick(out_weight, 1 - core)], axis=1)
    out_weight = out_weight.reshape(width, width)
    hiddens, sents, mixeds = zip(
        *[
            project_norm(
                mixed_parts[2 * s : 2 * s + 2], tokens_four, s, out_weight, gain_two, shift_two
            )
            for s in range(seqs)
        ]
    )
    arrived = exchange_all(dispatch(targets, sents, slots))

    sents, first_low = hold((sents, first_low))
    first_far = swap(first_low, 2)
    seconds, firsts = [[second_own], second_far], [[first_own], first_far]
    probs = []
    for h in halves:
        for s in range(seqs):
            part, _ = hold((qkvs[s][h], sents))
            probs.append(attention_probs(lens[s : s + 1], part, full))
    g_parts, probs = hold((g_parts, probs))
    activs_own = [grad_activ_pass(part, [second_own]) for part in g_parts]
    g_late, first_far[0] = hold((after(g_parts, activs_own), first_far[0]))
    activs_far = [grad_activ_pass(part, seconds[1]) for part in g_late]
    arrived, activs_own, activs_far, first_own, probs = hold(
        (arrived, activs_own, activs_far, first_own, probs)
    )
    x_parts = [arrived] + [group_send(arrived, r) for r in range(1, group)]
    owns = [hidden_pass(arrived, activs_own[0], firsts[0], f32)]
    x_parts[-1], owns = hold((x_parts[-1], owns))
    for r in range(1, group):
        owns.append(hidden_pass(x_parts[r], activs_own[r], firsts[0], f32))
    fars = [None] * group
    for r in list(range(1, group)) + [0]:
        fars[r] = hidden_pass(
            x_parts[r], activs_far[r], firsts[1], f32 if r == 0 else bf16, owns[r][2]
        )

    def sum_group(terms):
        total = terms[0]
        for r in range(1, group):
            total = total + group_send(terms[r], group - r).astype(f32)
        return total.astype(bf16)

    activ_parts = [[one[0] for one in owns], [one[0] for one in fars]]
    grad_pre_parts = [[one[1] for one in owns], [one[1] for one in fars]]
    grad_sent_rows = sum_group([one[2] for one in fars])
    grad_back = exchange_all(grad_sent_rows)
    grad_sent_rows, activ_parts, grad_pre_parts = hold(
        (grad_sent_rows, activ_parts, grad_pre_parts)
    )

    def send_grad(far, n, parts):
        return sub_send(far[n], experts - 1 - n // parts)

    def own_grads(whole, arriving, parts):
        order = [(experts - 1 - r) * parts + n for r in range(1, experts) for n in range(parts)]
        return assemble(sub, whole, [arriving[n] for n in order])

    cuts = 2
    *second_away, second_whole = expert_grad_pass(
        sub, *activ_parts, g_parts, experts, cuts
    )
    activ_parts, second_away = hold((activ_parts, second_away))
    early = (experts - 1) * cuts // 2
    second_sent = [send_grad(second_away, n, cuts) for n in range(early)]
    by_rows = list(zip(*activ_parts))
    terms = [
        group_send(down_pass(by_rows[r], seconds), group - r) for r in range(1, group)
    ]
    *first_away, first_whole = expert_grad_pass(
        sub, *grad_pre_parts, x_parts, experts, cuts
    )
    own_rows, terms, first_away = hold((by_rows[0], terms, first_away))
    result_rows = down_pass(own_rows, seconds, terms)
    grad_back, second_sent, first_away = hold((grad_back, second_sent, first_away))

    grad_hiddens, branches, grad_mixeds, small_two = zip(
        *[
            project_back(
                targets[s], grad_back, hiddens[s], cotangent_four, s, out_weight, gain_two
            )
            for s in range(seqs)
        ]
    )
    gm_chip = [chip_exchange(part) for part in grad_mixeds]

    own = width // devices
    pairs = n_exp // 2
    exp = lax.axis_index("exp")
    odd = exp % 2
    alike = [
        [e * n_ctx + c for e in range(n_exp) if e % 2 == which for c in range(n_ctx)]
        for which in range(2)
    ]
    tile = width // n_exp
    split = tile % LANES == 0

    def blocks_of(groups):
        if split:
            return split_grad_pass(groups, tile)
        terms = jnp.concatenate(
            [
                weight_grad_pass(lefts, rights).reshape(n_exp, tile, -1)[order]
                for order, lefts, rights in groups
            ],
            axis=2,
        )
        return [terms[:pairs].reshape(width // 2, -1), terms[pairs:].reshape(width // 2, -1)]

    def halve(away, kept):
        return kept, lax.ppermute(away, "exp", [(e, e ^ 1) for e in range(n_exp)])

    def joined(halved):
        total = add_terms(halved)
        return total.reshape(pairs * n_ctx, own, total.shape[1])

    def to_owner(terms):
        got = lax.all_to_all(
            terms, everyone, split_axis=0, concat_axis=0, tiled=True, axis_index_groups=alike
        )
        return got.astype(f32)

    def by_core_cols(got):
        got = jnp.sum(got.reshape(-1, CORES, own, got.shape[2]), axis=0)
        return jnp.transpose(got, (1, 0, 2))

    evens = jnp.arange(pairs, dtype=jnp.int32) * 2
    plain = jnp.concatenate([evens + 1 - odd, evens + odd])
    steps = n_exp // 4
    true_core, true_half, place = plain // (2 * steps), plain // steps % 2, plain % steps
    mixed_order = (true_half * CORES + (true_core + core) % CORES) * steps + place
    gm_chip, result_rows, second_away, first_away = hold(
        (gm_chip, result_rows, second_away, first_away)
    )
    gm_parts = [
        by_core(part[:, 0], other_core(part[:, 1]), axis=1).reshape(full, half) for part in gm_chip
    ]
    returned = exchange_all(result_rows)
    second_sent += [send_grad(second_away, n, cuts) for n in range(early, len(second_away))]

    wo_terms = halve(*blocks_of([(mixed_order, mixeds, branches)]))
    grad_qkvs = [[None, None] for s in range(seqs)]
    found_parts, w_terms, first_sent, previous = [], [], [], None
    call = 0
    for h in halves:
        for s in range(seqs):
            cols = slice(h * half // 2, (h + 1) * half // 2)
            gm_part = gm_parts[s][:, cols]
            if call == 0:
                first_sent = [send_grad(first_away, n, cuts) for n in range(len(first_away))]
            if call:
                gm_part, previous = hold((gm_part, previous))
            if call == calls - 2:
                gm_part, wo_terms = hold((gm_part, wo_terms))
            if call == calls - 1:
                gm_part, returned = hold((gm_part, returned))
            previous = attention_backward(qkvs[s][h], gm_part, probs[call])
            grad_qkvs[s][h] = previous
            call += 1
            if s == seqs - 1:
                terms = blocks_of([(plain, acts, [grad_qkvs[i][h] for i in range(seqs)])])
                previous, terms = hold((grad_qkvs[s][h], terms))
                grad_qkvs[s][h] = previous
                w_terms.append(halve(*terms))
            if h == 1:
                if call == calls - 1:
                    grad_qkvs[s][h], w_terms[0], second_sent, first_sent[0] = hold(
                        (grad_qkvs[s][h], w_terms[0], second_sent, first_sent[0])
                    )
                if call == calls:
                    grad_qkvs[s][h], found_parts = hold((grad_qkvs[s][h], found_parts))
                away, kept = grad_act_pass(core, grad_qkvs[s], qkv_weights, chips)
                previous, kept = hold((previous, kept))
                total = (kept.astype(f32) + other_core(away).astype(f32)).astype(bf16)
                if call == calls:
                    w_terms[1], returned, first_whole, found_parts = (
                        after(value, total)
                        for value in (w_terms[1], returned, first_whole, found_parts)
                    )
                found_parts.append(chip_send(total))
                grad_qkvs[s][h] = previous
    second_whole = after(second_whole, previous)
    value = joined([w_terms[1]])
    columns = value.shape[2]
    first = True
    upper_bits = [b for b in (2, 4, 8, 16) if b < n_exp]
    axes = [("exp", b) for b in upper_bits[::-1]] + [("ctx", b) for b in chip_bits[::-1]]
    value = value.reshape((2,) * len(axes) + (CORES, own, columns))
    for step in [("exp", b) for b in upper_bits] + axes[len(upper_bits) :]:
        axis, bit = step
        at = axes.index(step)
        index = exp if axis == "exp" else chip
        upper = jnp.where((index & bit) != 0, 1, 0)
        kept = lax.dynamic_index_in_dim(value, upper, at, keepdims=False)
        away = lax.dynamic_index_in_dim(value, 1 - upper, at, keepdims=False)
        if axis == "exp":
            other = lax.ppermute(away, "exp", [(e, e ^ bit) for e in range(n_exp)])
        else:
            other = ctx_send(away, lambda c: c ^ (bit * CORES))
        if first:
            other, found_parts[-1], first_sent[1:] = hold(
                (other, found_parts[-1], first_sent[1:])
            )
            first = False
        value = (kept.astype(f32) + other.astype(f32)).astype(bf16)
        axes.remove(step)
    second_sum = by_core(
        pick(value, core), other_core(pick(value, 1 - core)), axis=1
    ).astype(f32)
    grad_tokens, small_one = None, []
    for s in range(seqs):
        grad_tokens, sums = finish(
            chip, found_parts[s], tokens_four, grad_hiddens[s], gain_one, s, grad_tokens
        )
        small_one.append(sums)
    small_one = sum(small_one)
    grad_tokens = grad_tokens.reshape(tokens.shape)
    grad_expert_out = own_grads(second_whole, second_sent, cuts)
    grad_expert_in = own_grads(first_whole, first_sent, cuts)
    first_sum = to_owner(joined([w_terms[0], wo_terms]))
    grad_output = jnp.sum(first_sum[:, :, parts:], axis=0)
    grad_w = jnp.concatenate([by_core_cols(first_sum[:, :, :parts]), second_sum], axis=2)
    grad_w = grad_w.reshape(own, width // LANES, 3, LANES)
    grad_query, grad_key, grad_value = (grad_w[:, :, t].reshape(own, width) for t in range(3))

    block_out = None
    for s in range(seqs):
        block_out = combine(
            targets[s], returned, hiddens[s], tokens_four.shape, s, block_out
        )
    block_out = block_out.reshape(tokens.shape)
    small_two = sum(small_two)
    small = jnp.stack(
        [
            value.reshape(devices, own)
            for value in (small_one[0], small_one[1], small_two[0], small_two[1])
        ],
        axis=1,
    )
    small = jnp.sum(exchange_all(small), axis=0)
    return (
        block_out,
        grad_tokens,
        grad_query,
        grad_key,
        grad_value,
        grad_output,
        small[0],
        small[1],
        small[2],
        small[3],
        grad_expert_in,
        grad_expert_out,
    )


def solution(mesh):
    rows = P("exp", "ctx", None)
    weight = P(("exp", "ctx"), None)
    vector = P(("exp", "ctx"))
    return jax.shard_map(
        body,
        mesh=mesh,
        in_specs=(
            rows,
            P("exp"),
            P("ctx", "exp", None, None),
            rows,
            weight,
            weight,
            weight,
            weight,
            P(),
            P(),
            P(),
            P(),
            rows,
            rows,
        ),
        out_specs=(rows, rows, weight, weight, weight, weight)
        + (vector, vector, vector, vector)
        + (rows, rows),
        check_vma=False,
    )
```

```python
import functools

import jax
import jax.numpy as jnp
from jax import lax
from jax.experimental import pallas as pl
from jax.experimental.pallas import tpu as pltpu
from jax.sharding import PartitionSpec as P

HEAD_DIM = 64
LANES = 128
PAIR = 3 * LANES
BLOCK = 256
LOG2E = 1.4426950408889634
CORES = 2

eps_norm = 1e-05
masked_score = -1e30
f32 = jnp.float32
bf16 = jnp.bfloat16
NN = (((1,), (0,)), ((), ()))
NT = (((1,), (1,)), ((), ()))
TN = (((0,), (0,)), ((), ()))
VMEM_LIMIT = 56 * 1024 * 1024
PARAMS = pltpu.CompilerParams(vmem_limit_bytes=VMEM_LIMIT)


def cost(flops):
    return pl.CostEstimate(flops=int(flops / 10), bytes_accessed=1024, transcendentals=0)


hold = lax.optimization_barrier


def after(value, *others):
    return hold((value, others))[0]


def mm(a, b, dims=NN):
    return lax.dot_general(a, b, dims, preferred_element_type=f32)


def head_operands(length, q, k):
    full = q.shape[0]
    lane = lax.broadcasted_iota(jnp.int32, (full, LANES), 1)
    pos = lax.broadcasted_iota(jnp.int32, (full, LANES), 0)
    bias = jnp.where(pos < length, 0.0, masked_score).astype(f32)
    inside, q_aug, k_aug = [], [], []
    for head in range(2):
        own = (lane // HEAD_DIM) == head
        spare = lane == HEAD_DIM * (1 - head)
        inside.append(own)
        q_aug.append(jnp.where(own, q, jnp.where(spare, 1.0, 0.0)).astype(bf16))
        k_aug.append(jnp.where(own, k, jnp.where(spare, bias, 0.0)).astype(bf16))
    return inside, q_aug, k_aug


def attention_forward_kernel(len_ref, x_ref, o_ref):
    full = x_ref.shape[0]
    q, k, v = (x_ref[:, LANES * t : LANES * (t + 1)].astype(f32) for t in range(3))
    inside, q_aug, k_aug = head_operands(len_ref[pl.program_id(0)], q, k)
    v_own = [jnp.where(own, v, 0.0).astype(bf16) for own in inside]
    to_log2 = HEAD_DIM**-0.5 * LOG2E
    row = lax.broadcasted_iota(jnp.int32, (BLOCK, BLOCK), 0)
    col = lax.broadcasted_iota(jnp.int32, (BLOCK, BLOCK), 1)
    causal = col <= row
    for i in range(full // BLOCK):
        here, before = slice(i * BLOCK, (i + 1) * BLOCK), slice(0, i * BLOCK)
        total = jnp.zeros((BLOCK, LANES), f32)
        for head in range(2):
            qi = q_aug[head][here]
            s_here = jnp.where(causal, mm(qi, k_aug[head][here], NT) * to_log2, masked_score)
            top = jnp.max(s_here, axis=1, keepdims=True)
            if i:
                s_before = mm(qi, k_aug[head][before], NT) * to_log2
                top = jnp.maximum(top, jnp.max(s_before, axis=1, keepdims=True))
            p_here = jnp.exp2(s_here - top)
            mass = jnp.sum(p_here, axis=1, keepdims=True)
            if i:
                p_before = jnp.exp2(s_before - top)
                mass = mass + jnp.sum(p_before, axis=1, keepdims=True)
            inverse = 1.0 / mass
            total = total + mm((p_here * inverse).astype(bf16), v_own[head][here])
            if i:
                total = total + mm((p_before * inverse).astype(bf16), v_own[head][before])
        o_ref[here, :] = total.astype(bf16)


def attention_forward(lens, qkv, full):
    n_seq, pairs = qkv.shape[0] // full, qkv.shape[1] // PAIR
    return pl.pallas_call(
        attention_forward_kernel,
        grid_spec=pltpu.PrefetchScalarGridSpec(
            num_scalar_prefetch=1,
            grid=(n_seq, pairs),
            in_specs=[pl.BlockSpec((full, PAIR), lambda s, p, l: (s, p))],
            out_specs=pl.BlockSpec((full, LANES), lambda s, p, l: (s, p)),
        ),
        out_shape=jax.ShapeDtypeStruct((n_seq * full, pairs * LANES), bf16),
        compiler_params=PARAMS,
        cost_estimate=cost(n_seq * pairs * 2.5e9),
        name="attention_forward",
    )(lens, qkv)


def attention_probs_kernel(len_ref, x_ref, p_ref):
    full = x_ref.shape[0]
    q, k = (x_ref[:, LANES * t : LANES * (t + 1)].astype(f32) for t in range(2))
    _, q_aug, k_aug = head_operands(len_ref[pl.program_id(0)], q, k)
    to_log2 = HEAD_DIM**-0.5 * LOG2E
    row = lax.broadcasted_iota(jnp.int32, (BLOCK, BLOCK), 0)
    col = lax.broadcasted_iota(jnp.int32, (BLOCK, BLOCK), 1)
    causal = row <= col
    for i in range(full // BLOCK):
        here, before = slice(i * BLOCK, (i + 1) * BLOCK), slice(0, i * BLOCK)
        for head in range(2):
            qi = q_aug[head][here]
            s_here = jnp.where(causal, mm(k_aug[head][here], qi, NT) * to_log2, masked_score)
            top = jnp.max(s_here, axis=0, keepdims=True)
            if i:
                s_before = mm(k_aug[head][before], qi, NT) * to_log2
                top = jnp.maximum(top, jnp.max(s_before, axis=0, keepdims=True))
            p_here = jnp.exp2(s_here - top)
            mass = jnp.sum(p_here, axis=0, keepdims=True)
            if i:
                p_before = jnp.exp2(s_before - top)
                mass = mass + jnp.sum(p_before, axis=0, keepdims=True)
            inverse = 1.0 / mass
            p_ref[head, here, here] = (p_here * inverse).astype(bf16)
            if i:
                p_ref[head, before, here] = (p_before * inverse).astype(bf16)


def attention_probs(lens, qkv, full):
    n_seq, pairs = qkv.shape[0] // full, qkv.shape[1] // PAIR
    return pl.pallas_call(
        attention_probs_kernel,
        grid_spec=pltpu.PrefetchScalarGridSpec(
            num_scalar_prefetch=1,
            grid=(n_seq, pairs),
            in_specs=[pl.BlockSpec((full, PAIR), lambda s, p, l: (s, p))],
            out_specs=pl.BlockSpec((2, full, full), lambda s, p, l: (s * pairs + p, 0, 0)),
        ),
        out_shape=jax.ShapeDtypeStruct((n_seq * pairs * 2, full, full), bf16),
        compiler_params=PARAMS,
        cost_estimate=cost(n_seq * pairs * 2.0e9),
        name="attention_probs",
    )(lens, qkv)


def attention_backward_kernel(x_ref, g_ref, p_ref, o_ref, d_scr):
    full = x_ref.shape[0]
    q, k = (x_ref[:, LANES * t : LANES * (t + 1)].astype(f32) for t in range(2))
    v = x_ref[:, 2 * LANES : 3 * LANES]
    g = g_ref[...].astype(f32)
    head_of = lax.broadcasted_iota(jnp.int32, (full, LANES), 1) // HEAD_DIM
    inside = [head_of == head for head in range(2)]
    q_own = [jnp.where(own, q, 0.0).astype(bf16) for own in inside]
    k_own = [jnp.where(own, k, 0.0).astype(bf16) for own in inside]
    g_own = [jnp.where(own, g, 0.0).astype(bf16) for own in inside]
    scale = HEAD_DIM**-0.5
    count = full // BLOCK
    for i in range(count):
        here, until = slice(i * BLOCK, (i + 1) * BLOCK), slice(0, (i + 1) * BLOCK)
        dq = jnp.zeros((BLOCK, LANES), f32)
        for head in range(2):
            probs = p_ref[head, until, here].astype(f32)
            grad = mm(v[until], g_own[head][here], NT)
            delta = jnp.sum(grad * probs, axis=0, keepdims=True)
            d_score = (probs * (grad - delta)).astype(bf16)
            d_scr[head, until, here] = d_score
            dq = dq + mm(d_score, k_own[head][until], TN)
        o_ref[here, 0:LANES] = (dq * scale).astype(bf16)
    for j in range(count):
        here, after_ = slice(j * BLOCK, (j + 1) * BLOCK), slice(j * BLOCK, full)
        dk = mm(d_scr[0, here, after_], q_own[0][after_]) + mm(
            d_scr[1, here, after_], q_own[1][after_]
        )
        dv = mm(p_ref[0, here, after_], g_own[0][after_]) + mm(
            p_ref[1, here, after_], g_own[1][after_]
        )
        o_ref[here, LANES : 2 * LANES] = (dk * scale).astype(bf16)
        o_ref[here, 2 * LANES : 3 * LANES] = dv.astype(bf16)


def attention_backward(qkv, g, probs):
    full = probs.shape[1]
    n_seq, pairs = qkv.shape[0] // full, qkv.shape[1] // PAIR
    return pl.pallas_call(
        attention_backward_kernel,
        grid=(n_seq, pairs),
        in_specs=[
            pl.BlockSpec((full, PAIR), lambda s, p: (s, p)),
            pl.BlockSpec((full, LANES), lambda s, p: (s, p)),
            pl.BlockSpec((2, full, full), lambda s, p: (s * pairs + p, 0, 0)),
        ],
        out_specs=pl.BlockSpec((full, PAIR), lambda s, p: (s, p)),
        scratch_shapes=[pltpu.VMEM((2, full, full), bf16)],
        out_shape=jax.ShapeDtypeStruct(qkv.shape, bf16),
        compiler_params=PARAMS,
        cost_estimate=cost(n_seq * pairs * 3.0e9),
        name="attention_backward",
    )(qkv, g, probs)


def tile_of(count, most=320):
    return max(t for t in range(16, most + 1, 16) if count % t == 0)


def pieces_of(shards):
    start = 0
    for ref in shards:
        size = min(512, ref.shape[0])
        for h in range(0, ref.shape[0], size):
            yield ref, slice(h, h + size), slice(start, start + size)
            start += size


def shard_specs(shards):
    return [pl.BlockSpec(w.shape, lambda i: (0, 0)) for w in shards]


def hidden_of(shards):
    return sum(w.shape[0] for w in shards)


def grad_activ_kernel(g_ref, *refs):
    for w_ref, part, cols in pieces_of(refs[:-1]):
        refs[-1][:, cols] = mm(g_ref[...], w_ref[part, :], NT).astype(bf16)


def grad_activ_pass(g, shards):
    (count, width), hidden = g.shape, hidden_of(shards)
    tile = tile_of(count)
    return pl.pallas_call(
        grad_activ_kernel,
        grid=(count // tile,),
        in_specs=[pl.BlockSpec((tile, width), lambda i: (i, 0))] + shard_specs(shards),
        out_specs=pl.BlockSpec((tile, hidden), lambda i: (i, 0)),
        out_shape=jax.ShapeDtypeStruct((count, hidden), bf16),
        compiler_params=PARAMS,
        cost_estimate=cost(count * hidden * width / 2),
        name="grad_activ_pass",
    )(g, *shards)


def hidden_kernel(x_ref, ga_ref, *refs, before):
    shards, (a_ref, gp_ref, gs_ref) = refs[before:-3], refs[-3:]
    for w_ref, part, cols in pieces_of(shards):
        activ, slope = gelu_parts(mm(x_ref[...], w_ref[part, :], NT))
        a_ref[:, cols] = activ.astype(bf16)
        gp_ref[:, cols] = (ga_ref[:, cols].astype(f32) * slope).astype(bf16)
    total = product_of(gp_ref, shards)
    if before:
        total = total + refs[0][...]
    gs_ref[...] = total.astype(gs_ref.dtype)


def product_of(rows_ref, shards):
    total, start = None, 0
    for w_ref in shards:
        cols = slice(start, start + w_ref.shape[0])
        part = mm(rows_ref[:, cols], w_ref[...])
        total = part if total is None else total + part
        start += w_ref.shape[0]
    return total


def hidden_pass(x, grad_activ, shards, dtype, before=None):
    (count, width), hidden = x.shape, hidden_of(shards)
    tile = tile_of(count)
    wide = pl.BlockSpec((tile, hidden), lambda i: (i, 0))
    thin = pl.BlockSpec((tile, width), lambda i: (i, 0))
    more = [] if before is None else [before]
    return pl.pallas_call(
        functools.partial(hidden_kernel, before=len(more)),
        grid=(count // tile,),
        in_specs=[thin, wide] + [thin] * len(more) + shard_specs(shards),
        out_specs=[wide, wide, thin],
        out_shape=[jax.ShapeDtypeStruct((count, hidden), bf16)] * 2
        + [jax.ShapeDtypeStruct((count, width), dtype)],
        compiler_params=PARAMS,
        cost_estimate=cost(2 * count * hidden * width),
        name="hidden_pass",
    )(x, grad_activ, *more, *shards)


def down_kernel(*refs, own, more):
    last = len(refs) - 1 - more
    total = product_of(refs[0], refs[2 : 2 + own]) + product_of(refs[1], refs[2 + own : last])
    for term in refs[last:-1]:
        total = total + term[...].astype(f32)
    refs[-1][...] = total.astype(bf16)


def down_pass(activs, groups, terms=()):
    count, width = activs[0].shape[0], groups[0][0].shape[1]
    tile = tile_of(count)
    shards = list(groups[0]) + list(groups[1])
    return pl.pallas_call(
        functools.partial(down_kernel, own=len(groups[0]), more=len(terms)),
        grid=(count // tile,),
        in_specs=[pl.BlockSpec((tile, a.shape[1]), lambda i: (i, 0)) for a in activs]
        + shard_specs(shards)
        + [pl.BlockSpec((tile, width), lambda i: (i, 0)) for _ in terms],
        out_specs=pl.BlockSpec((tile, width), lambda i: (i, 0)),
        out_shape=jax.ShapeDtypeStruct((count, width), bf16),
        compiler_params=PARAMS,
        cost_estimate=cost(2 * count * hidden_of(shards) * width),
        name="down_pass",
    )(*activs, *shards, *terms)


def summed(lefts, rights):
    total = mm(lefts[0][...], rights[0][...], TN)
    for left, right in zip(lefts[1:], rights[1:]):
        total = total + mm(left[...], right[...], TN)
    return total


def weight_grad_kernel(*refs):
    count = len(refs) // 2
    refs[-1][...] = summed(refs[:count], refs[count:-1]).astype(bf16)


def weight_grad_pass(lefts, rights):
    hidden, width = lefts[0].shape[1], rights[0].shape[1]
    tile = min(256, hidden)
    return pl.pallas_call(
        weight_grad_kernel,
        grid=(hidden // tile,),
        in_specs=[pl.BlockSpec((v.shape[0], tile), lambda i: (0, i)) for v in lefts]
        + [pl.BlockSpec(v.shape, lambda i: (0, 0)) for v in rights],
        out_specs=pl.BlockSpec((tile, width), lambda i: (i, 0)),
        out_shape=jax.ShapeDtypeStruct((hidden, width), bf16),
        compiler_params=PARAMS,
        cost_estimate=cost(2 * lefts[0].size * width * len(lefts)),
        name="weight_grad_pass",
    )(*lefts, *rights)


def split_grad_kernel(order_ref, *refs, tile, counts):
    values, start, col = refs[:-2], 0, 0
    steps = order_ref.shape[0] // len(counts)
    totals = []
    for group, count in enumerate(counts):
        lefts, rights = values[start : start + count], values[start + count : start + 2 * count]
        first = group * steps + pl.program_id(0) * (steps // 2)
        places = [order_ref[first + n] for n in range(steps // 2)]
        total = None
        for left, right in zip(lefts, rights):
            chosen = jnp.concatenate(
                [left[:, pl.ds(pl.multiple_of(place * tile, tile), tile)] for place in places],
                axis=1,
            )
            part = mm(chosen, right[...], TN)
            total = part if total is None else total + part
        totals.append((slice(col, col + total.shape[1]), total.astype(bf16)))
        start += 2 * count
        col += total.shape[1]

    for which in range(2):

        @pl.when(pl.program_id(0) == which)
        def _(which=which):
            for cols, total in totals:
                refs[which - 2][:, cols] = total


def split_grad_pass(groups, tile):
    hidden = groups[0][1][0].shape[1]
    width = sum(rights[0].shape[1] for _, _, rights in groups)
    values = [v for _, lefts, rights in groups for v in (*lefts, *rights)]
    out = jax.ShapeDtypeStruct((hidden // 2, width), bf16)
    return pl.pallas_call(
        functools.partial(split_grad_kernel, tile=tile, counts=[len(g[1]) for g in groups]),
        grid_spec=pltpu.PrefetchScalarGridSpec(
            num_scalar_prefetch=1,
            grid=(2,),
            in_specs=[pl.BlockSpec(v.shape, lambda i, o: (0, 0)) for v in values],
            out_specs=[pl.BlockSpec(out.shape, lambda i, o: (0, 0))] * 2,
        ),
        out_shape=[out, out],
        compiler_params=PARAMS,
        cost_estimate=cost(2 * width * sum(v.size for v in groups[0][1])),
        name="split_grad_pass",
    )(jnp.concatenate([order for order, _, _ in groups]), *values)


def add_terms_kernel(*refs):
    col = 0
    for one, two in zip(refs[0:-1:2], refs[1:-1:2]):
        cols = slice(col, col + one.shape[1])
        refs[-1][:, cols] = (one[...].astype(f32) + two[...].astype(f32)).astype(bf16)
        col = cols.stop


def add_terms(pairs):
    count = pairs[0][0].shape[0]
    tile = min(128, count)
    values = [v for pair in pairs for v in pair]
    width = sum(pair[0].shape[1] for pair in pairs)
    return pl.pallas_call(
        add_terms_kernel,
        grid=(count // tile,),
        in_specs=[pl.BlockSpec((tile, v.shape[1]), lambda i: (i, 0)) for v in values],
        out_specs=pl.BlockSpec((tile, width), lambda i: (i, 0)),
        out_shape=jax.ShapeDtypeStruct((count, width), bf16),
        compiler_params=PARAMS,
        cost_estimate=cost(3.0e10),
        name="add_terms",
    )(*values)


def expert_grad_kernel(sub_ref, *refs, count, pieces, per):
    step = pl.program_id(0)
    rights = refs[2 * count : 3 * count]

    @pl.when(step < pieces * per)
    def _():
        total = summed(refs[count : 2 * count], rights).astype(bf16)
        for n in range(pieces):

            @pl.when((step >= n * per) & (step < (n + 1) * per))
            def _(n=n):
                refs[3 * count + n][...] = total

    @pl.when(step >= pieces * per)
    def _():
        refs[-1][0] = summed(refs[:count], rights)


def expert_grad_pass(sub, owns, others, rights, experts, parts):
    shard, width = owns[0].shape[1], rights[0].shape[1]
    tile = min(256, shard // parts)
    pieces, per, own = (experts - 1) * parts, shard // parts // tile, shard // tile
    far = pieces * per

    def piece_spec(n):
        return pl.BlockSpec((tile, width), lambda i, s: (jnp.clip(i - n * per, 0, per - 1), 0))

    return pl.pallas_call(
        functools.partial(expert_grad_kernel, count=len(owns), pieces=pieces, per=per),
        grid_spec=pltpu.PrefetchScalarGridSpec(
            num_scalar_prefetch=1,
            grid=(far + own,),
            in_specs=[
                pl.BlockSpec((v.shape[0], tile), lambda i, s: (0, jnp.clip(i - far, 0, own - 1)))
                for v in owns
            ]
            + [
                pl.BlockSpec((v.shape[0], tile), lambda i, s: (0, jnp.clip(i, 0, far - 1)))
                for v in others
            ]
            + [pl.BlockSpec(v.shape, lambda i, s: (0, 0)) for v in rights],
            out_specs=[piece_spec(n) for n in range(pieces)]
            + [
                pl.BlockSpec(
                    (1, tile, width), lambda i, s: (s[0], jnp.clip(i - far, 0, own - 1), 0)
                )
            ],
        ),
        out_shape=[jax.ShapeDtypeStruct((shard // parts, width), bf16)] * pieces
        + [jax.ShapeDtypeStruct((experts, shard, width), f32)],
        compiler_params=PARAMS,
        cost_estimate=cost(2 * experts * owns[0].size * width * len(owns)),
        name="expert_grad_pass",
    )(sub.reshape(1), *owns, *others, *rights)


def assemble_kernel(sub_ref, whole_ref, *refs):
    pieces, o_ref = refs[:-1], refs[-1]
    for n, piece in enumerate(pieces):

        @pl.when(pl.program_id(0) * pl.num_programs(1) + pl.program_id(1) == n)
        def _(piece=piece):
            o_ref[0] = piece[...].astype(f32)


def assemble(sub, whole, pieces):
    experts = whole.shape[0]
    parts = len(pieces) // (experts - 1)
    cut, width = pieces[0].shape

    def place(r, n, s):
        return (lax.rem(s[0] - r - 1 + experts, experts), n, 0)

    return pl.pallas_call(
        assemble_kernel,
        grid_spec=pltpu.PrefetchScalarGridSpec(
            num_scalar_prefetch=1,
            grid=(experts - 1, parts),
            in_specs=[pl.BlockSpec(memory_space=pl.ANY)]
            + [pl.BlockSpec((cut, width), lambda r, n, s: (0, 0)) for _ in pieces],
            out_specs=pl.BlockSpec((1, cut, width), place),
        ),
        out_shape=jax.ShapeDtypeStruct(whole.shape, f32),
        input_output_aliases={1: 0},
        compiler_params=PARAMS,
        cost_estimate=cost(3.0e10),
        name="assemble",
    )(sub.reshape(1), whole, *pieces)


def gelu_parts(pre):
    outer, inner = 0.7978845608028654, 0.044715
    square = pre * pre
    half = 0.5 + 0.5 * jnp.tanh(pre * (outer + outer * inner * square))
    value = pre * half
    slope = half + value * (1.0 - half) * (2.0 * outer + 6.0 * outer * inner * square)
    return value, slope


def dispatch_kernel(*refs):
    o_ref, count = refs[-1], len(refs) // 2
    tile = o_ref.shape[0]
    total = None
    for t_ref, v_ref in zip(refs[:count], refs[count:-1]):
        rows = v_ref.shape[0]
        slot = lax.broadcasted_iota(jnp.int32, (tile, rows), 0) + pl.program_id(0) * tile
        chosen = jnp.where(t_ref[...] == slot, 1.0, 0.0).astype(bf16)
        part = mm(chosen, v_ref[...])
        total = part if total is None else total + part
    o_ref[...] = total.astype(bf16)


def dispatch(targets, values, slots):
    tile, width = tile_of(slots), values[0].shape[1]
    return pl.pallas_call(
        dispatch_kernel,
        grid=(slots // tile,),
        in_specs=[pl.BlockSpec((1, v.shape[0]), lambda i: (0, 0)) for v in values]
        + [pl.BlockSpec(v.shape, lambda i: (0, 0)) for v in values],
        out_specs=pl.BlockSpec((tile, width), lambda i: (i, 0)),
        out_shape=jax.ShapeDtypeStruct((slots, width), bf16),
        compiler_params=PARAMS,
        cost_estimate=cost(2 * slots * width * sum(v.shape[0] for v in values)),
        name="dispatch",
    )(*[t.reshape(1, -1) for t in targets], *values)


def returned_rows(target, rows_ref):
    slots = rows_ref.shape[0]
    slot = lax.broadcasted_iota(jnp.int32, (target.shape[0], slots), 1)
    return mm(jnp.where(target == slot, 1.0, 0.0).astype(bf16), rows_ref[...])


def combine_kernel(t_ref, rows_ref, h_ref, *refs):
    refs[-1][0, 0] = (h_ref[...] + returned_rows(t_ref[...], rows_ref)).astype(bf16)


def into_whole(whole, place):
    if whole is None:
        return [], [], {}
    return [pl.BlockSpec(memory_space=pl.ANY)], [whole], {place: 0}


def combine(target, rows, hidden, shape, seq, whole):
    chips, _, span, width = shape
    specs, arrays, aliases = into_whole(whole, 3)
    return pl.pallas_call(
        combine_kernel,
        grid=(chips,),
        in_specs=[
            pl.BlockSpec((span, 1), lambda j: (j, 0)),
            pl.BlockSpec(rows.shape, lambda j: (0, 0)),
            pl.BlockSpec((span, width), lambda j: (j, 0)),
        ]
        + specs,
        out_specs=pl.BlockSpec((1, 1, span, width), lambda j: (j, seq, 0, 0)),
        out_shape=jax.ShapeDtypeStruct(shape, bf16),
        input_output_aliases=aliases,
        compiler_params=PARAMS,
        cost_estimate=cost(20 * chips * span * width * rows.shape[0]),
        name="combine",
    )(target.reshape(-1, 1), rows, hidden, *arrays)


def project_kernel(a_ref, b_ref, t_ref, w_ref, gain_ref, shift_ref, h_ref, s_ref, m_ref):
    mixed = jnp.concatenate([a_ref[0, 0], a_ref[0, 1], b_ref[0, 0], b_ref[0, 1]], axis=1)
    m_ref[...] = mixed
    hidden = t_ref[0, 0].astype(f32) + mm(mixed, w_ref[...])
    h_ref[...] = hidden
    normal, _ = norm_parts(hidden)
    s_ref[...] = (normal * gain_ref[...] + shift_ref[...]).astype(bf16)


def project_norm(parts, tokens, seq, weight, gain, shift):
    chips, cores, span, cols = parts[0].shape
    width = tokens.shape[3]
    block = pl.BlockSpec((1, cores, span, cols), lambda j: (j, 0, 0, 0))
    row = pl.BlockSpec((1, width), lambda j: (0, 0))
    out = pl.BlockSpec((span, width), lambda j: (j, 0))
    return pl.pallas_call(
        project_kernel,
        grid=(chips,),
        in_specs=[
            block,
            block,
            pl.BlockSpec((1, 1, span, width), lambda j: (j, seq, 0, 0)),
            pl.BlockSpec((width, width), lambda j: (0, 0)),
            row,
            row,
        ],
        out_specs=[out] * 3,
        out_shape=[
            jax.ShapeDtypeStruct((chips * span, width), dtype) for dtype in (f32, bf16, bf16)
        ],
        compiler_params=PARAMS,
        cost_estimate=cost(2 * chips * span * width * width),
        name="project_norm",
    )(*parts, tokens, weight, gain.reshape(1, -1), shift.reshape(1, -1))


def project_back_kernel(
    t_ref, rows_ref, h_ref, c_ref, w_ref, gain_ref, gh_ref, gb_ref, gm_ref, small_ref
):
    grad = returned_rows(t_ref[...], rows_ref)
    normal, inverse = norm_parts(h_ref[...])
    grad_hidden = c_ref[0, 0].astype(f32) + norm_back(grad, normal, inverse, gain_ref[...])
    gh_ref[...] = grad_hidden
    branch = grad_hidden.astype(bf16)
    gb_ref[...] = branch
    mixed = mm(branch, w_ref[...], NT).astype(bf16)
    cols = gm_ref.shape[3] // 2
    for half in range(2):
        for k in range(CORES):
            at = (half * CORES + k) * cols
            gm_ref[0, k, :, half * cols : (half + 1) * cols] = mixed[:, at : at + cols]
    sums = jnp.concatenate(
        [
            jnp.sum(grad * normal, axis=0, keepdims=True),
            jnp.sum(grad, axis=0, keepdims=True),
        ],
        axis=0,
    )

    @pl.when(pl.program_id(0) == 0)
    def _():
        small_ref[...] = sums

    @pl.when(pl.program_id(0) > 0)
    def _():
        small_ref[...] += sums


def project_back(target, rows, hidden, cotangent, seq, weight, gain):
    chips, _, span, width = cotangent.shape
    out = pl.BlockSpec((span, width), lambda j: (j, 0))
    return pl.pallas_call(
        project_back_kernel,
        grid=(chips,),
        in_specs=[
            pl.BlockSpec((span, 1), lambda j: (j, 0)),
            pl.BlockSpec(rows.shape, lambda j: (0, 0)),
            out,
            pl.BlockSpec((1, 1, span, width), lambda j: (j, seq, 0, 0)),
            pl.BlockSpec((width, width), lambda j: (0, 0)),
            pl.BlockSpec((1, width), lambda j: (0, 0)),
        ],
        out_specs=[
            out,
            out,
            pl.BlockSpec((1, CORES, span, width // CORES), lambda j: (j, 0, 0, 0)),
            pl.BlockSpec((2, width), lambda j: (0, 0)),
        ],
        out_shape=[
            jax.ShapeDtypeStruct((chips * span, width), f32),
            jax.ShapeDtypeStruct((chips * span, width), bf16),
            jax.ShapeDtypeStruct((chips, CORES, span, width // CORES), bf16),
            jax.ShapeDtypeStruct((2, width), f32),
        ],
        compiler_params=PARAMS,
        cost_estimate=cost(6 * chips * span * width * width),
        name="project_back",
    )(target.reshape(-1, 1), rows, hidden, cotangent, weight, gain.reshape(1, -1))


def grad_act_kernel(core_ref, *refs):
    count = (len(refs) - 2) // 2
    total = None
    for d_ref, w_ref in zip(refs[:count], refs[count:-2]):
        part = mm(d_ref[...], w_ref[...], NT)
        total = part if total is None else total + part
    for which in range(2):

        @pl.when(pl.program_id(0) == which)
        def _(which=which):
            refs[which - 2][0] = total.astype(bf16)


def grad_act_pass(core, grads, weights, chips):
    width = weights[0].shape[0]
    span = grads[0].shape[0] // (chips * CORES)
    out = jax.ShapeDtypeStruct((chips, span, width), bf16)

    def rows(which, j, c):
        return (j * CORES + jnp.where(which == 0, 1 - c[0], c[0]), 0)

    return pl.pallas_call(
        grad_act_kernel,
        grid_spec=pltpu.PrefetchScalarGridSpec(
            num_scalar_prefetch=1,
            grid=(2, chips),
            in_specs=[pl.BlockSpec((span, g.shape[1]), rows) for g in grads]
            + [pl.BlockSpec(w.shape, lambda which, j, c: (0, 0)) for w in weights],
            out_specs=[
                pl.BlockSpec(
                    (1, span, width), lambda which, j, c: (jnp.where(which == 0, j, chips - 1), 0, 0)
                ),
                pl.BlockSpec(
                    (1, span, width), lambda which, j, c: (jnp.where(which == 1, j, 0), 0, 0)
                ),
            ],
        ),
        out_shape=[out, out],
        compiler_params=PARAMS,
        cost_estimate=cost(2 * sum(g.size for g in grads) * width),
        name="grad_act_pass",
    )(core.reshape(1), *grads, *weights)


def finish_kernel(chip_ref, *refs, chips):
    found, (t_ref, gh_ref, gain_ref) = refs[:chips], refs[chips : chips + 3]
    o_ref, small_ref, grad_ref = refs[-3:]
    step = pl.program_id(0)
    place = lax.rem(chip_ref[0] - step + chips, chips)
    for n, part in enumerate(found):

        @pl.when(place == n)
        def _(part=part):
            grad_ref[...] = part[...].astype(f32)

    grad = grad_ref[...]
    normal, inverse = norm_parts(t_ref[0, 0].astype(f32))
    o_ref[0, 0] = (gh_ref[...] + norm_back(grad, normal, inverse, gain_ref[...])).astype(bf16)
    sums = jnp.concatenate(
        [
            jnp.sum(grad * normal, axis=0, keepdims=True),
            jnp.sum(grad, axis=0, keepdims=True),
        ],
        axis=0,
    )

    @pl.when(step == 0)
    def _():
        small_ref[...] = sums

    @pl.when(step > 0)
    def _():
        small_ref[...] += sums


def finish(chip, found, tokens, grad_hidden, gain, seq, whole):
    chips, _, span, width = tokens.shape
    specs, arrays, aliases = into_whole(whole, chips + 4)
    return pl.pallas_call(
        functools.partial(finish_kernel, chips=chips),
        grid_spec=pltpu.PrefetchScalarGridSpec(
            num_scalar_prefetch=1,
            grid=(chips,),
            in_specs=[pl.BlockSpec((span, width), lambda j, c: (0, 0)) for _ in found]
            + [
                pl.BlockSpec((1, 1, span, width), lambda j, c: (j, seq, 0, 0)),
                pl.BlockSpec((span, width), lambda j, c: (j, 0)),
                pl.BlockSpec((1, width), lambda j, c: (0, 0)),
            ]
            + specs,
            out_specs=[
                pl.BlockSpec((1, 1, span, width), lambda j, c: (j, seq, 0, 0)),
                pl.BlockSpec((2, width), lambda j, c: (0, 0)),
            ],
            scratch_shapes=[pltpu.VMEM((span, width), f32)],
        ),
        out_shape=[
            jax.ShapeDtypeStruct(tokens.shape, bf16),
            jax.ShapeDtypeStruct((2, width), f32),
        ],
        input_output_aliases=aliases,
        compiler_params=PARAMS,
        cost_estimate=cost(2.0e10),
        name="finish",
    )(chip.reshape(1), *found, tokens, grad_hidden, gain.reshape(1, -1), *arrays)


def norm_parts(values):
    average = jnp.mean(values, axis=-1, keepdims=True)
    centered = values - average
    variance = jnp.mean(centered * centered, axis=-1, keepdims=True)
    inverse = lax.rsqrt(variance + eps_norm)
    return centered * inverse, inverse


def norm_back(grad, normal, inverse, gain):
    inner = grad * gain
    mean_one = jnp.mean(inner, axis=-1, keepdims=True)
    mean_two = jnp.mean(inner * normal, axis=-1, keepdims=True)
    return inverse * (inner - mean_one - normal * mean_two)


def body(
    tokens,
    lengths,
    expert_ids,
    cotangent,
    query_weight,
    key_weight,
    value_weight,
    output_weight,
    gain_one,
    shift_one,
    gain_two,
    shift_two,
    expert_in,
    expert_out,
):
    seq_local, span, width = tokens.shape
    rows = seq_local * span
    n_ctx, n_exp = lax.axis_size("ctx"), lax.axis_size("exp")
    ctx = lax.axis_index("ctx")
    chips = n_ctx // CORES
    chip, core = ctx // CORES, ctx % CORES
    seqs = seq_local // chips
    full = span * n_ctx
    half = width // CORES
    experts = expert_in.shape[0]
    group = n_ctx // experts
    sub, member = ctx // group, ctx % group
    shard = expert_in.shape[1]
    all_experts = experts * n_exp
    capacity = max(2, rows * 5 // (4 * all_experts))
    devices = n_exp * n_ctx
    everyone = ("exp", "ctx")

    def ctx_send(value, target):
        return lax.ppermute(value, "ctx", [(c, target(c)) for c in range(n_ctx)])

    def other_core(value):
        return ctx_send(value, lambda c: c ^ 1)

    def to_chip(value, shift):
        return ctx_send(value, lambda c: ((c // CORES + shift) % chips) * CORES + c % CORES)

    def pick(value, index):
        return lax.dynamic_index_in_dim(value, index, 0, keepdims=False)

    def in_order(found, mine, size):
        out = []
        for place in range(size):
            chosen = found[0]
            for r in range(1, size):
                chosen = jnp.where((mine - place) % size == r, found[r], chosen)
            out.append(chosen)
        return jnp.stack(out)

    def chip_send(value):
        return [pick(value, chip)] + [
            to_chip(pick(value, (chip + r) % chips), r) for r in range(1, chips)
        ]

    def chip_join(found):
        return in_order(found, chip, chips)

    def chip_exchange(value):
        return chip_join(chip_send(value))

    def by_core(mine, other, axis=0):
        first = jnp.where(core == 0, mine, other)
        second = jnp.where(core == 0, other, mine)
        return jnp.stack([first, second], axis=axis)

    def exchange_all(value):
        return lax.all_to_all(value, everyone, split_axis=0, concat_axis=0, tiled=True)

    def by_pair(weight):
        return weight.astype(bf16).reshape(weight.shape[0], width // LANES, 1, LANES)

    exp_bits = [b for b in (2, 4, 8, 16) if b < n_exp]
    chip_bits = [b for b in (1, 2, 4, 8) if b < chips]

    def double(state, axis, bit):
        value, keys = state
        if axis == "exp":
            other = lax.ppermute(value, "exp", [(e, e ^ bit) for e in range(n_exp)])
            index, key = lax.axis_index("exp"), (0, -bit)
        else:
            other = ctx_send(value, lambda c: c ^ (bit * CORES))
            index, key = chip, (1, -bit)
        keys = sorted(keys + [key])
        at = keys.index(key)
        upper = (index & bit) != 0
        low, high = jnp.where(upper, other, value), jnp.where(upper, value, other)
        return jnp.stack([low, high], axis=at), keys

    def gather_cores(weight):
        kept = lax.dynamic_index_in_dim(weight, core, 1, keepdims=False)
        away = lax.dynamic_index_in_dim(weight, 1 - core, 1, keepdims=False)
        return by_core(kept, other_core(away)), [(2, 0)]

    def gather(state, steps):
        for axis, bit in steps:
            state = double(state, axis, bit)
        return state

    first_steps = [("exp", bit) for bit in exp_bits]
    last_steps = [("exp", 1)] + [("ctx", bit) for bit in chip_bits]

    local_qkv = jnp.concatenate(
        [by_pair(query_weight), by_pair(key_weight), by_pair(value_weight)], axis=2
    ).reshape(query_weight.shape[0], CORES, 3 * half)
    parts = 3 * half // 2

    gathered, keys = gather_cores(local_qkv)
    gathered, tokens, expert_ids, expert_out, cotangent = hold(
        (gathered, tokens, expert_ids, expert_out, cotangent)
    )

    ids_flat = expert_ids.reshape(rows)
    positions = ctx * span + jnp.arange(span)
    live = (positions[None, :] < lengths[:, None]).reshape(rows)
    onehot = ((ids_flat[:, None] == jnp.arange(all_experts)[None, :]) & live[:, None]).astype(
        jnp.int32
    )
    place = jnp.arange(rows)
    earlier = (place[None, :] < place[:, None]).astype(bf16)
    ranks = jnp.sum(onehot * mm(earlier, onehot.astype(bf16)).astype(jnp.int32), axis=1)
    keep = live & (ranks < capacity)
    target = jnp.where(keep, ids_flat * capacity + ranks, -1)
    targets = target.reshape(chips, seqs, span)
    targets = [targets[:, s].reshape(chips * span) for s in range(seqs)]
    slots = all_experts * capacity

    inputs = tokens.astype(f32).reshape(rows, width)
    normal_one, inverse_one = norm_parts(inputs)
    act = (normal_one * gain_one + shift_one).astype(bf16).reshape(chips, seqs, span, width)
    tokens_four = tokens.reshape(chips, seqs, span, width)
    cotangent_four = cotangent.reshape(chips, seqs, span, width)
    acts = []
    for s in range(seqs):
        act_chip = chip_exchange(act[:, s])
        acts.append(by_core(act_chip, other_core(act_chip), axis=1).reshape(full, width))

    def sub_send(value, shift):
        return ctx_send(value, lambda c: ((c // group + shift) % experts) * group + c % group)

    def group_send(value, shift):
        return ctx_send(value, lambda c: (c // group) * group + (c % group + shift) % group)

    def casts(weight):
        own, *others = [pick(weight, (sub + r) % experts).astype(bf16) for r in range(experts)]
        return own, others

    def swap(others, parts):
        cut = shard // parts
        return [
            sub_send(low[n * cut : (n + 1) * cut], r)
            for r, low in enumerate(others, 1)
            for n in range(parts)
        ]

    state = gather((gathered, keys), first_steps)
    streams = [
        ((state[0][..., :parts], state[1]), last_steps),
        ((state[0][..., parts:], state[1]), last_steps[::-1]),
    ]
    streams = [(gather(part, steps[:1]), steps[1:]) for part, steps in streams]
    values = [part[0] for part, _ in streams]
    values, expert_in, expert_out, cotangent_late = hold(
        (values, expert_in, expert_out, cotangent)
    )
    grad_send = dispatch([target], [cotangent_late.reshape(rows, width)], slots)
    first_own, first_low = casts(expert_in)
    second_own, second_low = casts(expert_out)
    qkv_weights = [
        gather((value, part[1]), steps)[0].reshape(width, parts)
        for value, (part, steps) in zip(values, streams)
    ]
    out_low = output_weight.astype(bf16)
    acts, qkv_weights, grad_send, second_low, out_low = hold(
        (acts, qkv_weights, grad_send, second_low, out_low)
    )
    grad_arrived = exchange_all(grad_send)
    out_all = lax.all_gather(out_low, everyone, axis=0, tiled=True)
    second_far = swap(second_low, 4)

    lens = lax.dynamic_slice_in_dim(lengths, chip * seqs, seqs)
    halves = range(2)
    calls = 2 * seqs
    qkvs, mixed_parts, previous = [], [], None
    for s in range(seqs):
        qkvs.append([mm(acts[s], weight).astype(bf16) for weight in qkv_weights])
        for h in halves:
            call = s * 2 + h
            if call > 1:
                n = slice(call - 2, call - 1)
                qkvs[s][h], second_far[n] = hold((qkvs[s][h], second_far[n]))
            if call:
                qkvs[s][h], previous = hold((qkvs[s][h], previous))
            mixed_chip = attention_forward(lens[s : s + 1], qkvs[s][h], full)
            previous = mixed_chip
            if call == calls - 1:
                mixed_chip, grad_arrived, mixed_parts = hold(
                    (mixed_chip, grad_arrived, mixed_parts)
                )
            mixed_chip = mixed_chip.reshape(chips, CORES, span, half // 2)
            mixed_own = lax.dynamic_index_in_dim(mixed_chip, core, 1, keepdims=False)
            mixed_away = lax.dynamic_index_in_dim(mixed_chip, 1 - core, 1, keepdims=False)
            mixed_parts.append(chip_send(jnp.stack([mixed_own, other_core(mixed_away)], axis=1)))
    mixed_parts = [chip_join(found) for found in mixed_parts]

    g_parts = [grad_arrived] + [group_send(grad_arrived, r) for r in range(1, group)]

    out_weight = out_all.reshape(CORES, 2, half // 2, width)
    out_weight = jnp.stack([pick(out_weight, core), pick(out_weight, 1 - core)], axis=1)
    out_weight = out_weight.reshape(width, width)
    hiddens, sents, mixeds = zip(
        *[
            project_norm(
                mixed_parts[2 * s : 2 * s + 2], tokens_four, s, out_weight, gain_two, shift_two
            )
            for s in range(seqs)
        ]
    )
    sents, second_far[2] = hold((sents, second_far[2]))
    arrived = exchange_all(dispatch(targets, sents, slots))

    sents, first_low = hold((sents, first_low))
    first_far = swap(first_low, 2)
    seconds, firsts = [[second_own], second_far], [[first_own], first_far]
    probs = []
    for h in halves:
        for s in range(seqs):
            part, _ = hold((qkvs[s][h], sents))
            probs.append(attention_probs(lens[s : s + 1], part, full))
    g_parts, probs = hold((g_parts, probs))
    activs_own = [grad_activ_pass(part, [second_own]) for part in g_parts]
    g_late, first_far[0] = hold((after(g_parts, activs_own), first_far[0]))
    activs_far = [grad_activ_pass(part, seconds[1]) for part in g_late]
    arrived, activs_own, activs_far, first_own, probs = hold(
        (arrived, activs_own, activs_far, first_own, probs)
    )
    x_parts = [arrived] + [group_send(arrived, r) for r in range(1, group)]
    owns = [hidden_pass(arrived, activs_own[0], firsts[0], f32)]
    x_parts[-1], owns = hold((x_parts[-1], owns))
    for r in range(1, group):
        owns.append(hidden_pass(x_parts[r], activs_own[r], firsts[0], f32))
    fars = [None] * group
    for r in list(range(1, group)) + [0]:
        fars[r] = hidden_pass(
            x_parts[r], activs_far[r], firsts[1], f32 if r == 0 else bf16, owns[r][2]
        )

    def sum_group(terms):
        total = terms[0]
        for r in range(1, group):
            total = total + group_send(terms[r], group - r).astype(f32)
        return total.astype(bf16)

    activ_parts = [[one[0] for one in owns], [one[0] for one in fars]]
    grad_pre_parts = [[one[1] for one in owns], [one[1] for one in fars]]
    grad_sent_rows = sum_group([one[2] for one in fars])
    grad_back = exchange_all(grad_sent_rows)
    grad_sent_rows, activ_parts, grad_pre_parts = hold(
        (grad_sent_rows, activ_parts, grad_pre_parts)
    )

    def send_grad(far, n, parts):
        return sub_send(far[n], experts - 1 - n // parts)

    def own_grads(whole, arriving, parts):
        order = [(experts - 1 - r) * parts + n for r in range(1, experts) for n in range(parts)]
        return assemble(sub, whole, [arriving[n] for n in order])

    cuts = 2
    *second_away, second_whole = expert_grad_pass(
        sub, *activ_parts, g_parts, experts, cuts
    )
    activ_parts, second_away = hold((activ_parts, second_away))
    early = (experts - 1) * cuts // 2
    second_sent = [send_grad(second_away, n, cuts) for n in range(early)]
    by_rows = list(zip(*activ_parts))
    terms = [
        group_send(down_pass(by_rows[r], seconds), group - r) for r in range(1, group)
    ]
    *first_away, first_whole = expert_grad_pass(
        sub, *grad_pre_parts, x_parts, experts, cuts
    )
    own_rows, terms, first_away = hold((by_rows[0], terms, first_away))
    result_rows = down_pass(own_rows, seconds, terms)
    grad_back, second_sent, first_away = hold((grad_back, second_sent, first_away))

    grad_hiddens, branches, grad_mixeds, small_two = zip(
        *[
            project_back(
                targets[s], grad_back, hiddens[s], cotangent_four, s, out_weight, gain_two
            )
            for s in range(seqs)
        ]
    )
    gm_chip = [chip_exchange(part) for part in grad_mixeds]

    own = width // devices
    pairs = n_exp // 2
    exp = lax.axis_index("exp")
    odd = exp % 2
    alike = [
        [e * n_ctx + c for e in range(n_exp) if e % 2 == which for c in range(n_ctx)]
        for which in range(2)
    ]
    tile = width // n_exp
    split = tile % LANES == 0

    def blocks_of(groups):
        if split:
            return split_grad_pass(groups, tile)
        terms = jnp.concatenate(
            [
                weight_grad_pass(lefts, rights).reshape(n_exp, tile, -1)[order]
                for order, lefts, rights in groups
            ],
            axis=2,
        )
        return [terms[:pairs].reshape(width // 2, -1), terms[pairs:].reshape(width // 2, -1)]

    def halve(away, kept):
        return kept, lax.ppermute(away, "exp", [(e, e ^ 1) for e in range(n_exp)])

    def joined(halved):
        total = add_terms(halved)
        return total.reshape(pairs * n_ctx, own, total.shape[1])

    def to_owner(terms):
        got = lax.all_to_all(
            terms, everyone, split_axis=0, concat_axis=0, tiled=True, axis_index_groups=alike
        )
        return got.astype(f32)

    def by_core_cols(got):
        got = jnp.sum(got.reshape(-1, CORES, own, got.shape[2]), axis=0)
        return jnp.transpose(got, (1, 0, 2))

    evens = jnp.arange(pairs, dtype=jnp.int32) * 2
    plain = jnp.concatenate([evens + 1 - odd, evens + odd])
    steps = n_exp // 4
    true_core, true_half, place = plain // (2 * steps), plain // steps % 2, plain % steps
    mixed_order = (true_half * CORES + (true_core + core) % CORES) * steps + place
    gm_chip, result_rows, second_away, first_away = hold(
        (gm_chip, result_rows, second_away, first_away)
    )
    gm_parts = [
        by_core(part[:, 0], other_core(part[:, 1]), axis=1).reshape(full, half) for part in gm_chip
    ]
    returned = exchange_all(result_rows)
    second_sent += [send_grad(second_away, n, cuts) for n in range(early, len(second_away))]

    wo_terms = halve(*blocks_of([(mixed_order, mixeds, branches)]))
    grad_qkvs = [[None, None] for s in range(seqs)]
    found_parts, w_terms, first_sent, previous = [], [], [], None
    call = 0
    for h in halves:
        for s in range(seqs):
            cols = slice(h * half // 2, (h + 1) * half // 2)
            gm_part = gm_parts[s][:, cols]
            if call == 0:
                first_sent = [send_grad(first_away, n, cuts) for n in range(len(first_away))]
            if call:
                gm_part, previous = hold((gm_part, previous))
            if call == calls - 2:
                gm_part, wo_terms = hold((gm_part, wo_terms))
            if call == calls - 1:
                gm_part, returned = hold((gm_part, returned))
            previous = attention_backward(qkvs[s][h], gm_part, probs[call])
            grad_qkvs[s][h] = previous
            call += 1
            if s == seqs - 1:
                terms = blocks_of([(plain, acts, [grad_qkvs[i][h] for i in range(seqs)])])
                previous, terms = hold((grad_qkvs[s][h], terms))
                grad_qkvs[s][h] = previous
                w_terms.append(halve(*terms))
            if h == 1:
                if call == calls - 1:
                    grad_qkvs[s][h], w_terms[0], second_sent, first_sent[0] = hold(
                        (grad_qkvs[s][h], w_terms[0], second_sent, first_sent[0])
                    )
                if call == calls:
                    grad_qkvs[s][h], found_parts = hold((grad_qkvs[s][h], found_parts))
                away, kept = grad_act_pass(core, grad_qkvs[s], qkv_weights, chips)
                previous, kept = hold((previous, kept))
                total = (kept.astype(f32) + other_core(away).astype(f32)).astype(bf16)
                if call == calls:
                    w_terms[1], returned, first_whole, found_parts = (
                        after(value, total)
                        for value in (w_terms[1], returned, first_whole, found_parts)
                    )
                found_parts.append(chip_send(total))
                grad_qkvs[s][h] = previous
    second_whole = after(second_whole, previous)
    value = joined([w_terms[1]])
    columns = value.shape[2]
    first = True
    upper_bits = [b for b in (2, 4, 8, 16) if b < n_exp]
    axes = [("exp", b) for b in upper_bits[::-1]] + [("ctx", b) for b in chip_bits[::-1]]
    value = value.reshape((2,) * len(axes) + (CORES, own, columns))
    for step in [("exp", b) for b in upper_bits] + axes[len(upper_bits) :]:
        axis, bit = step
        at = axes.index(step)
        index = exp if axis == "exp" else chip
        upper = jnp.where((index & bit) != 0, 1, 0)
        kept = lax.dynamic_index_in_dim(value, upper, at, keepdims=False)
        away = lax.dynamic_index_in_dim(value, 1 - upper, at, keepdims=False)
        if axis == "exp":
            other = lax.ppermute(away, "exp", [(e, e ^ bit) for e in range(n_exp)])
        else:
            other = ctx_send(away, lambda c: c ^ (bit * CORES))
        if first:
            other, found_parts[-1], first_sent[1:] = hold(
                (other, found_parts[-1], first_sent[1:])
            )
            first = False
        value = (kept.astype(f32) + other.astype(f32)).astype(bf16)
        axes.remove(step)
    second_sum = by_core(
        pick(value, core), other_core(pick(value, 1 - core)), axis=1
    ).astype(f32)
    grad_tokens, small_one = None, []
    for s in range(seqs):
        grad_tokens, sums = finish(
            chip, found_parts[s], tokens_four, grad_hiddens[s], gain_one, s, grad_tokens
        )
        small_one.append(sums)
    small_one = sum(small_one)
    grad_tokens = grad_tokens.reshape(tokens.shape)
    grad_expert_out = own_grads(second_whole, second_sent, cuts)
    grad_expert_in = own_grads(first_whole, first_sent, cuts)
    first_sum = to_owner(joined([w_terms[0], wo_terms]))
    grad_output = jnp.sum(first_sum[:, :, parts:], axis=0)
    grad_w = jnp.concatenate([by_core_cols(first_sum[:, :, :parts]), second_sum], axis=2)
    grad_w = grad_w.reshape(own, width // LANES, 3, LANES)
    grad_query, grad_key, grad_value = (grad_w[:, :, t].reshape(own, width) for t in range(3))

    block_out = None
    for s in range(seqs):
        block_out = combine(
            targets[s], returned, hiddens[s], tokens_four.shape, s, block_out
        )
    block_out = block_out.reshape(tokens.shape)
    small_two = sum(small_two)
    small = jnp.stack(
        [
            value.reshape(devices, own)
            for value in (small_one[0], small_one[1], small_two[0], small_two[1])
        ],
        axis=1,
    )
    small = jnp.sum(exchange_all(small), axis=0)
    return (
        block_out,
        grad_tokens,
        grad_query,
        grad_key,
        grad_value,
        grad_output,
        small[0],
        small[1],
        small[2],
        small[3],
        grad_expert_in,
        grad_expert_out,
    )


def solution(mesh):
    rows = P("exp", "ctx", None)
    weight = P(("exp", "ctx"), None)
    vector = P(("exp", "ctx"))
    return jax.shard_map(
        body,
        mesh=mesh,
        in_specs=(
            rows,
            P("exp"),
            P("ctx", "exp", None, None),
            rows,
            weight,
            weight,
            weight,
            weight,
            P(),
            P(),
            P(),
            P(),
            rows,
            rows,
        ),
        out_specs=(rows, rows, weight, weight, weight, weight)
        + (vector, vector, vector, vector)
        + (rows, rows),
        check_vma=False,
    )
```

```python
import functools

import jax
import jax.numpy as jnp
from jax import lax
from jax.experimental import pallas as pl
from jax.experimental.pallas import tpu as pltpu
from jax.sharding import PartitionSpec as P

HEAD_DIM = 64
LANES = 128
PAIR = 3 * LANES
BLOCK = 256
LOG2E = 1.4426950408889634
CORES = 2

eps_norm = 1e-05
masked_score = -1e30
f32 = jnp.float32
bf16 = jnp.bfloat16
NN = (((1,), (0,)), ((), ()))
NT = (((1,), (1,)), ((), ()))
TN = (((0,), (0,)), ((), ()))
VMEM_LIMIT = 56 * 1024 * 1024
PARAMS = pltpu.CompilerParams(vmem_limit_bytes=VMEM_LIMIT)


def cost(flops):
    return pl.CostEstimate(flops=int(flops / 10), bytes_accessed=1024, transcendentals=0)


hold = lax.optimization_barrier


def after(value, *others):
    return hold((value, others))[0]


def mm(a, b, dims=NN):
    return lax.dot_general(a, b, dims, preferred_element_type=f32)


def head_operands(length, q, k):
    full = q.shape[0]
    lane = lax.broadcasted_iota(jnp.int32, (full, LANES), 1)
    pos = lax.broadcasted_iota(jnp.int32, (full, LANES), 0)
    bias = jnp.where(pos < length, 0.0, masked_score).astype(f32)
    inside, q_aug, k_aug = [], [], []
    for head in range(2):
        own = (lane // HEAD_DIM) == head
        spare = lane == HEAD_DIM * (1 - head)
        inside.append(own)
        q_aug.append(jnp.where(own, q, jnp.where(spare, 1.0, 0.0)).astype(bf16))
        k_aug.append(jnp.where(own, k, jnp.where(spare, bias, 0.0)).astype(bf16))
    return inside, q_aug, k_aug


def attention_forward_kernel(len_ref, x_ref, o_ref):
    full = x_ref.shape[0]
    q, k, v = (x_ref[:, LANES * t : LANES * (t + 1)].astype(f32) for t in range(3))
    inside, q_aug, k_aug = head_operands(len_ref[pl.program_id(0)], q, k)
    v_own = [jnp.where(own, v, 0.0).astype(bf16) for own in inside]
    to_log2 = HEAD_DIM**-0.5 * LOG2E
    row = lax.broadcasted_iota(jnp.int32, (BLOCK, BLOCK), 0)
    col = lax.broadcasted_iota(jnp.int32, (BLOCK, BLOCK), 1)
    causal = col <= row
    for i in range(full // BLOCK):
        here, before = slice(i * BLOCK, (i + 1) * BLOCK), slice(0, i * BLOCK)
        total = jnp.zeros((BLOCK, LANES), f32)
        for head in range(2):
            qi = q_aug[head][here]
            s_here = jnp.where(causal, mm(qi, k_aug[head][here], NT) * to_log2, masked_score)
            top = jnp.max(s_here, axis=1, keepdims=True)
            if i:
                s_before = mm(qi, k_aug[head][before], NT) * to_log2
                top = jnp.maximum(top, jnp.max(s_before, axis=1, keepdims=True))
            p_here = jnp.exp2(s_here - top)
            mass = jnp.sum(p_here, axis=1, keepdims=True)
            if i:
                p_before = jnp.exp2(s_before - top)
                mass = mass + jnp.sum(p_before, axis=1, keepdims=True)
            inverse = 1.0 / mass
            total = total + mm((p_here * inverse).astype(bf16), v_own[head][here])
            if i:
                total = total + mm((p_before * inverse).astype(bf16), v_own[head][before])
        o_ref[here, :] = total.astype(bf16)


def attention_forward(lens, qkv, full):
    n_seq, pairs = qkv.shape[0] // full, qkv.shape[1] // PAIR
    return pl.pallas_call(
        attention_forward_kernel,
        grid_spec=pltpu.PrefetchScalarGridSpec(
            num_scalar_prefetch=1,
            grid=(n_seq, pairs),
            in_specs=[pl.BlockSpec((full, PAIR), lambda s, p, l: (s, p))],
            out_specs=pl.BlockSpec((full, LANES), lambda s, p, l: (s, p)),
        ),
        out_shape=jax.ShapeDtypeStruct((n_seq * full, pairs * LANES), bf16),
        compiler_params=PARAMS,
        cost_estimate=cost(n_seq * pairs * 2.5e9),
        name="attention_forward",
    )(lens, qkv)


def attention_probs_kernel(len_ref, x_ref, p_ref):
    full = x_ref.shape[0]
    q, k = (x_ref[:, LANES * t : LANES * (t + 1)].astype(f32) for t in range(2))
    _, q_aug, k_aug = head_operands(len_ref[pl.program_id(0)], q, k)
    to_log2 = HEAD_DIM**-0.5 * LOG2E
    row = lax.broadcasted_iota(jnp.int32, (BLOCK, BLOCK), 0)
    col = lax.broadcasted_iota(jnp.int32, (BLOCK, BLOCK), 1)
    causal = row <= col
    for i in range(full // BLOCK):
        here, before = slice(i * BLOCK, (i + 1) * BLOCK), slice(0, i * BLOCK)
        for head in range(2):
            qi = q_aug[head][here]
            s_here = jnp.where(causal, mm(k_aug[head][here], qi, NT) * to_log2, masked_score)
            top = jnp.max(s_here, axis=0, keepdims=True)
            if i:
                s_before = mm(k_aug[head][before], qi, NT) * to_log2
                top = jnp.maximum(top, jnp.max(s_before, axis=0, keepdims=True))
            p_here = jnp.exp2(s_here - top)
            mass = jnp.sum(p_here, axis=0, keepdims=True)
            if i:
                p_before = jnp.exp2(s_before - top)
                mass = mass + jnp.sum(p_before, axis=0, keepdims=True)
            inverse = 1.0 / mass
            p_ref[head, here, here] = (p_here * inverse).astype(bf16)
            if i:
                p_ref[head, before, here] = (p_before * inverse).astype(bf16)


def attention_probs(lens, qkv, full):
    n_seq, pairs = qkv.shape[0] // full, qkv.shape[1] // PAIR
    return pl.pallas_call(
        attention_probs_kernel,
        grid_spec=pltpu.PrefetchScalarGridSpec(
            num_scalar_prefetch=1,
            grid=(n_seq, pairs),
            in_specs=[pl.BlockSpec((full, PAIR), lambda s, p, l: (s, p))],
            out_specs=pl.BlockSpec((2, full, full), lambda s, p, l: (s * pairs + p, 0, 0)),
        ),
        out_shape=jax.ShapeDtypeStruct((n_seq * pairs * 2, full, full), bf16),
        compiler_params=PARAMS,
        cost_estimate=cost(n_seq * pairs * 2.0e9),
        name="attention_probs",
    )(lens, qkv)


def attention_backward_kernel(x_ref, g_ref, p_ref, o_ref, d_scr):
    full = x_ref.shape[0]
    q, k = (x_ref[:, LANES * t : LANES * (t + 1)].astype(f32) for t in range(2))
    v = x_ref[:, 2 * LANES : 3 * LANES]
    g = g_ref[...].astype(f32)
    head_of = lax.broadcasted_iota(jnp.int32, (full, LANES), 1) // HEAD_DIM
    inside = [head_of == head for head in range(2)]
    q_own = [jnp.where(own, q, 0.0).astype(bf16) for own in inside]
    k_own = [jnp.where(own, k, 0.0).astype(bf16) for own in inside]
    g_own = [jnp.where(own, g, 0.0).astype(bf16) for own in inside]
    scale = HEAD_DIM**-0.5
    count = full // BLOCK
    for i in range(count):
        here, until = slice(i * BLOCK, (i + 1) * BLOCK), slice(0, (i + 1) * BLOCK)
        dq = jnp.zeros((BLOCK, LANES), f32)
        for head in range(2):
            probs = p_ref[head, until, here].astype(f32)
            grad = mm(v[until], g_own[head][here], NT)
            delta = jnp.sum(grad * probs, axis=0, keepdims=True)
            d_score = (probs * (grad - delta)).astype(bf16)
            d_scr[head, until, here] = d_score
            dq = dq + mm(d_score, k_own[head][until], TN)
        o_ref[here, 0:LANES] = (dq * scale).astype(bf16)
    for j in range(count):
        here, after_ = slice(j * BLOCK, (j + 1) * BLOCK), slice(j * BLOCK, full)
        dk = mm(d_scr[0, here, after_], q_own[0][after_]) + mm(
            d_scr[1, here, after_], q_own[1][after_]
        )
        dv = mm(p_ref[0, here, after_], g_own[0][after_]) + mm(
            p_ref[1, here, after_], g_own[1][after_]
        )
        o_ref[here, LANES : 2 * LANES] = (dk * scale).astype(bf16)
        o_ref[here, 2 * LANES : 3 * LANES] = dv.astype(bf16)


def attention_backward(qkv, g, probs):
    full = probs.shape[1]
    n_seq, pairs = qkv.shape[0] // full, qkv.shape[1] // PAIR
    return pl.pallas_call(
        attention_backward_kernel,
        grid=(n_seq, pairs),
        in_specs=[
            pl.BlockSpec((full, PAIR), lambda s, p: (s, p)),
            pl.BlockSpec((full, LANES), lambda s, p: (s, p)),
            pl.BlockSpec((2, full, full), lambda s, p: (s * pairs + p, 0, 0)),
        ],
        out_specs=pl.BlockSpec((full, PAIR), lambda s, p: (s, p)),
        scratch_shapes=[pltpu.VMEM((2, full, full), bf16)],
        out_shape=jax.ShapeDtypeStruct(qkv.shape, bf16),
        compiler_params=PARAMS,
        cost_estimate=cost(n_seq * pairs * 3.0e9),
        name="attention_backward",
    )(qkv, g, probs)


def tile_of(count, most=320):
    return max(t for t in range(16, most + 1, 16) if count % t == 0)


def pieces_of(shards):
    start = 0
    for ref in shards:
        size = min(512, ref.shape[0])
        for h in range(0, ref.shape[0], size):
            yield ref, slice(h, h + size), slice(start, start + size)
            start += size


def shard_specs(shards):
    return [pl.BlockSpec(w.shape, lambda i: (0, 0)) for w in shards]


def hidden_of(shards):
    return sum(w.shape[0] for w in shards)


def grad_activ_kernel(g_ref, *refs):
    for w_ref, part, cols in pieces_of(refs[:-1]):
        refs[-1][:, cols] = mm(g_ref[...], w_ref[part, :], NT).astype(bf16)


def grad_activ_pass(g, shards):
    (count, width), hidden = g.shape, hidden_of(shards)
    tile = tile_of(count)
    return pl.pallas_call(
        grad_activ_kernel,
        grid=(count // tile,),
        in_specs=[pl.BlockSpec((tile, width), lambda i: (i, 0))] + shard_specs(shards),
        out_specs=pl.BlockSpec((tile, hidden), lambda i: (i, 0)),
        out_shape=jax.ShapeDtypeStruct((count, hidden), bf16),
        compiler_params=PARAMS,
        cost_estimate=cost(count * hidden * width / 2),
        name="grad_activ_pass",
    )(g, *shards)


def hidden_kernel(x_ref, ga_ref, *refs, before):
    shards, (a_ref, gp_ref, gs_ref) = refs[before:-3], refs[-3:]
    for w_ref, part, cols in pieces_of(shards):
        activ, slope = gelu_parts(mm(x_ref[...], w_ref[part, :], NT))
        a_ref[:, cols] = activ.astype(bf16)
        gp_ref[:, cols] = (ga_ref[:, cols].astype(f32) * slope).astype(bf16)
    total = product_of(gp_ref, shards)
    if before:
        total = total + refs[0][...].astype(f32)
    gs_ref[...] = total.astype(gs_ref.dtype)


def product_of(rows_ref, shards):
    total, start = None, 0
    for w_ref in shards:
        cols = slice(start, start + w_ref.shape[0])
        part = mm(rows_ref[:, cols], w_ref[...])
        total = part if total is None else total + part
        start += w_ref.shape[0]
    return total


def hidden_pass(x, grad_activ, shards, dtype, before=None):
    (count, width), hidden = x.shape, hidden_of(shards)
    tile = tile_of(count)
    wide = pl.BlockSpec((tile, hidden), lambda i: (i, 0))
    thin = pl.BlockSpec((tile, width), lambda i: (i, 0))
    more = [] if before is None else [before]
    return pl.pallas_call(
        functools.partial(hidden_kernel, before=len(more)),
        grid=(count // tile,),
        in_specs=[thin, wide] + [thin] * len(more) + shard_specs(shards),
        out_specs=[wide, wide, thin],
        out_shape=[jax.ShapeDtypeStruct((count, hidden), bf16)] * 2
        + [jax.ShapeDtypeStruct((count, width), dtype)],
        compiler_params=PARAMS,
        cost_estimate=cost(2 * count * hidden * width),
        name="hidden_pass",
    )(x, grad_activ, *more, *shards)


def down_kernel(*refs, own, more):
    last = len(refs) - 1 - more
    total = product_of(refs[0], refs[2 : 2 + own]) + product_of(refs[1], refs[2 + own : last])
    for term in refs[last:-1]:
        total = total + term[...].astype(f32)
    refs[-1][...] = total.astype(bf16)


def down_pass(activs, groups, terms=()):
    count, width = activs[0].shape[0], groups[0][0].shape[1]
    tile = tile_of(count)
    shards = list(groups[0]) + list(groups[1])
    return pl.pallas_call(
        functools.partial(down_kernel, own=len(groups[0]), more=len(terms)),
        grid=(count // tile,),
        in_specs=[pl.BlockSpec((tile, a.shape[1]), lambda i: (i, 0)) for a in activs]
        + shard_specs(shards)
        + [pl.BlockSpec((tile, width), lambda i: (i, 0)) for _ in terms],
        out_specs=pl.BlockSpec((tile, width), lambda i: (i, 0)),
        out_shape=jax.ShapeDtypeStruct((count, width), bf16),
        compiler_params=PARAMS,
        cost_estimate=cost(2 * count * hidden_of(shards) * width),
        name="down_pass",
    )(*activs, *shards, *terms)


def summed(lefts, rights):
    total = mm(lefts[0][...], rights[0][...], TN)
    for left, right in zip(lefts[1:], rights[1:]):
        total = total + mm(left[...], right[...], TN)
    return total


def weight_grad_kernel(*refs):
    count = len(refs) // 2
    refs[-1][...] = summed(refs[:count], refs[count:-1]).astype(bf16)


def weight_grad_pass(lefts, rights):
    hidden, width = lefts[0].shape[1], rights[0].shape[1]
    tile = min(256, hidden)
    return pl.pallas_call(
        weight_grad_kernel,
        grid=(hidden // tile,),
        in_specs=[pl.BlockSpec((v.shape[0], tile), lambda i: (0, i)) for v in lefts]
        + [pl.BlockSpec(v.shape, lambda i: (0, 0)) for v in rights],
        out_specs=pl.BlockSpec((tile, width), lambda i: (i, 0)),
        out_shape=jax.ShapeDtypeStruct((hidden, width), bf16),
        compiler_params=PARAMS,
        cost_estimate=cost(2 * lefts[0].size * width * len(lefts)),
        name="weight_grad_pass",
    )(*lefts, *rights)


def split_grad_kernel(order_ref, *refs, tile, counts):
    values, start, col = refs[:-2], 0, 0
    steps = order_ref.shape[0] // len(counts)
    totals = []
    for group, count in enumerate(counts):
        lefts, rights = values[start : start + count], values[start + count : start + 2 * count]
        first = group * steps + pl.program_id(0) * (steps // 2)
        places = [order_ref[first + n] for n in range(steps // 2)]
        total = None
        for left, right in zip(lefts, rights):
            chosen = jnp.concatenate(
                [left[:, pl.ds(pl.multiple_of(place * tile, tile), tile)] for place in places],
                axis=1,
            )
            part = mm(chosen, right[...], TN)
            total = part if total is None else total + part
        totals.append((slice(col, col + total.shape[1]), total.astype(bf16)))
        start += 2 * count
        col += total.shape[1]

    for which in range(2):

        @pl.when(pl.program_id(0) == which)
        def _(which=which):
            for cols, total in totals:
                refs[which - 2][:, cols] = total


def split_grad_pass(groups, tile):
    hidden = groups[0][1][0].shape[1]
    width = sum(rights[0].shape[1] for _, _, rights in groups)
    values = [v for _, lefts, rights in groups for v in (*lefts, *rights)]
    out = jax.ShapeDtypeStruct((hidden // 2, width), bf16)
    return pl.pallas_call(
        functools.partial(split_grad_kernel, tile=tile, counts=[len(g[1]) for g in groups]),
        grid_spec=pltpu.PrefetchScalarGridSpec(
            num_scalar_prefetch=1,
            grid=(2,),
            in_specs=[pl.BlockSpec(v.shape, lambda i, o: (0, 0)) for v in values],
            out_specs=[pl.BlockSpec(out.shape, lambda i, o: (0, 0))] * 2,
        ),
        out_shape=[out, out],
        compiler_params=PARAMS,
        cost_estimate=cost(2 * width * sum(v.size for v in groups[0][1])),
        name="split_grad_pass",
    )(jnp.concatenate([order for order, _, _ in groups]), *values)


def add_terms_kernel(*refs):
    col = 0
    for one, two in zip(refs[0:-1:2], refs[1:-1:2]):
        cols = slice(col, col + one.shape[1])
        refs[-1][:, cols] = (one[...].astype(f32) + two[...].astype(f32)).astype(bf16)
        col = cols.stop


def add_terms(pairs):
    count = pairs[0][0].shape[0]
    tile = min(128, count)
    values = [v for pair in pairs for v in pair]
    width = sum(pair[0].shape[1] for pair in pairs)
    return pl.pallas_call(
        add_terms_kernel,
        grid=(count // tile,),
        in_specs=[pl.BlockSpec((tile, v.shape[1]), lambda i: (i, 0)) for v in values],
        out_specs=pl.BlockSpec((tile, width), lambda i: (i, 0)),
        out_shape=jax.ShapeDtypeStruct((count, width), bf16),
        compiler_params=PARAMS,
        cost_estimate=cost(3.0e10),
        name="add_terms",
    )(*values)


def expert_grad_kernel(sub_ref, *refs, count, pieces, per):
    step = pl.program_id(0)
    rights = refs[2 * count : 3 * count]

    @pl.when(step < pieces * per)
    def _():
        total = summed(refs[count : 2 * count], rights).astype(bf16)
        for n in range(pieces):

            @pl.when((step >= n * per) & (step < (n + 1) * per))
            def _(n=n):
                refs[3 * count + n][...] = total

    @pl.when(step >= pieces * per)
    def _():
        refs[-1][0] = summed(refs[:count], rights)


def expert_grad_pass(sub, owns, others, rights, experts, parts):
    shard, width = owns[0].shape[1], rights[0].shape[1]
    tile = min(256, shard // parts)
    pieces, per, own = (experts - 1) * parts, shard // parts // tile, shard // tile
    far = pieces * per

    def piece_spec(n):
        return pl.BlockSpec((tile, width), lambda i, s: (jnp.clip(i - n * per, 0, per - 1), 0))

    return pl.pallas_call(
        functools.partial(expert_grad_kernel, count=len(owns), pieces=pieces, per=per),
        grid_spec=pltpu.PrefetchScalarGridSpec(
            num_scalar_prefetch=1,
            grid=(far + own,),
            in_specs=[
                pl.BlockSpec((v.shape[0], tile), lambda i, s: (0, jnp.clip(i - far, 0, own - 1)))
                for v in owns
            ]
            + [
                pl.BlockSpec((v.shape[0], tile), lambda i, s: (0, jnp.clip(i, 0, far - 1)))
                for v in others
            ]
            + [pl.BlockSpec(v.shape, lambda i, s: (0, 0)) for v in rights],
            out_specs=[piece_spec(n) for n in range(pieces)]
            + [
                pl.BlockSpec(
                    (1, tile, width), lambda i, s: (s[0], jnp.clip(i - far, 0, own - 1), 0)
                )
            ],
        ),
        out_shape=[jax.ShapeDtypeStruct((shard // parts, width), bf16)] * pieces
        + [jax.ShapeDtypeStruct((experts, shard, width), f32)],
        compiler_params=PARAMS,
        cost_estimate=cost(2 * experts * owns[0].size * width * len(owns)),
        name="expert_grad_pass",
    )(sub.reshape(1), *owns, *others, *rights)


def assemble_kernel(sub_ref, whole_ref, *refs):
    pieces, o_ref = refs[:-1], refs[-1]
    for n, piece in enumerate(pieces):

        @pl.when(pl.program_id(0) * pl.num_programs(1) + pl.program_id(1) == n)
        def _(piece=piece):
            o_ref[0] = piece[...].astype(f32)


def assemble(sub, whole, pieces):
    experts = whole.shape[0]
    parts = len(pieces) // (experts - 1)
    cut, width = pieces[0].shape

    def place(r, n, s):
        return (lax.rem(s[0] - r - 1 + experts, experts), n, 0)

    return pl.pallas_call(
        assemble_kernel,
        grid_spec=pltpu.PrefetchScalarGridSpec(
            num_scalar_prefetch=1,
            grid=(experts - 1, parts),
            in_specs=[pl.BlockSpec(memory_space=pl.ANY)]
            + [pl.BlockSpec((cut, width), lambda r, n, s: (0, 0)) for _ in pieces],
            out_specs=pl.BlockSpec((1, cut, width), place),
        ),
        out_shape=jax.ShapeDtypeStruct(whole.shape, f32),
        input_output_aliases={1: 0},
        compiler_params=PARAMS,
        cost_estimate=cost(3.0e10),
        name="assemble",
    )(sub.reshape(1), whole, *pieces)


def gelu_parts(pre):
    outer, inner = 0.7978845608028654, 0.044715
    square = pre * pre
    half = 0.5 + 0.5 * jnp.tanh(pre * (outer + outer * inner * square))
    value = pre * half
    slope = half + value * (1.0 - half) * (2.0 * outer + 6.0 * outer * inner * square)
    return value, slope


def dispatch_kernel(*refs):
    o_ref, count = refs[-1], len(refs) // 2
    tile = o_ref.shape[0]
    total = None
    for t_ref, v_ref in zip(refs[:count], refs[count:-1]):
        rows = v_ref.shape[0]
        slot = lax.broadcasted_iota(jnp.int32, (tile, rows), 0) + pl.program_id(0) * tile
        chosen = jnp.where(t_ref[...] == slot, 1.0, 0.0).astype(bf16)
        part = mm(chosen, v_ref[...])
        total = part if total is None else total + part
    o_ref[...] = total.astype(bf16)


def dispatch(targets, values, slots):
    tile, width = tile_of(slots), values[0].shape[1]
    return pl.pallas_call(
        dispatch_kernel,
        grid=(slots // tile,),
        in_specs=[pl.BlockSpec((1, v.shape[0]), lambda i: (0, 0)) for v in values]
        + [pl.BlockSpec(v.shape, lambda i: (0, 0)) for v in values],
        out_specs=pl.BlockSpec((tile, width), lambda i: (i, 0)),
        out_shape=jax.ShapeDtypeStruct((slots, width), bf16),
        compiler_params=PARAMS,
        cost_estimate=cost(2 * slots * width * sum(v.shape[0] for v in values)),
        name="dispatch",
    )(*[t.reshape(1, -1) for t in targets], *values)


def returned_rows(target, rows_ref):
    slots = rows_ref.shape[0]
    slot = lax.broadcasted_iota(jnp.int32, (target.shape[0], slots), 1)
    return mm(jnp.where(target == slot, 1.0, 0.0).astype(bf16), rows_ref[...])


def combine_kernel(t_ref, rows_ref, h_ref, *refs):
    refs[-1][0, 0] = (h_ref[...] + returned_rows(t_ref[...], rows_ref)).astype(bf16)


def into_whole(whole, place):
    if whole is None:
        return [], [], {}
    return [pl.BlockSpec(memory_space=pl.ANY)], [whole], {place: 0}


def combine(target, rows, hidden, shape, seq, whole):
    chips, _, span, width = shape
    specs, arrays, aliases = into_whole(whole, 3)
    return pl.pallas_call(
        combine_kernel,
        grid=(chips,),
        in_specs=[
            pl.BlockSpec((span, 1), lambda j: (j, 0)),
            pl.BlockSpec(rows.shape, lambda j: (0, 0)),
            pl.BlockSpec((span, width), lambda j: (j, 0)),
        ]
        + specs,
        out_specs=pl.BlockSpec((1, 1, span, width), lambda j: (j, seq, 0, 0)),
        out_shape=jax.ShapeDtypeStruct(shape, bf16),
        input_output_aliases=aliases,
        compiler_params=PARAMS,
        cost_estimate=cost(20 * chips * span * width * rows.shape[0]),
        name="combine",
    )(target.reshape(-1, 1), rows, hidden, *arrays)


def project_kernel(a_ref, b_ref, t_ref, w_ref, gain_ref, shift_ref, h_ref, s_ref, m_ref):
    mixed = jnp.concatenate([a_ref[0, 0], a_ref[0, 1], b_ref[0, 0], b_ref[0, 1]], axis=1)
    m_ref[...] = mixed
    hidden = t_ref[0, 0].astype(f32) + mm(mixed, w_ref[...])
    h_ref[...] = hidden
    normal, _ = norm_parts(hidden)
    s_ref[...] = (normal * gain_ref[...] + shift_ref[...]).astype(bf16)


def project_norm(parts, tokens, seq, weight, gain, shift):
    chips, cores, span, cols = parts[0].shape
    width = tokens.shape[3]
    block = pl.BlockSpec((1, cores, span, cols), lambda j: (j, 0, 0, 0))
    row = pl.BlockSpec((1, width), lambda j: (0, 0))
    out = pl.BlockSpec((span, width), lambda j: (j, 0))
    return pl.pallas_call(
        project_kernel,
        grid=(chips,),
        in_specs=[
            block,
            block,
            pl.BlockSpec((1, 1, span, width), lambda j: (j, seq, 0, 0)),
            pl.BlockSpec((width, width), lambda j: (0, 0)),
            row,
            row,
        ],
        out_specs=[out] * 3,
        out_shape=[
            jax.ShapeDtypeStruct((chips * span, width), dtype) for dtype in (f32, bf16, bf16)
        ],
        compiler_params=PARAMS,
        cost_estimate=cost(2 * chips * span * width * width),
        name="project_norm",
    )(*parts, tokens, weight, gain.reshape(1, -1), shift.reshape(1, -1))


def project_back_kernel(
    t_ref, rows_ref, h_ref, c_ref, w_ref, gain_ref, gh_ref, gb_ref, gm_ref, small_ref
):
    grad = returned_rows(t_ref[...], rows_ref)
    normal, inverse = norm_parts(h_ref[...])
    grad_hidden = c_ref[0, 0].astype(f32) + norm_back(grad, normal, inverse, gain_ref[...])
    gh_ref[...] = grad_hidden
    branch = grad_hidden.astype(bf16)
    gb_ref[...] = branch
    mixed = mm(branch, w_ref[...], NT).astype(bf16)
    cols = gm_ref.shape[3] // 2
    for half in range(2):
        for k in range(CORES):
            at = (half * CORES + k) * cols
            gm_ref[0, k, :, half * cols : (half + 1) * cols] = mixed[:, at : at + cols]
    sums = jnp.concatenate(
        [
            jnp.sum(grad * normal, axis=0, keepdims=True),
            jnp.sum(grad, axis=0, keepdims=True),
        ],
        axis=0,
    )

    @pl.when(pl.program_id(0) == 0)
    def _():
        small_ref[...] = sums

    @pl.when(pl.program_id(0) > 0)
    def _():
        small_ref[...] += sums


def project_back(target, rows, hidden, cotangent, seq, weight, gain):
    chips, _, span, width = cotangent.shape
    out = pl.BlockSpec((span, width), lambda j: (j, 0))
    return pl.pallas_call(
        project_back_kernel,
        grid=(chips,),
        in_specs=[
            pl.BlockSpec((span, 1), lambda j: (j, 0)),
            pl.BlockSpec(rows.shape, lambda j: (0, 0)),
            out,
            pl.BlockSpec((1, 1, span, width), lambda j: (j, seq, 0, 0)),
            pl.BlockSpec((width, width), lambda j: (0, 0)),
            pl.BlockSpec((1, width), lambda j: (0, 0)),
        ],
        out_specs=[
            out,
            out,
            pl.BlockSpec((1, CORES, span, width // CORES), lambda j: (j, 0, 0, 0)),
            pl.BlockSpec((2, width), lambda j: (0, 0)),
        ],
        out_shape=[
            jax.ShapeDtypeStruct((chips * span, width), f32),
            jax.ShapeDtypeStruct((chips * span, width), bf16),
            jax.ShapeDtypeStruct((chips, CORES, span, width // CORES), bf16),
            jax.ShapeDtypeStruct((2, width), f32),
        ],
        compiler_params=PARAMS,
        cost_estimate=cost(6 * chips * span * width * width),
        name="project_back",
    )(target.reshape(-1, 1), rows, hidden, cotangent, weight, gain.reshape(1, -1))


def grad_act_kernel(core_ref, *refs):
    count = (len(refs) - 2) // 2
    total = None
    for d_ref, w_ref in zip(refs[:count], refs[count:-2]):
        part = mm(d_ref[...], w_ref[...], NT)
        total = part if total is None else total + part
    for which in range(2):

        @pl.when(pl.program_id(0) == which)
        def _(which=which):
            refs[which - 2][0] = total.astype(bf16)


def grad_act_pass(core, grads, weights, chips):
    width = weights[0].shape[0]
    span = grads[0].shape[0] // (chips * CORES)
    out = jax.ShapeDtypeStruct((chips, span, width), bf16)

    def rows(which, j, c):
        return (j * CORES + jnp.where(which == 0, 1 - c[0], c[0]), 0)

    return pl.pallas_call(
        grad_act_kernel,
        grid_spec=pltpu.PrefetchScalarGridSpec(
            num_scalar_prefetch=1,
            grid=(2, chips),
            in_specs=[pl.BlockSpec((span, g.shape[1]), rows) for g in grads]
            + [pl.BlockSpec(w.shape, lambda which, j, c: (0, 0)) for w in weights],
            out_specs=[
                pl.BlockSpec(
                    (1, span, width), lambda which, j, c: (jnp.where(which == 0, j, chips - 1), 0, 0)
                ),
                pl.BlockSpec(
                    (1, span, width), lambda which, j, c: (jnp.where(which == 1, j, 0), 0, 0)
                ),
            ],
        ),
        out_shape=[out, out],
        compiler_params=PARAMS,
        cost_estimate=cost(2 * sum(g.size for g in grads) * width),
        name="grad_act_pass",
    )(core.reshape(1), *grads, *weights)


def finish_kernel(chip_ref, *refs, chips):
    found, (t_ref, gh_ref, gain_ref) = refs[:chips], refs[chips : chips + 3]
    o_ref, small_ref, grad_ref = refs[-3:]
    step = pl.program_id(0)
    place = lax.rem(chip_ref[0] - step + chips, chips)
    for n, part in enumerate(found):

        @pl.when(place == n)
        def _(part=part):
            grad_ref[...] = part[...].astype(f32)

    grad = grad_ref[...]
    normal, inverse = norm_parts(t_ref[0, 0].astype(f32))
    o_ref[0, 0] = (gh_ref[...] + norm_back(grad, normal, inverse, gain_ref[...])).astype(bf16)
    sums = jnp.concatenate(
        [
            jnp.sum(grad * normal, axis=0, keepdims=True),
            jnp.sum(grad, axis=0, keepdims=True),
        ],
        axis=0,
    )

    @pl.when(step == 0)
    def _():
        small_ref[...] = sums

    @pl.when(step > 0)
    def _():
        small_ref[...] += sums


def finish(chip, found, tokens, grad_hidden, gain, seq, whole):
    chips, _, span, width = tokens.shape
    specs, arrays, aliases = into_whole(whole, chips + 4)
    return pl.pallas_call(
        functools.partial(finish_kernel, chips=chips),
        grid_spec=pltpu.PrefetchScalarGridSpec(
            num_scalar_prefetch=1,
            grid=(chips,),
            in_specs=[pl.BlockSpec((span, width), lambda j, c: (0, 0)) for _ in found]
            + [
                pl.BlockSpec((1, 1, span, width), lambda j, c: (j, seq, 0, 0)),
                pl.BlockSpec((span, width), lambda j, c: (j, 0)),
                pl.BlockSpec((1, width), lambda j, c: (0, 0)),
            ]
            + specs,
            out_specs=[
                pl.BlockSpec((1, 1, span, width), lambda j, c: (j, seq, 0, 0)),
                pl.BlockSpec((2, width), lambda j, c: (0, 0)),
            ],
            scratch_shapes=[pltpu.VMEM((span, width), f32)],
        ),
        out_shape=[
            jax.ShapeDtypeStruct(tokens.shape, bf16),
            jax.ShapeDtypeStruct((2, width), f32),
        ],
        input_output_aliases=aliases,
        compiler_params=PARAMS,
        cost_estimate=cost(2.0e10),
        name="finish",
    )(chip.reshape(1), *found, tokens, grad_hidden, gain.reshape(1, -1), *arrays)


def norm_parts(values):
    average = jnp.mean(values, axis=-1, keepdims=True)
    centered = values - average
    variance = jnp.mean(centered * centered, axis=-1, keepdims=True)
    inverse = lax.rsqrt(variance + eps_norm)
    return centered * inverse, inverse


def norm_back(grad, normal, inverse, gain):
    inner = grad * gain
    mean_one = jnp.mean(inner, axis=-1, keepdims=True)
    mean_two = jnp.mean(inner * normal, axis=-1, keepdims=True)
    return inverse * (inner - mean_one - normal * mean_two)


def body(
    tokens,
    lengths,
    expert_ids,
    cotangent,
    query_weight,
    key_weight,
    value_weight,
    output_weight,
    gain_one,
    shift_one,
    gain_two,
    shift_two,
    expert_in,
    expert_out,
):
    seq_local, span, width = tokens.shape
    rows = seq_local * span
    n_ctx, n_exp = lax.axis_size("ctx"), lax.axis_size("exp")
    ctx = lax.axis_index("ctx")
    chips = n_ctx // CORES
    chip, core = ctx // CORES, ctx % CORES
    seqs = seq_local // chips
    full = span * n_ctx
    half = width // CORES
    experts = expert_in.shape[0]
    group = n_ctx // experts
    sub, member = ctx // group, ctx % group
    shard = expert_in.shape[1]
    all_experts = experts * n_exp
    capacity = max(2, rows * 5 // (4 * all_experts))
    devices = n_exp * n_ctx
    everyone = ("exp", "ctx")

    def ctx_send(value, target):
        return lax.ppermute(value, "ctx", [(c, target(c)) for c in range(n_ctx)])

    def other_core(value):
        return ctx_send(value, lambda c: c ^ 1)

    def to_chip(value, shift):
        return ctx_send(value, lambda c: ((c // CORES + shift) % chips) * CORES + c % CORES)

    def pick(value, index):
        return lax.dynamic_index_in_dim(value, index, 0, keepdims=False)

    def in_order(found, mine, size):
        out = []
        for place in range(size):
            chosen = found[0]
            for r in range(1, size):
                chosen = jnp.where((mine - place) % size == r, found[r], chosen)
            out.append(chosen)
        return jnp.stack(out)

    def chip_send(value):
        return [pick(value, chip)] + [
            to_chip(pick(value, (chip + r) % chips), r) for r in range(1, chips)
        ]

    def chip_join(found):
        return in_order(found, chip, chips)

    def chip_exchange(value):
        return chip_join(chip_send(value))

    def by_core(mine, other, axis=0):
        first = jnp.where(core == 0, mine, other)
        second = jnp.where(core == 0, other, mine)
        return jnp.stack([first, second], axis=axis)

    def exchange_all(value):
        return lax.all_to_all(value, everyone, split_axis=0, concat_axis=0, tiled=True)

    def by_pair(weight):
        return weight.astype(bf16).reshape(weight.shape[0], width // LANES, 1, LANES)

    exp_bits = [b for b in (2, 4, 8, 16) if b < n_exp]
    chip_bits = [b for b in (1, 2, 4, 8) if b < chips]

    def double(state, axis, bit):
        value, keys = state
        if axis == "exp":
            other = lax.ppermute(value, "exp", [(e, e ^ bit) for e in range(n_exp)])
            index, key = lax.axis_index("exp"), (0, -bit)
        else:
            other = ctx_send(value, lambda c: c ^ (bit * CORES))
            index, key = chip, (1, -bit)
        keys = sorted(keys + [key])
        at = keys.index(key)
        upper = (index & bit) != 0
        low, high = jnp.where(upper, other, value), jnp.where(upper, value, other)
        return jnp.stack([low, high], axis=at), keys

    def gather_cores(weight):
        kept = lax.dynamic_index_in_dim(weight, core, 1, keepdims=False)
        away = lax.dynamic_index_in_dim(weight, 1 - core, 1, keepdims=False)
        return by_core(kept, other_core(away)), [(2, 0)]

    def gather(state, steps):
        for axis, bit in steps:
            state = double(state, axis, bit)
        return state

    first_steps = [("exp", bit) for bit in exp_bits]
    last_steps = [("exp", 1)] + [("ctx", bit) for bit in chip_bits]

    local_qkv = jnp.concatenate(
        [by_pair(query_weight), by_pair(key_weight), by_pair(value_weight)], axis=2
    ).reshape(query_weight.shape[0], CORES, 3 * half)
    parts = 3 * half // 2

    gathered, keys = gather_cores(local_qkv)
    gathered, tokens, expert_ids, expert_out, cotangent = hold(
        (gathered, tokens, expert_ids, expert_out, cotangent)
    )

    ids_flat = expert_ids.reshape(rows)
    positions = ctx * span + jnp.arange(span)
    live = (positions[None, :] < lengths[:, None]).reshape(rows)
    onehot = ((ids_flat[:, None] == jnp.arange(all_experts)[None, :]) & live[:, None]).astype(
        jnp.int32
    )
    place = jnp.arange(rows)
    earlier = (place[None, :] < place[:, None]).astype(bf16)
    ranks = jnp.sum(onehot * mm(earlier, onehot.astype(bf16)).astype(jnp.int32), axis=1)
    keep = live & (ranks < capacity)
    target = jnp.where(keep, ids_flat * capacity + ranks, -1)
    targets = target.reshape(chips, seqs, span)
    targets = [targets[:, s].reshape(chips * span) for s in range(seqs)]
    slots = all_experts * capacity

    inputs = tokens.astype(f32).reshape(rows, width)
    normal_one, inverse_one = norm_parts(inputs)
    act = (normal_one * gain_one + shift_one).astype(bf16).reshape(chips, seqs, span, width)
    tokens_four = tokens.reshape(chips, seqs, span, width)
    cotangent_four = cotangent.reshape(chips, seqs, span, width)
    acts = []
    for s in range(seqs):
        act_chip = chip_exchange(act[:, s])
        acts.append(by_core(act_chip, other_core(act_chip), axis=1).reshape(full, width))

    def sub_send(value, shift):
        return ctx_send(value, lambda c: ((c // group + shift) % experts) * group + c % group)

    def group_send(value, shift):
        return ctx_send(value, lambda c: (c // group) * group + (c % group + shift) % group)

    def casts(weight):
        own, *others = [pick(weight, (sub + r) % experts).astype(bf16) for r in range(experts)]
        return own, others

    def swap(others, parts):
        cut = shard // parts
        return [
            sub_send(low[n * cut : (n + 1) * cut], r)
            for r, low in enumerate(others, 1)
            for n in range(parts)
        ]

    state = gather((gathered, keys), first_steps)
    streams = [
        ((state[0][..., :parts], state[1]), last_steps),
        ((state[0][..., parts:], state[1]), last_steps[::-1]),
    ]
    streams = [(gather(part, steps[:1]), steps[1:]) for part, steps in streams]
    values = [part[0] for part, _ in streams]
    values, expert_in, expert_out, cotangent_late = hold(
        (values, expert_in, expert_out, cotangent)
    )
    grad_send = dispatch([target], [cotangent_late.reshape(rows, width)], slots)
    first_own, first_low = casts(expert_in)
    second_own, second_low = casts(expert_out)
    qkv_weights = [
        gather((value, part[1]), steps)[0].reshape(width, parts)
        for value, (part, steps) in zip(values, streams)
    ]
    out_low = output_weight.astype(bf16)
    acts, qkv_weights, grad_send, second_low, out_low = hold(
        (acts, qkv_weights, grad_send, second_low, out_low)
    )
    grad_arrived = exchange_all(grad_send)
    out_all = lax.all_gather(out_low, everyone, axis=0, tiled=True)
    second_far = swap(second_low, 4)

    lens = lax.dynamic_slice_in_dim(lengths, chip * seqs, seqs)
    halves = range(2)
    calls = 2 * seqs
    qkvs, mixed_parts, previous = [], [], None
    for s in range(seqs):
        qkvs.append([mm(acts[s], weight).astype(bf16) for weight in qkv_weights])
        for h in halves:
            call = s * 2 + h
            if call > 1:
                n = slice(call - 2, call - 1)
                qkvs[s][h], second_far[n] = hold((qkvs[s][h], second_far[n]))
            if call:
                qkvs[s][h], previous = hold((qkvs[s][h], previous))
            mixed_chip = attention_forward(lens[s : s + 1], qkvs[s][h], full)
            previous = mixed_chip
            if call == calls - 1:
                mixed_chip, grad_arrived, mixed_parts = hold(
                    (mixed_chip, grad_arrived, mixed_parts)
                )
            mixed_chip = mixed_chip.reshape(chips, CORES, span, half // 2)
            mixed_own = lax.dynamic_index_in_dim(mixed_chip, core, 1, keepdims=False)
            mixed_away = lax.dynamic_index_in_dim(mixed_chip, 1 - core, 1, keepdims=False)
            mixed_parts.append(chip_send(jnp.stack([mixed_own, other_core(mixed_away)], axis=1)))
    mixed_parts = [chip_join(found) for found in mixed_parts]

    g_parts = [grad_arrived] + [group_send(grad_arrived, r) for r in range(1, group)]

    out_weight = out_all.reshape(CORES, 2, half // 2, width)
    out_weight = jnp.stack([pick(out_weight, core), pick(out_weight, 1 - core)], axis=1)
    out_weight = out_weight.reshape(width, width)
    hiddens, sents, mixeds = zip(
        *[
            project_norm(
                mixed_parts[2 * s : 2 * s + 2], tokens_four, s, out_weight, gain_two, shift_two
            )
            for s in range(seqs)
        ]
    )
    sents, second_far[2] = hold((sents, second_far[2]))
    arrived = exchange_all(dispatch(targets, sents, slots))

    sents, first_low = hold((sents, first_low))
    first_far = swap(first_low, 2)
    seconds, firsts = [[second_own], second_far], [[first_own], first_far]
    probs = []
    for h in halves:
        for s in range(seqs):
            part, _ = hold((qkvs[s][h], sents))
            probs.append(attention_probs(lens[s : s + 1], part, full))
    g_parts, probs = hold((g_parts, probs))
    activs_own = [grad_activ_pass(part, [second_own]) for part in g_parts]
    g_late, first_far[0] = hold((after(g_parts, activs_own), first_far[0]))
    activs_far = [grad_activ_pass(part, seconds[1]) for part in g_late]
    arrived, activs_own, activs_far, first_own, probs = hold(
        (arrived, activs_own, activs_far, first_own, probs)
    )
    x_parts = [arrived] + [group_send(arrived, r) for r in range(1, group)]
    owns = [hidden_pass(arrived, activs_own[0], firsts[0], bf16)]
    x_parts[-1], owns = hold((x_parts[-1], owns))
    for r in range(1, group):
        owns.append(hidden_pass(x_parts[r], activs_own[r], firsts[0], bf16))
    fars = [None] * group
    for r in list(range(1, group)) + [0]:
        fars[r] = hidden_pass(
            x_parts[r], activs_far[r], firsts[1], f32 if r == 0 else bf16, owns[r][2]
        )

    def sum_group(terms):
        total = terms[0]
        for r in range(1, group):
            total = total + group_send(terms[r], group - r).astype(f32)
        return total.astype(bf16)

    activ_parts = [[one[0] for one in owns], [one[0] for one in fars]]
    grad_pre_parts = [[one[1] for one in owns], [one[1] for one in fars]]
    grad_sent_rows = sum_group([one[2] for one in fars])
    grad_back = exchange_all(grad_sent_rows)
    grad_sent_rows, activ_parts, grad_pre_parts = hold(
        (grad_sent_rows, activ_parts, grad_pre_parts)
    )

    def send_grad(far, n, parts):
        return sub_send(far[n], experts - 1 - n // parts)

    def own_grads(whole, arriving, parts):
        order = [(experts - 1 - r) * parts + n for r in range(1, experts) for n in range(parts)]
        return assemble(sub, whole, [arriving[n] for n in order])

    cuts = 2
    *second_away, second_whole = expert_grad_pass(
        sub, *activ_parts, g_parts, experts, cuts
    )
    activ_parts, second_away = hold((activ_parts, second_away))
    early = (experts - 1) * cuts // 2
    second_sent = [send_grad(second_away, n, cuts) for n in range(early)]
    by_rows = list(zip(*activ_parts))
    terms = [
        group_send(down_pass(by_rows[r], seconds), group - r) for r in range(1, group)
    ]
    *first_away, first_whole = expert_grad_pass(
        sub, *grad_pre_parts, x_parts, experts, cuts
    )
    own_rows, terms, first_away = hold((by_rows[0], terms, first_away))
    result_rows = down_pass(own_rows, seconds, terms)
    grad_back, second_sent, first_away, result_rows = hold(
        (grad_back, second_sent, first_away, result_rows)
    )

    grad_hiddens, branches, grad_mixeds, small_two = zip(
        *[
            project_back(
                targets[s], grad_back, hiddens[s], cotangent_four, s, out_weight, gain_two
            )
            for s in range(seqs)
        ]
    )
    gm_chip = [chip_exchange(part) for part in grad_mixeds]

    own = width // devices
    pairs = n_exp // 2
    exp = lax.axis_index("exp")
    odd = exp % 2
    alike = [
        [e * n_ctx + c for e in range(n_exp) if e % 2 == which for c in range(n_ctx)]
        for which in range(2)
    ]
    tile = width // n_exp
    split = tile % LANES == 0

    def blocks_of(groups):
        if split:
            return split_grad_pass(groups, tile)
        terms = jnp.concatenate(
            [
                weight_grad_pass(lefts, rights).reshape(n_exp, tile, -1)[order]
                for order, lefts, rights in groups
            ],
            axis=2,
        )
        return [terms[:pairs].reshape(width // 2, -1), terms[pairs:].reshape(width // 2, -1)]

    def halve(away, kept):
        return kept, lax.ppermute(away, "exp", [(e, e ^ 1) for e in range(n_exp)])

    def joined(halved):
        total = add_terms(halved)
        return total.reshape(pairs * n_ctx, own, total.shape[1])

    def to_owner(terms):
        got = lax.all_to_all(
            terms, everyone, split_axis=0, concat_axis=0, tiled=True, axis_index_groups=alike
        )
        return got.astype(f32)

    def by_core_cols(got):
        got = jnp.sum(got.reshape(-1, CORES, own, got.shape[2]), axis=0)
        return jnp.transpose(got, (1, 0, 2))

    evens = jnp.arange(pairs, dtype=jnp.int32) * 2
    plain = jnp.concatenate([evens + 1 - odd, evens + odd])
    steps = n_exp // 4
    true_core, true_half, place = plain // (2 * steps), plain // steps % 2, plain % steps
    mixed_order = (true_half * CORES + (true_core + core) % CORES) * steps + place
    gm_chip, result_rows, second_away, first_away = hold(
        (gm_chip, result_rows, second_away, first_away)
    )
    gm_parts = [
        by_core(part[:, 0], other_core(part[:, 1]), axis=1).reshape(full, half) for part in gm_chip
    ]
    returned = exchange_all(result_rows)
    second_sent += [send_grad(second_away, n, cuts) for n in range(early, len(second_away))]

    wo_terms = halve(*blocks_of([(mixed_order, mixeds, branches)]))
    grad_qkvs = [[None, None] for s in range(seqs)]
    found_parts, w_terms, first_sent, previous = [], [], [], None
    call = 0
    for h in halves:
        for s in range(seqs):
            cols = slice(h * half // 2, (h + 1) * half // 2)
            gm_part = gm_parts[s][:, cols]
            if call == 0:
                first_sent = [send_grad(first_away, n, cuts) for n in range(len(first_away))]
            if call:
                gm_part, previous = hold((gm_part, previous))
            if call == calls - 2:
                gm_part, wo_terms = hold((gm_part, wo_terms))
            if call == calls - 1:
                gm_part, returned = hold((gm_part, returned))
            previous = attention_backward(qkvs[s][h], gm_part, probs[call])
            grad_qkvs[s][h] = previous
            call += 1
            if s == seqs - 1:
                terms = blocks_of([(plain, acts, [grad_qkvs[i][h] for i in range(seqs)])])
                previous, terms = hold((grad_qkvs[s][h], terms))
                grad_qkvs[s][h] = previous
                w_terms.append(halve(*terms))
            if h == 1:
                if call == calls - 1:
                    grad_qkvs[s][h], w_terms[0], second_sent, first_sent[0] = hold(
                        (grad_qkvs[s][h], w_terms[0], second_sent, first_sent[0])
                    )
                if call == calls:
                    grad_qkvs[s][h], found_parts = hold((grad_qkvs[s][h], found_parts))
                away, kept = grad_act_pass(core, grad_qkvs[s], qkv_weights, chips)
                previous, kept = hold((previous, kept))
                total = (kept.astype(f32) + other_core(away).astype(f32)).astype(bf16)
                if call == calls:
                    w_terms[1], returned, first_whole, found_parts = (
                        after(value, total)
                        for value in (w_terms[1], returned, first_whole, found_parts)
                    )
                found_parts.append(chip_send(total))
                grad_qkvs[s][h] = previous
    second_whole = after(second_whole, previous)
    value = joined([w_terms[1]])
    columns = value.shape[2]
    first = True
    upper_bits = [b for b in (2, 4, 8, 16) if b < n_exp]
    axes = [("exp", b) for b in upper_bits[::-1]] + [("ctx", b) for b in chip_bits[::-1]]
    value = value.reshape((2,) * len(axes) + (CORES, own, columns))
    for step in [("exp", b) for b in upper_bits] + axes[len(upper_bits) :]:
        axis, bit = step
        at = axes.index(step)
        index = exp if axis == "exp" else chip
        upper = jnp.where((index & bit) != 0, 1, 0)
        kept = lax.dynamic_index_in_dim(value, upper, at, keepdims=False)
        away = lax.dynamic_index_in_dim(value, 1 - upper, at, keepdims=False)
        if axis == "exp":
            other = lax.ppermute(away, "exp", [(e, e ^ bit) for e in range(n_exp)])
        else:
            other = ctx_send(away, lambda c: c ^ (bit * CORES))
        if first:
            other, found_parts[-1], first_sent[1:] = hold(
                (other, found_parts[-1], first_sent[1:])
            )
            first = False
        value = (kept.astype(f32) + other.astype(f32)).astype(bf16)
        axes.remove(step)
    second_sum = by_core(
        pick(value, core), other_core(pick(value, 1 - core)), axis=1
    ).astype(f32)
    grad_tokens, small_one = None, []
    for s in range(seqs):
        grad_tokens, sums = finish(
            chip, found_parts[s], tokens_four, grad_hiddens[s], gain_one, s, grad_tokens
        )
        small_one.append(sums)
    small_one = sum(small_one)
    grad_tokens = grad_tokens.reshape(tokens.shape)
    grad_expert_out = own_grads(second_whole, second_sent, cuts)
    grad_expert_in = own_grads(first_whole, first_sent, cuts)
    first_sum = to_owner(joined([w_terms[0], wo_terms]))
    grad_output = jnp.sum(first_sum[:, :, parts:], axis=0)
    grad_w = jnp.concatenate([by_core_cols(first_sum[:, :, :parts]), second_sum], axis=2)
    grad_w = grad_w.reshape(own, width // LANES, 3, LANES)
    grad_query, grad_key, grad_value = (grad_w[:, :, t].reshape(own, width) for t in range(3))

    block_out = None
    for s in range(seqs):
        block_out = combine(
            targets[s], returned, hiddens[s], tokens_four.shape, s, block_out
        )
    block_out = block_out.reshape(tokens.shape)
    small_two = sum(small_two)
    small = jnp.stack(
        [
            value.reshape(devices, own)
            for value in (small_one[0], small_one[1], small_two[0], small_two[1])
        ],
        axis=1,
    )
    small = jnp.sum(exchange_all(small), axis=0)
    return (
        block_out,
        grad_tokens,
        grad_query,
        grad_key,
        grad_value,
        grad_output,
        small[0],
        small[1],
        small[2],
        small[3],
        grad_expert_in,
        grad_expert_out,
    )


def solution(mesh):
    rows = P("exp", "ctx", None)
    weight = P(("exp", "ctx"), None)
    vector = P(("exp", "ctx"))
    return jax.shard_map(
        body,
        mesh=mesh,
        in_specs=(
            rows,
            P("exp"),
            P("ctx", "exp", None, None),
            rows,
            weight,
            weight,
            weight,
            weight,
            P(),
            P(),
            P(),
            P(),
            rows,
            rows,
        ),
        out_specs=(rows, rows, weight, weight, weight, weight)
        + (vector, vector, vector, vector)
        + (rows, rows),
        check_vma=False,
    )
```
